512 devices in a mesh: seq: 128 (over x, z, core), head: 4 (over y).
Axes of the slice: x: 4, y: 4, z: 16, core: 2. Of those that a mesh axis runs over, the one named last changes fastest.
Arguments:
- queries: bfloat16 [32768, 1024], P('seq', 'head'), may hold values from -8 to 8
- keys: bfloat16 [32768, 1024], P('seq', 'head'), may hold values from -8 to 8
- values: bfloat16 [32768, 1024], P('seq', 'head'), may hold values from -6 to 6
- out_grad: bfloat16 [32768, 1024], P('seq', 'head'), may hold values from -6 to 6
- w_out: bfloat16 [1024, 1024], P('head'), may hold values from -0.1875 to 0.1875
- cluster_ids: int32 [16, 32768, 1], P('head', 'seq'), may hold values from 0 to 255; in each aligned block of 256 rows (0 to 255, 256 to 511, ..., all dimensions but the last counted through in order) at most 2 rows name the same one
Outputs:
- query_grad: bfloat16 [32768, 1024], P('seq', 'head')
- key_grad: bfloat16 [32768, 1024], P('seq', 'head')
- value_grad: bfloat16 [32768, 1024], P('seq', 'head')
- centroid_sums: float32 [256, 1024], P('seq', 'head')
The draws below stay inside these ranges and needn't reach their ends.
Inputs may be any that keep to these rules, and one draw needn't show every extreme that they name: `cluster_ids`: within each head, among the frames of one device, no cluster is named by more than 2 frames.
All inputs are finite; a program needn't handle non-finite values.
Results may differ from the reference program's by a relative error of at most 0.012.
The reference program's roundings to bfloat16 on the way (of `d_out`, `probs_low` and `dscores`) count: a program that leaves them out, or rounds other values in their place, can miss the bound.
Values may be sent and summed in bfloat16 or wider, within the bound.
A program may use at most 64 MiB of HBM per device.

```python
import math
import jax
import jax.numpy as jnp
import numpy as np
from jax import lax

H = 16
HD = 64
CLUSTERS = 256
TOK_DEV = 256
D = 1024
MOST = 2
FRAMES = 32768
N_SEQ = 128


def draw_queries(key, part):
    key = jax.random.fold_in(key, 11)
    noise_key = jax.random.fold_in(key, 0)
    noise = jax.random.normal(noise_key, (FRAMES, D), jnp.float32)
    field = noise
    return jnp.clip(field, -8.0, 8.0).astype(jnp.bfloat16)


def draw_keys(key, part):
    key = jax.random.fold_in(key, 23)
    noise = jax.random.normal(key, (FRAMES, D), jnp.float32)
    field = noise
    return jnp.clip(field, -8.0, 8.0).astype(jnp.bfloat16)


def block_scale(rng, shape, cuts, smallest, largest):
    loudness = 1.0
    for axis_at, blocks in cuts:
        steps = jax.random.uniform(jax.random.fold_in(jax.random.fold_in(rng, 6), axis_at), (blocks,), jnp.float32, smallest / len(cuts), largest / len(cuts))
        loudness = loudness * jnp.repeat(jnp.exp(steps), shape[axis_at] // blocks).reshape((-1,) + (1,) * (len(shape) - 1 - axis_at))
    return loudness


def assign_block(stream_key, own, number, rows, count, top, bound, lean):
    order = jax.random.permutation(stream_key, count)
    crowded, ordinary = load_shares(count, rows * top, bound, lean, True), load_shares(count, rows * top, bound, lean, False)
    places = jnp.arange(count)

    def named(lengths, rotation):
        used = int((lengths > 0).sum())
        fixed = max(1, used // 4)
        moved = fixed + (places - fixed + rotation * (used - fixed)) % max(1, count - fixed)
        return jnp.zeros((count,), jnp.int32).at[order[jnp.where(places < fixed, places, moved)]].set(jnp.asarray(lengths, jnp.int32))

    lengths = jnp.where(number % 4 == 0, named(crowded, number // 4), named(ordinary, number - number // 4 - 1))
    mixed = jax.random.permutation(jax.random.fold_in(own, 3), count)
    giver, taker = mixed[0:count // 2 * 2:2], mixed[1:count // 2 * 2:2]
    room = jnp.minimum(lengths[giver] - 1, bound - lengths[taker]) // 2
    room = jnp.where((giver == order[0]) | (taker == order[0]) | (lengths[taker] == 0), 0, jnp.maximum(room, 0))
    moved = jax.random.randint(jax.random.fold_in(own, 4), (count // 2,), 0, 1 << 20) % (room + 1)
    lengths = lengths.at[giver].add(-moved).at[taker].add(moved)
    items = jnp.searchsorted(jnp.cumsum(lengths), jnp.arange(rows * top), side="right").astype(jnp.int32)
    table = items.reshape(top, rows).T
    table = table[jax.random.permutation(jax.random.fold_in(own, 1), rows)]
    rotation = jax.random.randint(jax.random.fold_in(own, 2), (rows, 1), 0, top)
    return jnp.take_along_axis(table, (jnp.arange(top)[None, :] + rotation) % top, axis=1)


def load_shares(number_of, total, most, skew, full):
    portions = [(1 << 20) // math.isqrt(standing ** skew) + 1 for standing in range(1, number_of + 1)]
    largest = most if full else min(most, max(-(-total // number_of), total * portions[0] // sum(portions)))
    least = 1 if total - largest >= number_of - 1 else 0
    given, spare = [largest] + [least] * (number_of - 1), total - largest - least * (number_of - 1)
    while spare > 0:
        free = [i for i in range(1, number_of) if given[i] < largest] or [i for i in range(1, number_of) if given[i] < most]
        pool, budget = sum([portions[i] for i in free]), spare
        for i in free:
            addition = min(most - given[i], max(1, budget * portions[i] // pool), spare)
            given[i] = given[i] + addition
            spare = spare - addition
    return np.array(given)


def bell_draw(key, shape, scale, limit, shards=(), kind=jnp.bfloat16):
    values = scale * jax.random.normal(key, shape, jnp.float32)
    if shards:
        values = values * block_scale(key, shape, shards, -0.22, 0.18)
    return jnp.clip(values, -limit, limit).astype(kind)


def setup_inputs(seed: int = 0) -> dict:
    streams_of = jax.random.split(jax.random.key(seed), 7)
    queries = draw_queries(jax.random.fold_in(streams_of[6], 71), 0)
    keys = draw_keys(jax.random.fold_in(streams_of[6], 71), 0)
    values = bell_draw(streams_of[2], (FRAMES, D), 1.0, 6.0, ((0, 128), (1, 4)))
    out_grad = bell_draw(streams_of[3], (FRAMES, D), 1.0, 6.0, ((0, 128), (1, 4)))
    w_out = bell_draw(streams_of[4], (D, D), D ** -0.5, 0.1875, ((0, 4),))
    cluster_ids_keys = jax.random.split(jax.random.fold_in(streams_of[5], 1), H * FRAMES // TOK_DEV)
    cluster_ids_turns = jax.random.permutation(jax.random.fold_in(streams_of[5], 3), H * FRAMES // TOK_DEV)
    cluster_ids = jax.vmap(lambda own, number: assign_block(jax.random.fold_in(streams_of[5], 2), own, number, TOK_DEV, CLUSTERS, 1, MOST, 1))(cluster_ids_keys, cluster_ids_turns).reshape((H, FRAMES, 1))
    return {"queries": queries, "keys": keys, "values": values, "out_grad": out_grad, "w_out": w_out, "cluster_ids": cluster_ids}


def cluster_block(block, live):
    q_rows = block[:, :HD]
    k_rows = block[:, HD:2 * HD]
    v_rows = block[:, 2 * HD:3 * HD]
    g_rows = block[:, 3 * HD:]
    scores = 0.125 * jnp.dot(q_rows, k_rows.T, preferred_element_type=jnp.float32)
    scores = jnp.where(live[None, :], scores, jnp.float32(-1e30))
    top = jnp.max(scores, axis=1, keepdims=True)
    expo = jnp.exp(scores - top)
    probs = expo / jnp.sum(expo, axis=1, keepdims=True)
    probs_low = probs.astype(jnp.bfloat16)
    attended = jnp.dot(probs_low, v_rows, preferred_element_type=jnp.float32)
    delta = jnp.sum(g_rows.astype(jnp.float32) * attended, axis=1, keepdims=True)
    dprobs = jnp.dot(g_rows, v_rows.T, preferred_element_type=jnp.float32)
    dscores = (probs * (dprobs - delta)).astype(jnp.bfloat16)
    dq_rows = (0.125 * jnp.dot(dscores, k_rows, preferred_element_type=jnp.float32)).astype(jnp.bfloat16)
    dk_rows = (0.125 * jnp.dot(dscores.T, q_rows, preferred_element_type=jnp.float32)).astype(jnp.bfloat16)
    dv_rows = jnp.dot(probs_low.T, g_rows, preferred_element_type=jnp.float32).astype(jnp.bfloat16)
    return jnp.concatenate([dq_rows, dk_rows, dv_rows], axis=1)


def head_grads(args):
    q_head, k_head, v_head, g_head, ids_head = args
    frames = ids_head.shape[0]
    capacity = MOST * N_SEQ
    order = jnp.argsort(ids_head, stable=True).astype(jnp.int32)
    counts = jnp.zeros((CLUSTERS,), jnp.int32).at[ids_head].add(jnp.ones((frames,), jnp.int32))
    starts = jnp.cumsum(counts).astype(jnp.int32) - counts
    sorted_ids = ids_head[order]
    rank = jnp.arange(frames, dtype=jnp.int32) - starts[sorted_ids]
    slot = (sorted_ids * capacity + rank).astype(jnp.int32)
    rows = jnp.concatenate([q_head, k_head, v_head, g_head], axis=1)[order]
    buffer = jnp.zeros((CLUSTERS * capacity, 4 * HD), jnp.bfloat16).at[slot].set(rows)
    buffer = buffer.reshape(CLUSTERS, capacity, 4 * HD)
    live = jnp.arange(capacity, dtype=jnp.int32)[None, :] < counts[:, None]
    grads = lax.map(lambda pair: cluster_block(pair[0], pair[1]), (buffer, live))
    picked = grads.reshape(CLUSTERS * capacity, 3 * HD)[slot]
    result = jnp.zeros((frames, 3 * HD), jnp.bfloat16).at[order].set(picked)
    key_sums = jnp.zeros((CLUSTERS, HD), jnp.float32).at[ids_head].add(k_head.astype(jnp.float32))
    return result, key_sums


def reference(queries, keys, values, out_grad, w_out, cluster_ids):
    frames = queries.shape[0]
    d_out = jnp.dot(out_grad, w_out.T, preferred_element_type=jnp.float32).astype(jnp.bfloat16)

    def split_heads(array):
        return array.reshape(frames, H, HD).transpose(1, 0, 2)

    results, key_sums = lax.map(head_grads, (split_heads(queries), split_heads(keys), split_heads(values), split_heads(d_out), cluster_ids[:, :, 0]))

    def join_heads(part):
        return part.transpose(1, 0, 2).reshape(frames, H * HD)

    query_grad = join_heads(results[:, :, :HD])
    key_grad = join_heads(results[:, :, HD:2 * HD])
    value_grad = join_heads(results[:, :, 2 * HD:])
    centroid_sums = key_sums.transpose(1, 0, 2).reshape(CLUSTERS, H * HD)
    return (query_grad, key_grad, value_grad, centroid_sums)
```

```python
import jax
import jax.numpy as jnp
from jax import lax
from jax.sharding import PartitionSpec as P

HD = 64
CLUSTERS = 256
MOST = 2
EMPTY = 64.0


def cluster_block(block, live):
    q_rows = block[:, :HD]
    k_rows = block[:, HD : 2 * HD]
    v_rows = block[:, 2 * HD : 3 * HD]
    g_rows = block[:, 3 * HD :]
    scores = 0.125 * jnp.dot(q_rows, k_rows.T, preferred_element_type=jnp.float32)
    scores = jnp.where(live[None, :], scores, jnp.float32(-1e30))
    top = jnp.max(scores, axis=1, keepdims=True)
    expo = jnp.exp(scores - top)
    probs = expo / jnp.sum(expo, axis=1, keepdims=True)
    probs_low = probs.astype(jnp.bfloat16)
    attended = jnp.dot(probs_low, v_rows, preferred_element_type=jnp.float32)
    delta = jnp.sum(g_rows.astype(jnp.float32) * attended, axis=1, keepdims=True)
    dprobs = jnp.dot(g_rows, v_rows.T, preferred_element_type=jnp.float32)
    dscores = (probs * (dprobs - delta)).astype(jnp.bfloat16)
    dq_rows = (0.125 * jnp.dot(dscores, k_rows, preferred_element_type=jnp.float32)).astype(
        jnp.bfloat16
    )
    dk_rows = (0.125 * jnp.dot(dscores.T, q_rows, preferred_element_type=jnp.float32)).astype(
        jnp.bfloat16
    )
    dv_rows = jnp.dot(probs_low.T, g_rows, preferred_element_type=jnp.float32).astype(jnp.bfloat16)
    return jnp.concatenate([dq_rows, dk_rows, dv_rows], axis=1)


def attend(received, per_owner):
    count_items = received.shape[0]
    owners = received.shape[1]
    capacity = owners * MOST
    blocks = received.reshape(count_items, owners, per_owner, MOST, 4 * HD)
    blocks = blocks.transpose(0, 2, 1, 3, 4).reshape(count_items * per_owner, capacity, 4 * HD)
    live = blocks[:, :, 0] < EMPTY / 2
    grads = lax.map(lambda pair: cluster_block(pair[0], pair[1]), (blocks, live))
    grads = grads.reshape(count_items, per_owner, owners, MOST, 3 * HD).transpose(0, 2, 1, 3, 4)
    returned = grads.reshape(count_items, owners, per_owner * MOST, 3 * HD)
    key_sums = jnp.sum(blocks[:, :, HD : 2 * HD].astype(jnp.float32), axis=1).reshape(
        count_items, per_owner, HD
    )
    return (returned, key_sums)


def shards(queries, keys, values, out_grad, w_out, cluster_ids):
    frames = queries.shape[0]
    heads = cluster_ids.shape[0]
    owners = lax.axis_size("seq")
    per_owner = CLUSTERS // owners
    d_out = lax.dot_general(
        lax.all_gather(out_grad, "head", axis=1, tiled=True),
        w_out,
        (((1,), (1,)), ((), ())),
        preferred_element_type=jnp.float32,
    ).astype(jnp.bfloat16)

    def split_heads(array):
        return array.reshape(frames, heads, HD).transpose(1, 0, 2)

    key_heads = split_heads(keys)
    rows = jnp.concatenate(
        [split_heads(queries), key_heads, split_heads(values), split_heads(d_out)], axis=2
    )
    ids = cluster_ids[:, :, 0]
    member = (ids[:, :, None] == jnp.arange(CLUSTERS, dtype=jnp.int32)[None, None, :]).astype(
        jnp.int32
    )
    running = jnp.cumsum(member, axis=1)
    rank = jnp.sum(member * (running - 1), axis=2)
    slot = ids * MOST + rank
    flat_index = (jnp.arange(heads, dtype=jnp.int32)[:, None] * (CLUSTERS * MOST) + slot).reshape(
        -1
    )
    empty_row = jnp.where(jnp.arange(4 * HD) == 0, EMPTY, 0.0).astype(jnp.bfloat16)
    outgoing = (
        jnp.broadcast_to(empty_row, (heads * CLUSTERS * MOST, 4 * HD))
        .at[flat_index]
        .set(rows.reshape(-1, 4 * HD))
    )
    outgoing = outgoing.reshape(heads, owners, per_owner * MOST, 4 * HD)
    received = lax.all_to_all(outgoing, "seq", split_axis=1, concat_axis=1, tiled=True)
    returned, key_sums = attend(received, per_owner)
    arrived = lax.all_to_all(returned, "seq", split_axis=1, concat_axis=1, tiled=True)
    picked = arrived.reshape(heads * CLUSTERS * MOST, 3 * HD)[flat_index].reshape(
        heads, frames, 3 * HD
    )

    def join_heads(part):
        return part.transpose(1, 0, 2).reshape(frames, heads * HD)

    query_grad = join_heads(picked[:, :, :HD])
    key_grad = join_heads(picked[:, :, HD : 2 * HD])
    value_grad = join_heads(picked[:, :, 2 * HD :])
    centroid_sums = key_sums.transpose(1, 0, 2).reshape(per_owner, heads * HD)
    return (query_grad, key_grad, value_grad, centroid_sums)


def solution(mesh):
    placed = (
        P("seq", "head"),
        P("seq", "head"),
        P("seq", "head"),
        P("seq", "head"),
        P("head", None),
        P("head", "seq", None),
    )
    return jax.shard_map(
        shards,
        mesh=mesh,
        in_specs=placed,
        out_specs=(P("seq", "head"), P("seq", "head"), P("seq", "head"), P("seq", "head")),
        check_vma=False,
    )
```

```python
import functools

import jax
import jax.numpy as jnp
from jax import lax
from jax.experimental import pallas as pl
from jax.experimental.pallas import tpu as pltpu
from jax.sharding import PartitionSpec as P

HD = 64
CLUSTERS = 256
EMPTY = 64.0
MESH = pl.DeviceIdType.MESH
BF = jnp.bfloat16
F32 = jnp.float32
NZ = 16
NXC = 8
NY = 4
CAP = 64
HALF = 32


def iota(shape, dim):
    return lax.broadcasted_iota(jnp.int32, shape, dim)


def onehot(cond):
    return jnp.where(cond, 1.0, 0.0).astype(BF)


def nn(a, b):
    return jnp.dot(a, b, preferred_element_type=F32)


def nt(a, b):
    return lax.dot_general(a, b, (((1,), (1,)), ((), ())), preferred_element_type=F32)


def tn(a, b):
    return lax.dot_general(a, b, (((0,), (0,)), ((), ())), preferred_element_type=F32)


def swap_halves(x):
    return jnp.concatenate([x[:, HD:], x[:, :HD]], axis=1)


def cluster_block(qk, vg):
    low = iota((256, 2 * HD), 1) < HD
    q, k = qk[:, :HD], qk[:, HD:]
    v, g = vg[:, :HD], vg[:, HD:]
    live = qk[:, 0:1].astype(F32) < EMPTY / 2
    scores = jnp.where(live, 0.125 * nt(k, q), jnp.float32(-1e30))
    expo = jnp.exp(scores - jnp.max(scores, axis=0, keepdims=True))
    probs = expo / jnp.sum(expo, axis=0, keepdims=True)
    probs_low = probs.astype(BF)
    dprobs = nt(v, g)
    delta = jnp.sum(probs_low.astype(F32) * dprobs, axis=0, keepdims=True)
    dscores = (probs * (dprobs - delta)).astype(BF)
    dk = 0.125 * nn(dscores, qk)
    dq = 0.125 * tn(dscores, qk)
    dv = nn(probs_low, vg)
    return jnp.where(low, dk, dq).astype(BF), jnp.where(low, swap_halves(dv), dv).astype(BF)


def kernel(
    q_ref, k_ref, v_ref, og_ref, w_ref, ids_ref,
    dq_ref, dk_ref, dv_ref, cs_ref,
    ogr, meta_s, meta_r, zqk_s, zqk_r, zvg_s, zvg_r, xs, xr, yb, zb, xbs, xbr,
    zbqk_s, zbqk_r, zbdv_s, zbdv_r, tcol, tslot,
    sem_s, sem_r, sem_l,
):
    me, hd = lax.axis_index("seq"), lax.axis_index("head")
    x, z, c = me // (2 * NZ), (me // 2) % NZ, me % 2
    xc = x * 2 + c

    def zpeer(i):
        to = (z + i) % NZ
        return to, (x * (2 * NZ) + to * 2 + c, hd)

    def xpeer(i):
        to = (xc + i) % NXC
        return to, ((to // 2) * (2 * NZ) + z * 2 + to % 2, hd)

    def ypeer(i):
        return (me, (hd + i) % NY)

    zorder = [8, 7, 9, 6, 10, 5, 11, 4, 12, 3, 13, 2, 14, 1, 15]
    barrier = pltpu.get_barrier_semaphore()
    peers = [ypeer(i) for i in range(1, NY)]
    peers += [zpeer(i)[1] for i in range(1, NZ)] + [xpeer(i)[1] for i in range(1, NXC)]
    for peer in peers:
        pl.semaphore_signal(barrier, inc=1, device_id=peer, device_id_type=MESH)

    sub, lane = iota((256, 256), 0), iota((256, 256), 1)
    earlier = onehot(sub < lane)
    ones = jnp.ones((256, 256), BF)
    group = sub // 16 == lane // 16
    before = onehot(group & (lane < sub))
    upto_pair = onehot(group & (lane // 2 <= sub // 2))
    before_pair = onehot(group & (lane // 2 < sub // 2))
    member, count, zof = [], [], []
    for h in range(4):
        ids = ids_ref[h : h + 1, :]
        row = ((ids >> 2) & 15) * 16 + (ids >> 6) * 4 + (ids & 3)
        zof.append((row >> 4).astype(F32))
        member.append(onehot(sub == row))
        count.append(nn(member[h], ones).astype(BF))
    targets = []
    meta = jnp.zeros((8, 128), F32)
    mrow = iota((8, 128), 0)
    for h in range(4):
        other = nn(before_pair if h % 2 == 0 else upto_pair, count[h ^ 1])
        place = nn(before, count[h]) + other + nn(member[h], earlier)
        pos = jnp.sum(member[h].astype(F32) * place, axis=0, keepdims=True)
        fits = pos < CAP
        lower = pos < HALF
        targets.append(jnp.where(fits, zof[h] * CAP + pos, -1.0))
        targets.append(jnp.where(lower, zof[h] * HALF + pos, -1.0))
        targets.append(jnp.where(fits & (pos >= HALF), zof[h] * HALF + pos - HALF, -1.0))
        held = nt(jnp.ones((8, 256), BF), member[h])
        meta = jnp.where(mrow == 2 * h, held[:, :128], meta)
        meta = jnp.where(mrow == 2 * h + 1, held[:, 128:], meta)
    meta_s[...] = meta.astype(BF)
    meta_r[pl.ds(z, 1)] = meta.astype(BF)[None]
    tcol[...] = jnp.concatenate(targets + [jnp.zeros((128 - 12, 256), F32)], axis=0).T

    def beside(a_ref, b, p):
        a = a_ref[:, p * 128 : (p + 1) * 128].astype(F32)
        b = b[:, p * 128 : (p + 1) * 128].astype(F32)
        low = iota((256, 128), 1) < HD
        return (
            jnp.where(low, a, swap_halves(b)).astype(BF),
            jnp.where(low, swap_halves(a), b).astype(BF),
        )

    def pack(pair, p, out):
        both = jnp.concatenate(pair, axis=0)
        goal = jnp.concatenate([targets[6 * p], targets[6 * p + 3]], axis=1).astype(jnp.int32)
        step = 4 * CAP
        for part in range(4):
            pick = onehot(iota((step, 512), 0) + part * step == goal)
            rows = nn(pick, both).astype(BF)
            out[p, part * 4 : part * 4 + 4] = rows.reshape(4, CAP, 128)

    pl.semaphore_wait(barrier, NY - 1 + NZ - 1 + NXC - 1)

    def remote(src, dst, sem, peer):
        pltpu.make_async_remote_copy(
            src_ref=src, dst_ref=dst, send_sem=sem_s.at[sem], recv_sem=sem_r.at[sem],
            device_id=peer, device_id_type=MESH,
        ).start()

    def settle(buf, n, sem, which):
        part = buf.at[pl.ds(0, n)]
        pltpu.make_async_copy(part, part, which.at[sem]).wait()

    for i in range(1, NY):
        remote(og_ref, ogr.at[hd], 0, ypeer(i))
    for i in zorder:
        remote(meta_s, meta_r.at[z], 1, zpeer(i)[1])

    def send_z(src, dst, p, sem):
        for i in zorder:
            to, peer = zpeer(i)
            remote(src.at[p, to], dst.at[p, z], sem, peer)
        own = pltpu.make_async_copy(src.at[p, z], dst.at[p, z], sem_l.at[sem])
        own.start()

    def wait_z(src, dst, p, sem):
        settle(dst.at[p], NZ - 1, sem, sem_r)
        pltpu.make_async_copy(src.at[p, z], dst.at[p, z], sem_l.at[sem]).wait()

    def send_x(src, dst, p, sem):
        for i in range(1, NXC):
            to, peer = xpeer(i)
            remote(src.at[p, to], dst.at[p, xc], sem, peer)
        pltpu.make_async_copy(src.at[p, xc], dst.at[p, xc], sem_l.at[sem]).start()

    def wait_x(src, dst, p, sem):
        settle(dst.at[p], NXC - 1, sem, sem_r)
        pltpu.make_async_copy(src.at[p, xc], dst.at[p, xc], sem_l.at[sem]).wait()

    pack(beside(q_ref, k_ref, 0), 0, zqk_s)
    send_z(zqk_s, zqk_r, 0, 2)
    qk_b = beside(q_ref, k_ref, 1)
    settle(ogr, NY - 1, 0, sem_r)
    grad = jnp.zeros((256, 256), F32)
    for i in range(NY):
        y = (hd + i) % NY
        piece = og_ref[...] if i == 0 else ogr[pl.ds(y, 1)][0]
        grad += nt(piece, w_ref[pl.ds(y, 1)][0])
    d_out = grad.astype(BF)
    pack(beside(v_ref, d_out, 0), 0, zvg_s)
    send_z(zvg_s, zvg_r, 0, 4)
    pack(qk_b, 1, zqk_s)
    send_z(zqk_s, zqk_r, 1, 3)
    pack(beside(v_ref, d_out, 1), 1, zvg_s)
    send_z(zvg_s, zvg_r, 1, 5)

    settle(meta_r, NZ - 1, 1, sem_r)
    r_i, l_i = iota((128, 128), 0), iota((128, 128), 1)
    slot_row = (l_i // 8) * 2 + (l_i // 2) % 2
    select = onehot((r_i % 16 == slot_row) & (r_i // 16 == z % 8) & (l_i < 64))
    found = nn(meta_r[...].reshape(128, 128), select)
    half = r_i % 2 == z // 8
    smaller = onehot(r_i < l_i)
    l16 = iota((16, 128), 1)
    for p in range(2):
        mine = jnp.where(half & ((r_i // 2) % 4 == 2 * p + (l_i // 4) % 2), found, 0.0)
        held = jnp.sum(mine.reshape(16, 8, 128), axis=1)
        taken = held > (l16 % 2).astype(F32)
        ahead = nn(onehot(taken), smaller)
        tslot[p] = jnp.where(taken, ahead, float(CAP))

    s_i, o_i = iota((256, 256), 0), iota((256, 256), 1)

    def source(o):
        return ((o // 2) % 16) * 16 + (o // 128) * 8 + ((o // 32) % 4) * 2 + o % 2

    perm = onehot(o_i == source(s_i))
    perm_back = onehot(s_i == source(o_i))
    mark = jnp.where((iota((16, 256), 0) == 0) & (iota((16, 256), 1) == 0), EMPTY, 0.0)
    mark = mark.astype(BF)

    def expand(p):
        for s in range(NZ):
            slot = tslot[p, s : s + 1, 0:64].astype(jnp.int32)
            pick = onehot(iota((CAP + 16, 64), 0) == slot)
            rows = jnp.concatenate([zqk_r[p, s], zvg_r[p, s]], axis=1)
            rows = tn(pick, jnp.concatenate([rows, mark], axis=0))
            rows = [rows[:, :128].reshape(8, 8, 128), rows[:, 128:].reshape(8, 8, 128)]
            xs[p, :, s] = jnp.concatenate(rows, axis=1).astype(BF)

    def work(p):
        for i in range(NXC):
            rows = nn(perm, xr[p, i].reshape(256, 128)).astype(BF)
            for b in range(8):
                yb[b, i * 32 : (i + 1) * 32, :] = rows[b * 32 : (b + 1) * 32]
        sums = []
        for b in range(4):
            zb[b], zb[4 + b] = cluster_block(yb[b], yb[4 + b])
            sums.append(jnp.sum(yb[b].astype(F32), axis=0, keepdims=True))
        for j in range(2):
            cs_ref[j : j + 1, p * 128 : (p + 1) * 128] = jnp.concatenate(
                [sums[j][:, HD:], sums[2 + j][:, HD:]], axis=1
            )
        for i in range(NXC):
            rows = [zb[b, i * 32 : (i + 1) * 32, :] for b in range(8)]
            rows = nn(perm_back, jnp.concatenate(rows, axis=0)).astype(BF)
            xbs[p, i] = rows.reshape(16, 16, 128)

    def compact(p):
        low = iota((HALF, 128), 1) < HD
        for s in range(NZ):
            slot = tslot[p, s : s + 1, 0:64].astype(jnp.int32)
            back = xbr[p, :, s].astype(F32)
            bqk = back[:, :8].reshape(64, 128).astype(BF)
            bdv = back[:, 8:].reshape(64, 128).astype(BF)
            zbqk_s[p, s] = nn(onehot(iota((CAP, 64), 0) == slot), bqk).astype(BF)
            at = iota((HALF, 64), 0)
            first = nn(onehot(at == slot), bdv)
            second = nn(onehot((at + HALF == slot) & (slot < CAP)), bdv)
            zbdv_s[p, s] = jnp.where(low, first, second).astype(BF)

    def unpack(p):
        keys, values, queries = [], [], []
        for h in (2 * p, 2 * p + 1):
            def pick(k, n):
                col = tcol[:, 3 * h + k : 3 * h + k + 1].astype(jnp.int32)
                return onehot(iota((256, NZ * n), 1) == col)

            got = nn(pick(0, CAP), zbqk_r[p].reshape(NZ * CAP, 128))
            dv_rows = zbdv_r[p].reshape(NZ * HALF, 128)
            first, second = nn(pick(1, HALF), dv_rows), nn(pick(2, HALF), dv_rows)
            keys.append(got[:, :HD])
            queries.append(got[:, HD:])
            values.append(first[:, :HD] + second[:, HD:])
        for ref, parts in ((dq_ref, queries), (dk_ref, keys), (dv_ref, values)):
            ref[:, p * 128 : (p + 1) * 128] = jnp.concatenate(parts, axis=1).astype(BF)

    def wait_rows(p):
        wait_z(zqk_s, zqk_r, p, 2 + p)
        wait_z(zvg_s, zvg_r, p, 4 + p)

    def send_back(p):
        wait_x(xbs, xbr, p, 8 + p)
        compact(p)
        send_z(zbqk_s, zbqk_r, p, 10 + p)
        send_z(zbdv_s, zbdv_r, p, 12 + p)

    wait_rows(0)
    expand(0)
    send_x(xs, xr, 0, 6)
    wait_x(xs, xr, 0, 6)
    work(0)
    send_x(xbs, xbr, 0, 8)
    wait_rows(1)
    expand(1)
    send_x(xs, xr, 1, 7)
    send_back(0)
    wait_x(xs, xr, 1, 7)
    work(1)
    send_x(xbs, xbr, 1, 9)
    send_back(1)
    for p in range(2):
        wait_z(zbqk_s, zbqk_r, p, 10 + p)
        wait_z(zbdv_s, zbdv_r, p, 12 + p)
        unpack(p)

    for i in range(1, NY):
        pltpu.make_async_copy(og_ref, og_ref, sem_s.at[0]).wait()
    for i in range(1, NZ):
        pltpu.make_async_copy(meta_s, meta_s, sem_s.at[1]).wait()
    for p in range(2):
        settle(zqk_s.at[p], NZ - 1, 2 + p, sem_s)
        settle(zvg_s.at[p], NZ - 1, 4 + p, sem_s)
        settle(xs.at[p], NXC - 1, 6 + p, sem_s)
        settle(xbs.at[p], NXC - 1, 8 + p, sem_s)
        settle(zbqk_s.at[p], NZ - 1, 10 + p, sem_s)
        settle(zbdv_s.at[p], NZ - 1, 12 + p, sem_s)


def shards(queries, keys, values, out_grad, w_out, cluster_ids):
    frames, width = queries.shape
    heads = cluster_ids.shape[0]
    vmem = pl.BlockSpec(memory_space=pltpu.VMEM)
    grad = jax.ShapeDtypeStruct((frames, width), BF)

    def buf(*shape):
        return pltpu.VMEM(shape, BF)

    w_parts = w_out.reshape(width, NY, width).transpose(1, 0, 2)
    return pl.pallas_call(
        kernel,
        name="routed_attention",
        out_shape=(grad, grad, grad, jax.ShapeDtypeStruct((2, width), F32)),
        in_specs=[vmem] * 6,
        out_specs=(vmem,) * 4,
        scratch_shapes=[
            buf(NY, frames, width),
            buf(8, 128),
            buf(NZ, 8, 128),
            buf(2, NZ, CAP, 128),
            buf(2, NZ, CAP, 128),
            buf(2, NZ, CAP, 128),
            buf(2, NZ, CAP, 128),
            buf(2, NXC, NZ, 16, 128),
            buf(2, NXC, NZ, 16, 128),
            buf(8, 256, 128),
            buf(8, 256, 128),
            buf(2, NXC, NZ, 16, 128),
            buf(2, NXC, NZ, 16, 128),
            buf(2, NZ, CAP, 128),
            buf(2, NZ, CAP, 128),
            buf(2, NZ, HALF, 128),
            buf(2, NZ, HALF, 128),
            pltpu.VMEM((256, 128), F32),
            pltpu.VMEM((2, NZ, 128), F32),
            pltpu.SemaphoreType.DMA((14,)),
            pltpu.SemaphoreType.DMA((14,)),
            pltpu.SemaphoreType.DMA((14,)),
        ],
        compiler_params=pltpu.CompilerParams(
            collective_id=0, has_side_effects=True, vmem_limit_bytes=48 << 20
        ),
    )(queries, keys, values, out_grad, w_parts, cluster_ids.reshape(heads, frames))


def solution(mesh):
    placed = (
        P("seq", "head"),
        P("seq", "head"),
        P("seq", "head"),
        P("seq", "head"),
        P("head", None),
        P("head", "seq", None),
    )
    return jax.shard_map(
        shards,
        mesh=mesh,
        in_specs=placed,
        out_specs=(P("seq", "head"), P("seq", "head"), P("seq", "head"), P("seq", "head")),
        check_vma=False,
    )
```

```python
import functools

import jax
import jax.numpy as jnp
from jax import lax
from jax.experimental import pallas as pl
from jax.experimental.pallas import tpu as pltpu
from jax.sharding import PartitionSpec as P

HD = 64
CLUSTERS = 256
MOST = 2
EMPTY = 64.0
MESH = pl.DeviceIdType.MESH
BF = jnp.bfloat16
F32 = jnp.float32
NZ = 16
NXC = 8
NY = 4
CAP = 40
HALF = 24
ROWS = 2 * CAP
BACK = CAP + HALF
NONE = float(ROWS)


def iota(shape, dim):
    return lax.broadcasted_iota(jnp.int32, shape, dim)


def onehot(cond):
    return jnp.where(cond, 1.0, 0.0).astype(BF)


def nn(a, b):
    return jnp.dot(a, b, preferred_element_type=F32)


def nt(a, b):
    return lax.dot_general(a, b, (((1,), (1,)), ((), ())), preferred_element_type=F32)


def tn(a, b):
    return lax.dot_general(a, b, (((0,), (0,)), ((), ())), preferred_element_type=F32)


def swap_halves(x):
    return jnp.concatenate([x[:, HD:], x[:, :HD]], axis=1)


def cluster_block(qk, vg):
    low = iota((256, 2 * HD), 1) < HD
    q, k = qk[:, :HD], qk[:, HD:]
    v, g = vg[:, :HD], vg[:, HD:]
    live = qk[:, 0:1].astype(F32) < EMPTY / 2
    scores = jnp.where(live, 0.125 * nt(k, q), jnp.float32(-1e30))
    expo = jnp.exp(scores - jnp.max(scores, axis=0, keepdims=True))
    probs = expo / jnp.sum(expo, axis=0, keepdims=True)
    probs_low = probs.astype(BF)
    dprobs = nt(v, g)
    delta = jnp.sum(probs_low.astype(F32) * dprobs, axis=0, keepdims=True)
    dscores = (probs * (dprobs - delta)).astype(BF)
    dk = 0.125 * nn(dscores, qk)
    dq = 0.125 * tn(dscores, qk)
    dv = nn(probs_low, vg)
    return jnp.where(low, dk, dq).astype(BF), jnp.where(low, swap_halves(dv), dv).astype(BF)


def kernel(
    q_ref, k_ref, v_ref, og_ref, w_ref, ids_ref,
    dq_ref, dk_ref, dv_ref, cs_ref, full_ref,
    ogr, meta_s, meta_r, zs, zr, xs, xr, yb, zb, xbs, xbr, zbs, zbr, tcol, tslot,
    sum_own, sum_s, sum_r, full_xs, full_xr, full_ys, full_yr,
    sem_s, sem_r, sem_l,
):
    me, hd = lax.axis_index("seq"), lax.axis_index("head")
    x, z, c = me // (2 * NZ), (me // 2) % NZ, me % 2
    xc = x * 2 + c

    def zpeer(i):
        to = (z + i) % NZ
        return to, (x * (2 * NZ) + to * 2 + c, hd)

    def xpeer(i):
        to = (xc + i) % NXC
        return to, ((to // 2) * (2 * NZ) + z * 2 + to % 2, hd)

    def ypeer(i):
        return (me, (hd + i) % NY)

    zorder = [8, 7, 9, 6, 10, 5, 11, 4, 12, 3, 13, 2, 14, 1, 15]
    barrier = pltpu.get_barrier_semaphore()
    peers = [ypeer(i) for i in range(1, NY)]
    peers += [zpeer(i)[1] for i in range(1, NZ)] + [xpeer(i)[1] for i in range(1, NXC)]
    for peer in peers:
        pl.semaphore_signal(barrier, inc=1, device_id=peer, device_id_type=MESH)

    sub, lane = iota((256, 256), 0), iota((256, 256), 1)
    earlier = onehot(sub < lane)
    ones = jnp.ones((256, 256), BF)
    group = sub // 16 == lane // 16
    before = onehot(group & (lane < sub))
    across = sub // 16 == (lane // 16 + NZ // 2) % NZ
    upto_pair = onehot(across & ((lane % 16) // 2 <= (sub % 16) // 2))
    before_pair = onehot(across & ((lane % 16) // 2 < (sub % 16) // 2))
    member, count, zof = [], [], []
    for h in range(4):
        ids = ids_ref[h : h + 1, :]
        row = ((ids >> 2) & 15) * 16 + (ids >> 6) * 4 + (ids & 3)
        zof.append((((row >> 4) + (h % 2) * (NZ // 2)) & (NZ - 1)).astype(F32))
        member.append(onehot(sub == row))
        count.append(nn(member[h], ones).astype(BF))
    targets = []
    meta = jnp.zeros((8, 128), F32)
    mrow = iota((8, 128), 0)
    for h in range(4):
        other = nn(before_pair if h % 2 == 0 else upto_pair, count[h ^ 1])
        place = nn(before, count[h]) + other + nn(member[h], earlier)
        pos = jnp.sum(member[h].astype(F32) * place, axis=0, keepdims=True)
        fits = pos < CAP
        lower = pos < HALF
        targets.append(jnp.where(fits, zof[h] * CAP + pos, -1.0))
        back = zof[h] * BACK + pos
        targets.append(jnp.where(fits, back, -1.0))
        targets.append(jnp.where(lower, back + CAP, -1.0))
        targets.append(jnp.where(fits & (pos >= HALF), back + CAP - HALF, -1.0))
        held = nt(jnp.ones((8, 256), BF), member[h])
        meta = jnp.where(mrow == 2 * h, held[:, :128], meta)
        meta = jnp.where(mrow == 2 * h + 1, held[:, 128:], meta)
    meta_s[...] = meta.astype(BF)
    meta_r[pl.ds(z, 1)] = meta.astype(BF)[None]
    tcol[...] = jnp.concatenate(targets + [jnp.zeros((128 - 16, 256), F32)], axis=0).T

    def beside(a_ref, b, p):
        a = a_ref[:, p * 128 : (p + 1) * 128].astype(F32)
        b = b[:, p * 128 : (p + 1) * 128].astype(F32)
        low = iota((256, 128), 1) < HD
        return (
            jnp.where(low, a, swap_halves(b)).astype(BF),
            jnp.where(low, swap_halves(a), b).astype(BF),
        )

    def pack(pair, p, at):
        both = jnp.concatenate(pair, axis=0)
        goal = jnp.concatenate([targets[8 * p], targets[8 * p + 4]], axis=1).astype(jnp.int32)
        step = 4 * CAP
        for part in range(4):
            pick = onehot(iota((step, 512), 0) + part * step == goal)
            rows = nn(pick, both).reshape(4, CAP, 128).astype(BF)
            zs[p, part * 4 : part * 4 + 4, at : at + CAP, :] = rows

    pl.semaphore_wait(barrier, NY - 1 + NZ - 1 + NXC - 1)

    def remote(src, dst, sem, peer):
        pltpu.make_async_remote_copy(
            src_ref=src, dst_ref=dst, send_sem=sem_s.at[sem], recv_sem=sem_r.at[sem],
            device_id=peer, device_id_type=MESH,
        ).start()

    def settle(buf, n, sem, which):
        part = buf.at[pl.ds(0, n)]
        pltpu.make_async_copy(part, part, which.at[sem]).wait()

    for i in range(1, NY):
        remote(og_ref, ogr.at[hd], 0, ypeer(i))
    for i in zorder:
        remote(meta_s, meta_r.at[z], 1, zpeer(i)[1])

    def send_z(src, dst, p, sem):
        for i in zorder:
            to, peer = zpeer(i)
            remote(src.at[p, to], dst.at[p, z], sem, peer)
        own = pltpu.make_async_copy(src.at[p, z], dst.at[p, z], sem_l.at[sem])
        own.start()

    def wait_z(src, dst, p, sem):
        settle(dst.at[p], NZ - 1, sem, sem_r)
        pltpu.make_async_copy(src.at[p, z], dst.at[p, z], sem_l.at[sem]).wait()

    def send_x(src, dst, p, sem):
        for i in range(1, NXC):
            to, peer = xpeer(i)
            remote(src.at[p, to], dst.at[p, xc], sem, peer)
        pltpu.make_async_copy(src.at[p, xc], dst.at[p, xc], sem_l.at[sem]).start()

    def wait_x(src, dst, p, sem):
        settle(dst.at[p], NXC - 1, sem, sem_r)
        pltpu.make_async_copy(src.at[p, xc], dst.at[p, xc], sem_l.at[sem]).wait()

    for p in range(2):
        pack(beside(q_ref, k_ref, p), p, 0)
    settle(ogr, NY - 1, 0, sem_r)
    grad = jnp.zeros((256, 256), F32)
    for i in range(NY):
        y = (hd + i) % NY
        piece = og_ref[...] if i == 0 else ogr[pl.ds(y, 1)][0]
        grad += nt(piece, w_ref[:, pl.ds(pl.multiple_of(y * 256, 256), 256)])
    d_out = grad.astype(BF)
    for p in range(2):
        pack(beside(v_ref, d_out, p), p, CAP)
        send_z(zs, zr, p, 2 + p)

    settle(meta_r, NZ - 1, 1, sem_r)
    r_i, l_i = iota((128, 128), 0), iota((128, 128), 1)
    slot_row = (l_i // 8) * 2 + (l_i // 2) % 2
    select = onehot((r_i % 16 == slot_row) & (r_i // 16 == z % 8) & (l_i < 64))
    meta_all = meta_r[...].reshape(128, 128)
    found = nn(meta_all, select)
    half = r_i % 2 == (z // 8 + (l_i // 4) % 2) % 2
    smaller = onehot(r_i < l_i)
    l16 = iota((16, 128), 1)
    for p in range(2):
        mine = jnp.where(half & ((r_i // 2) % 4 == 2 * p + (l_i // 4) % 2), found, 0.0)
        held = jnp.sum(mine.reshape(16, 8, 128), axis=1)
        taken = held > (l16 % 2).astype(F32)
        ahead = nn(onehot(taken), smaller)
        tslot[p] = jnp.where(taken, ahead, NONE)
    pair = (l_i // 8 == r_i // 8) & ((l_i % 8) // 4 == (r_i % 8) // 2)
    pair = pair & ((l_i % 2 + (l_i // 2) % 2) % 2 == r_i % 2)
    places = nn(onehot(pair), meta_all).astype(BF)
    places = nn(places, onehot(r_i // 16 == l_i))
    most = jnp.max(jnp.max(places, axis=0, keepdims=True), axis=1, keepdims=True)
    full = jnp.broadcast_to(jnp.where(most > CAP, 1.0, 0.0), (8, 128))
    full_xs[...] = full
    full_xr[pl.ds(xc, 1)] = full[None]
    for i in range(1, NXC):
        remote(full_xs, full_xr.at[xc], 10, xpeer(i)[1])

    s_i, o_i = iota((256, 256), 0), iota((256, 256), 1)

    def source(o):
        return ((o // 2) % 16) * 16 + (o // 128) * 8 + ((o // 32) % 4) * 2 + o % 2

    perm = onehot(o_i == source(s_i))
    perm_back = onehot(s_i == source(o_i))
    mark = jnp.where((iota((16, 128), 0) == 0) & (iota((16, 128), 1) == 0), EMPTY, 0.0)
    mark = mark.astype(BF)

    def expand(p):
        at = iota((ROWS + 16, 64), 0)
        for s in range(NZ):
            slot = tslot[p, s : s + 1, 0:64].astype(jnp.int32)
            rows = jnp.concatenate([zr[p, s], mark], axis=0)
            qk = tn(onehot(at == slot), rows).reshape(8, 8, 128)
            vg = tn(onehot(at == slot + CAP), rows).reshape(8, 8, 128)
            xs[p, :, s] = jnp.concatenate([qk, vg], axis=1).astype(BF)

    def work(p):
        for i in range(NXC):
            rows = nn(perm, xr[p, i].reshape(256, 128)).astype(BF)
            for b in range(8):
                yb[b, i * 32 : (i + 1) * 32, :] = rows[b * 32 : (b + 1) * 32]
        sums = []
        for b in range(4):
            zb[b], zb[4 + b] = cluster_block(yb[b], yb[4 + b])
            sums.append(jnp.sum(yb[b].astype(F32), axis=0, keepdims=True))
        for j in range(2):
            sum_own[j : j + 1, p * HD : (p + 1) * HD] = sums[j][:, HD:]
            sum_s[j : j + 1, p * HD : (p + 1) * HD] = sums[2 + j][:, HD:]
        for i in range(NXC):
            rows = [zb[b, i * 32 : (i + 1) * 32, :] for b in range(8)]
            rows = nn(perm_back, jnp.concatenate(rows, axis=0)).astype(BF)
            xbs[p, i] = rows.reshape(16, 16, 128)

    def compact(p):
        low = iota((BACK, 128), 1) < HD
        at = iota((BACK, 64), 0)
        for s in range(NZ):
            slot = tslot[p, s : s + 1, 0:64].astype(jnp.int32)
            back = xbr[p, :, s].astype(F32)
            back = [back[:, :8].reshape(64, 128), back[:, 8:].reshape(64, 128)]
            back = jnp.concatenate(back, axis=0).astype(BF)
            qk = at == slot
            lower = (at == slot + CAP) & (slot < HALF)
            upper = (at + HALF == slot + CAP) & (slot >= HALF) & (slot < CAP)
            first = nn(jnp.concatenate([onehot(qk), onehot(lower)], axis=1), back)
            second = nn(jnp.concatenate([onehot(qk), onehot(upper)], axis=1), back)
            zbs[p, s] = jnp.where(low, first, second).astype(BF)

    def unpack(p):
        keys, values, queries = [], [], []
        rows = zbr[p].reshape(NZ * BACK, 128)
        at = iota((256, NZ * BACK), 1)
        for h in (2 * p, 2 * p + 1):
            cols = tcol[:, 4 * h : 4 * h + 4].astype(jnp.int32)
            got = nn(onehot(at == cols[:, 1:2]), rows)
            first = nn(onehot(at == cols[:, 2:3]), rows)
            second = nn(onehot(at == cols[:, 3:4]), rows)
            keys.append(got[:, :HD])
            queries.append(got[:, HD:])
            values.append(first[:, :HD] + second[:, HD:])
        for ref, parts in ((dq_ref, queries), (dk_ref, keys), (dv_ref, values)):
            ref[:, p * 128 : (p + 1) * 128] = jnp.concatenate(parts, axis=1).astype(BF)

    def send_back(p):
        wait_x(xbs, xbr, p, 6 + p)
        compact(p)
        send_z(zbs, zbr, p, 8 + p)

    wait_z(zs, zr, 0, 2)
    expand(0)
    send_x(xs, xr, 0, 4)
    settle(full_xr, NXC - 1, 10, sem_r)
    full = jnp.max(full_xr[...], axis=0)
    full_ys[...] = full
    for i in range(1, NY):
        remote(full_ys, full_yr.at[hd], 11, ypeer(i))
    wait_x(xs, xr, 0, 4)
    work(0)
    send_x(xbs, xbr, 0, 6)
    wait_z(zs, zr, 1, 3)
    expand(1)
    send_x(xs, xr, 1, 5)
    send_back(0)
    wait_x(xs, xr, 1, 5)
    work(1)
    send_x(xbs, xbr, 1, 7)
    remote(sum_s, sum_r, 12, zpeer(NZ // 2)[1])
    send_back(1)
    pltpu.make_async_copy(sum_r, sum_r, sem_r.at[12]).wait()
    for p in range(2):
        cols = slice(p * HD, (p + 1) * HD)
        cs_ref[:, p * 128 : (p + 1) * 128] = jnp.concatenate(
            [sum_own[0:2, cols], sum_r[0:2, cols]], axis=1
        )
    settle(full_yr, NY - 1, 11, sem_r)
    for i in range(1, NY):
        full = jnp.maximum(full, full_yr[pl.ds((hd + i) % NY, 1)][0])
    full_ref[...] = full
    for p in range(2):
        wait_z(zbs, zbr, p, 8 + p)
        unpack(p)

    for i in range(1, NY):
        pltpu.make_async_copy(og_ref, og_ref, sem_s.at[0]).wait()
        pltpu.make_async_copy(full_ys, full_ys, sem_s.at[11]).wait()
    for i in range(1, NZ):
        pltpu.make_async_copy(meta_s, meta_s, sem_s.at[1]).wait()
    for i in range(1, NXC):
        pltpu.make_async_copy(full_xs, full_xs, sem_s.at[10]).wait()
    pltpu.make_async_copy(sum_s, sum_s, sem_s.at[12]).wait()
    for p in range(2):
        settle(zs.at[p], NZ - 1, 2 + p, sem_s)
        settle(xs.at[p], NXC - 1, 4 + p, sem_s)
        settle(xbs.at[p], NXC - 1, 6 + p, sem_s)
        settle(zbs.at[p], NZ - 1, 8 + p, sem_s)


def two_hop(queries, keys, values, out_grad, w_out, cluster_ids):
    frames, width = queries.shape
    heads = cluster_ids.shape[0]
    vmem = pl.BlockSpec(memory_space=pltpu.VMEM)
    grad = jax.ShapeDtypeStruct((frames, width), BF)

    def buf(*shape, dtype=BF):
        return pltpu.VMEM(shape, dtype)

    return pl.pallas_call(
        kernel,
        name="two_hop",
        out_shape=(
            grad, grad, grad,
            jax.ShapeDtypeStruct((2, width), F32), jax.ShapeDtypeStruct((8, 128), F32),
        ),
        in_specs=[vmem] * 6,
        out_specs=(vmem,) * 5,
        scratch_shapes=[
            buf(NY, frames, width),
            buf(8, 128),
            buf(NZ, 8, 128),
            buf(2, NZ, ROWS, 128),
            buf(2, NZ, ROWS, 128),
            buf(2, NXC, NZ, 16, 128),
            buf(2, NXC, NZ, 16, 128),
            buf(8, 256, 128),
            buf(8, 256, 128),
            buf(2, NXC, NZ, 16, 128),
            buf(2, NXC, NZ, 16, 128),
            buf(2, NZ, BACK, 128),
            buf(2, NZ, BACK, 128),
            buf(256, 128, dtype=F32),
            buf(2, NZ, 128, dtype=F32),
            buf(8, 128, dtype=F32),
            buf(8, 128, dtype=F32),
            buf(8, 128, dtype=F32),
            buf(8, 128, dtype=F32),
            buf(NXC, 8, 128, dtype=F32),
            buf(8, 128, dtype=F32),
            buf(NY, 8, 128, dtype=F32),
            pltpu.SemaphoreType.DMA((13,)),
            pltpu.SemaphoreType.DMA((13,)),
            pltpu.SemaphoreType.DMA((13,)),
        ],
        compiler_params=pltpu.CompilerParams(
            collective_id=0, has_side_effects=True, vmem_limit_bytes=48 << 20
        ),
    )(queries, keys, values, out_grad, w_out, cluster_ids.reshape(heads, frames))


def padded_block(block, live):
    q_rows = block[:, :HD]
    k_rows = block[:, HD : 2 * HD]
    v_rows = block[:, 2 * HD : 3 * HD]
    g_rows = block[:, 3 * HD :]
    scores = 0.125 * jnp.dot(q_rows, k_rows.T, preferred_element_type=jnp.float32)
    scores = jnp.where(live[None, :], scores, jnp.float32(-1e30))
    top = jnp.max(scores, axis=1, keepdims=True)
    expo = jnp.exp(scores - top)
    probs = expo / jnp.sum(expo, axis=1, keepdims=True)
    probs_low = probs.astype(jnp.bfloat16)
    attended = jnp.dot(probs_low, v_rows, preferred_element_type=jnp.float32)
    delta = jnp.sum(g_rows.astype(jnp.float32) * attended, axis=1, keepdims=True)
    dprobs = jnp.dot(g_rows, v_rows.T, preferred_element_type=jnp.float32)
    dscores = (probs * (dprobs - delta)).astype(jnp.bfloat16)
    dq_rows = (0.125 * jnp.dot(dscores, k_rows, preferred_element_type=jnp.float32)).astype(
        jnp.bfloat16
    )
    dk_rows = (0.125 * jnp.dot(dscores.T, q_rows, preferred_element_type=jnp.float32)).astype(
        jnp.bfloat16
    )
    dv_rows = jnp.dot(probs_low.T, g_rows, preferred_element_type=jnp.float32).astype(jnp.bfloat16)
    return jnp.concatenate([dq_rows, dk_rows, dv_rows], axis=1)


def padded_attend(received, per_owner):
    count_items = received.shape[0]
    owners = received.shape[1]
    capacity = owners * MOST
    blocks = received.reshape(count_items, owners, per_owner, MOST, 4 * HD)
    blocks = blocks.transpose(0, 2, 1, 3, 4).reshape(count_items * per_owner, capacity, 4 * HD)
    live = blocks[:, :, 0] < EMPTY / 2
    grads = lax.map(lambda pair: padded_block(pair[0], pair[1]), (blocks, live))
    grads = grads.reshape(count_items, per_owner, owners, MOST, 3 * HD).transpose(0, 2, 1, 3, 4)
    returned = grads.reshape(count_items, owners, per_owner * MOST, 3 * HD)
    key_sums = jnp.sum(blocks[:, :, HD : 2 * HD].astype(jnp.float32), axis=1).reshape(
        count_items, per_owner, HD
    )
    return (returned, key_sums)


def padded(queries, keys, values, out_grad, w_out, cluster_ids):
    frames = queries.shape[0]
    heads = cluster_ids.shape[0]
    owners = lax.axis_size("seq")
    per_owner = CLUSTERS // owners
    d_out = lax.dot_general(
        lax.all_gather(out_grad, "head", axis=1, tiled=True),
        w_out,
        (((1,), (1,)), ((), ())),
        preferred_element_type=jnp.float32,
    ).astype(jnp.bfloat16)

    def split_heads(array):
        return array.reshape(frames, heads, HD).transpose(1, 0, 2)

    key_heads = split_heads(keys)
    rows = jnp.concatenate(
        [split_heads(queries), key_heads, split_heads(values), split_heads(d_out)], axis=2
    )
    ids = cluster_ids[:, :, 0]
    member = (ids[:, :, None] == jnp.arange(CLUSTERS, dtype=jnp.int32)[None, None, :]).astype(
        jnp.int32
    )
    running = jnp.cumsum(member, axis=1)
    rank = jnp.sum(member * (running - 1), axis=2)
    slot = ids * MOST + rank
    flat_index = (jnp.arange(heads, dtype=jnp.int32)[:, None] * (CLUSTERS * MOST) + slot).reshape(
        -1
    )
    empty_row = jnp.where(jnp.arange(4 * HD) == 0, EMPTY, 0.0).astype(jnp.bfloat16)
    outgoing = (
        jnp.broadcast_to(empty_row, (heads * CLUSTERS * MOST, 4 * HD))
        .at[flat_index]
        .set(rows.reshape(-1, 4 * HD))
    )
    outgoing = outgoing.reshape(heads, owners, per_owner * MOST, 4 * HD)
    received = lax.all_to_all(outgoing, "seq", split_axis=1, concat_axis=1, tiled=True)
    returned, key_sums = padded_attend(received, per_owner)
    arrived = lax.all_to_all(returned, "seq", split_axis=1, concat_axis=1, tiled=True)
    picked = arrived.reshape(heads * CLUSTERS * MOST, 3 * HD)[flat_index].reshape(
        heads, frames, 3 * HD
    )

    def join_heads(part):
        return part.transpose(1, 0, 2).reshape(frames, heads * HD)

    query_grad = join_heads(picked[:, :, :HD])
    key_grad = join_heads(picked[:, :, HD : 2 * HD])
    value_grad = join_heads(picked[:, :, 2 * HD :])
    centroid_sums = key_sums.transpose(1, 0, 2).reshape(per_owner, heads * HD)
    return (query_grad, key_grad, value_grad, centroid_sums)


def shards(*args):
    *outs, full = two_hop(*args)
    return lax.cond(full[0, 0] > 0, lambda: tuple(padded(*args)), lambda: tuple(outs))


def solution(mesh):
    placed = (
        P("seq", "head"),
        P("seq", "head"),
        P("seq", "head"),
        P("seq", "head"),
        P("head", None),
        P("head", "seq", None),
    )
    return jax.shard_map(
        shards,
        mesh=mesh,
        in_specs=placed,
        out_specs=(P("seq", "head"), P("seq", "head"), P("seq", "head"), P("seq", "head")),
        check_vma=False,
    )
```

```python
import functools

import jax
import jax.numpy as jnp
from jax import lax
from jax.experimental import pallas as pl
from jax.experimental.pallas import tpu as pltpu
from jax.sharding import PartitionSpec as P

HD = 64
CLUSTERS = 256
MOST = 2
EMPTY = 64.0
MESH = pl.DeviceIdType.MESH
BF = jnp.bfloat16
F32 = jnp.float32
NZ = 16
NXC = 8
NY = 4
CAP = 40
HALF = 24
BACK = CAP + HALF
PARTS = ((0, 48), (48, 48), (96, 64))
ROWS = 160


def iota(shape, dim):
    return lax.broadcasted_iota(jnp.int32, shape, dim)


def onehot(cond):
    return jnp.where(cond, 1.0, 0.0).astype(BF)


def nn(a, b):
    return jnp.dot(a, b, preferred_element_type=F32)


def nt(a, b):
    return lax.dot_general(a, b, (((1,), (1,)), ((), ())), preferred_element_type=F32)


def tn(a, b):
    return lax.dot_general(a, b, (((0,), (0,)), ((), ())), preferred_element_type=F32)


def swap_halves(x):
    return jnp.concatenate([x[:, HD:], x[:, :HD]], axis=1)


def cluster_block(qk, vg):
    low = iota((256, 2 * HD), 1) < HD
    q, k = qk[:, :HD], qk[:, HD:]
    v, g = vg[:, :HD], vg[:, HD:]
    live = qk[:, 0:1].astype(F32) < EMPTY / 2
    scores = jnp.where(live, 0.125 * nt(k, q), jnp.float32(-1e30))
    expo = jnp.exp(scores - jnp.max(scores, axis=0, keepdims=True))
    probs = expo / jnp.sum(expo, axis=0, keepdims=True)
    probs_low = probs.astype(BF)
    dprobs = nt(v, g)
    delta = jnp.sum(probs_low.astype(F32) * dprobs, axis=0, keepdims=True)
    dscores = (probs * (dprobs - delta)).astype(BF)
    dk = 0.125 * nn(dscores, qk)
    dq = 0.125 * tn(dscores, qk)
    dv = nn(probs_low, vg)
    return jnp.where(low, dk, dq).astype(BF), jnp.where(low, swap_halves(dv), dv).astype(BF)


def kernel(
    q_ref, k_ref, v_ref, og_ref, w_ref, ids_ref,
    dq_ref, dk_ref, dv_ref, cs_ref, full_ref,
    ogr, meta_s, meta_r, zs, zr, xs, xr, yb, zb, xbs, xbr, zbs, zbr, tcol, tslot,
    sum_own, sum_s, sum_r, full_xs, full_xr, full_ys, full_yr,
    sem_s, sem_r, sem_l,
):
    me, hd = lax.axis_index("seq"), lax.axis_index("head")
    x, z, c = me // (2 * NZ), (me // 2) % NZ, me % 2
    xc = x * 2 + c

    def zpeer(i):
        to = (z + i) % NZ
        return to, (x * (2 * NZ) + to * 2 + c, hd)

    def xpeer(i):
        to = (xc + i) % NXC
        return to, ((to // 2) * (2 * NZ) + z * 2 + to % 2, hd)

    def ypeer(i):
        return (me, (hd + i) % NY)

    zorder = [8, 7, 9, 6, 10, 5, 11, 4, 12, 3, 13, 2, 14, 1, 15]
    barrier = pltpu.get_barrier_semaphore()
    peers = [ypeer(i) for i in range(1, NY)]
    peers += [zpeer(i)[1] for i in range(1, NZ)] + [xpeer(i)[1] for i in range(1, NXC)]
    for peer in peers:
        pl.semaphore_signal(barrier, inc=1, device_id=peer, device_id_type=MESH)

    sub, lane = iota((256, 256), 0), iota((256, 256), 1)
    earlier = onehot(sub < lane)
    ones = jnp.ones((256, 256), BF)
    before = onehot((sub // 16 == lane // 16) & (lane < sub))
    across = onehot(sub // 16 == (lane // 16 + NZ // 2) % NZ)
    member, count, zof = [], [], []
    for h in range(4):
        ids = ids_ref[h]
        row = ((ids >> 2) & 15) * 16 + (ids >> 6) * 4 + (ids & 3)
        zof.append((((row >> 4) + (h % 2) * (NZ // 2)) & (NZ - 1)).astype(F32))
        member.append(onehot(sub == row))
        count.append(nn(member[h], ones).astype(BF))
    poses, targets = [], []
    meta = jnp.zeros((8, 128), F32)
    mrow = iota((8, 128), 0)
    for h in range(4):
        place = nn(before, count[h]) + nn(member[h], earlier)
        if h % 2 == 1:
            place += nn(across, count[h - 1])
        pos = jnp.sum(member[h].astype(F32) * place, axis=0, keepdims=True)
        poses.append(pos)
        fits = pos < CAP
        back = zof[h] * BACK + pos
        targets.append(jnp.where(fits, back, -1.0))
        targets.append(jnp.where(pos < HALF, back + CAP, -1.0))
        targets.append(jnp.where(fits & (pos >= HALF), back + CAP - HALF, -1.0))
        held = nt(jnp.ones((8, 256), BF), member[h])
        meta = jnp.where(mrow == 2 * h, held[:, :128], meta)
        meta = jnp.where(mrow == 2 * h + 1, held[:, 128:], meta)
    meta_s[...] = meta.astype(BF)
    meta_r[pl.ds(z, 1)] = meta.astype(BF)[None]
    tcol[...] = jnp.concatenate(targets + [jnp.zeros((128 - 12, 256), F32)], axis=0).T

    def beside(a_ref, b, p):
        a = a_ref[:, p * 128 : (p + 1) * 128].astype(F32)
        b = b[:, p * 128 : (p + 1) * 128].astype(F32)
        low = iota((256, 128), 1) < HD
        return (
            jnp.where(low, a, swap_halves(b)).astype(BF),
            jnp.where(low, swap_halves(a), b).astype(BF),
        )

    def pack(part, pieces):
        at, n = PARTS[part]
        goals, rows = [], []
        for p, pair, first, last, to in pieces:
            for i in range(2):
                pos = poses[2 * p + i]
                fits = (pos >= first) & (pos < last)
                goals.append(jnp.where(fits, zof[2 * p + i] * n + pos + to, -1.0))
                rows.append(pair[i])
        goals = jnp.concatenate(goals, axis=1).astype(jnp.int32)
        rows = jnp.concatenate(rows, axis=0)
        for i in range(4):
            pick = onehot(iota((4 * n, 1024), 0) + i * 4 * n == goals)
            zs[i * 4 : i * 4 + 4, at : at + n, :] = nn(pick, rows).astype(BF).reshape(4, n, 128)

    pl.semaphore_wait(barrier, NY - 1 + NZ - 1 + NXC - 1)

    def remote(src, dst, sem, peer):
        pltpu.make_async_remote_copy(
            src_ref=src, dst_ref=dst, send_sem=sem_s.at[sem], recv_sem=sem_r.at[sem],
            device_id=peer, device_id_type=MESH,
        ).start()

    def settle(buf, n, sem, which, rows=None):
        part = buf.at[pl.ds(0, n)] if rows is None else buf.at[pl.ds(0, n), rows]
        pltpu.make_async_copy(part, part, which.at[sem]).wait()

    for i in range(1, NY):
        remote(og_ref, ogr.at[hd], 0, ypeer(i))
    for i in zorder:
        remote(meta_s, meta_r.at[z], 1, zpeer(i)[1])

    def send_z(src, dst, rows, sem):
        for i in zorder:
            to, peer = zpeer(i)
            remote(src.at[to, rows], dst.at[z, rows], sem, peer)
        pltpu.make_async_copy(src.at[z, rows], dst.at[z, rows], sem_l.at[sem]).start()

    def wait_z(src, dst, rows, sem):
        settle(dst, NZ - 1, sem, sem_r, rows)
        pltpu.make_async_copy(src.at[z, rows], dst.at[z, rows], sem_l.at[sem]).wait()

    def send_x(src, dst, p, i, sem):
        for step in range(1, NXC):
            to, peer = xpeer(step)
            remote(src.at[p, i, to], dst.at[p, i, xc], sem, peer)
        pltpu.make_async_copy(src.at[p, i, xc], dst.at[p, i, xc], sem_l.at[sem]).start()

    def wait_x(src, dst, p, i, sem):
        settle(dst.at[p, i], NXC - 1, sem, sem_r)
        pltpu.make_async_copy(src.at[p, i, xc], dst.at[p, i, xc], sem_l.at[sem]).wait()

    rows_of = [pl.ds(at, n) for at, n in PARTS]
    qk = [beside(q_ref, k_ref, p) for p in range(2)]
    pack(0, [(0, qk[0], 0, CAP, 0), (1, qk[1], 0, 8, CAP)])
    send_z(zs, zr, rows_of[0], 2)
    settle(ogr, NY - 1, 0, sem_r)
    grad = jnp.zeros((256, 256), F32)
    for i in range(NY):
        y = (hd + i) % NY
        piece = og_ref[...] if i == 0 else ogr[pl.ds(y, 1)][0]
        grad += nt(piece, w_ref[:, pl.ds(pl.multiple_of(y * 256, 256), 256)])
    d_out = grad.astype(BF)
    vg = [beside(v_ref, d_out, p) for p in range(2)]
    pack(1, [(0, vg[0], 0, CAP, 0), (1, qk[1], 8, 16, CAP - 8)])
    send_z(zs, zr, rows_of[1], 3)
    pack(2, [(1, qk[1], 16, CAP, -16), (1, vg[1], 0, CAP, CAP - 16)])
    send_z(zs, zr, rows_of[2], 4)

    settle(meta_r, NZ - 1, 1, sem_r)
    r_i, l_i = iota((128, 128), 0), iota((128, 128), 1)
    meta_all = meta_r[...].reshape(128, 128)
    slot_row = ((l_i // 8) % 8) * 2 + (l_i // 2) % 2
    found = nn(meta_all, onehot((r_i % 16 == slot_row) & (r_i // 16 == z % 8)))
    half = r_i % 2 == (z // 8 + l_i // 64) % 2

    def slot(o):
        return (o // 8) * 4 + o % 4

    smaller = onehot(((r_i // 4) % 2 == 0) & (slot(r_i) < slot(l_i)))
    l16 = iota((16, 128), 1)
    first_kind = (l16 // 4) % 2 == 0
    for p in range(2):
        mine = jnp.where(half & ((r_i // 2) % 4 == 2 * p + l_i // 64), found, 0.0)
        held = jnp.sum(mine.reshape(16, 8, 128), axis=1)
        taken = held > (l16 % 2).astype(F32)
        t = nn(onehot(taken), smaller)
        if p == 0:
            there, empty = jnp.where(first_kind, t, t + 48), 96.0
        else:
            there = jnp.where(first_kind, jnp.where(t < 8, t + 40, t + 80), t + 120)
            empty = float(ROWS)
        tslot[p] = jnp.where(taken, there, jnp.where(first_kind, empty, -1.0))
        fits = taken & (t < CAP)
        lower = jnp.where(t < HALF, t + CAP, -1.0)
        upper = jnp.where(t >= HALF, t + CAP - HALF, -1.0)
        tslot[2 + p] = jnp.where(fits, jnp.where(first_kind, t, lower), -1.0)
        tslot[4 + p] = jnp.where(fits, jnp.where(first_kind, t, upper), -1.0)
    pair = (l_i // 8 == r_i // 8) & ((l_i % 8) // 4 == (r_i % 8) // 2)
    pair = pair & ((l_i % 2 + (l_i // 2) % 2) % 2 == r_i % 2)
    places = nn(onehot(pair), meta_all).astype(BF)
    places = nn(places, onehot(r_i // 16 == l_i))
    most = jnp.max(jnp.max(places, axis=0, keepdims=True), axis=1, keepdims=True)
    full = jnp.broadcast_to(jnp.where(most > CAP, 1.0, 0.0), (8, 128))
    full_xs[...] = full
    full_xr[pl.ds(xc, 1)] = full[None]
    for i in range(1, NXC):
        remote(full_xs, full_xr.at[xc], 13, xpeer(i)[1])

    s_i, o_i = iota((256, 256), 0), iota((256, 256), 1)

    def source(o):
        return ((o // 32) % 2) * 128 + ((o // 2) % 16) * 8 + (o // 128) * 4 + ((o // 64) % 2) * 2 + o % 2

    perm = onehot(o_i == source(s_i))
    perm_back = onehot(s_i == source(o_i))
    mark = jnp.where((iota((16, 128), 0) == 0) & (iota((16, 128), 1) == 0), EMPTY, 0.0)
    mark = mark.astype(BF)

    def expand(p):
        n = (96, ROWS)[p]
        at = iota((n + 16, 128), 0)
        for s in range(NZ):
            pick = onehot(at == tslot[p, s : s + 1, :].astype(jnp.int32))
            rows = tn(pick, jnp.concatenate([zr[s, 0:n, :], mark], axis=0))
            xs[p, :, :, s * 8 : s * 8 + 8, :] = rows.reshape(2, 8, 8, 128).astype(BF)

    def work(p, h):
        for i in range(4):
            rows = nn(perm, xr[p, h, 2 * i : 2 * i + 2].reshape(256, 128)).astype(BF)
            for b in range(4):
                yb[b, i * 64 : (i + 1) * 64, :] = rows[b * 64 : (b + 1) * 64]
        for j in range(2):
            zb[j], zb[2 + j] = cluster_block(yb[j], yb[2 + j])
            total = jnp.sum(yb[j].astype(F32), axis=0, keepdims=True)
            (sum_own, sum_s)[h][j : j + 1, p * HD : (p + 1) * HD] = total[:, HD:]
        for i in range(4):
            rows = [zb[b, i * 64 : (i + 1) * 64, :] for b in range(4)]
            rows = nn(perm_back, jnp.concatenate(rows, axis=0)).astype(BF)
            xbs[p, h, 2 * i : 2 * i + 2] = rows.reshape(2, 128, 128)

    def compact(p):
        low = iota((BACK, 128), 1) < HD
        at = iota((BACK, 128), 0)
        for s in range(NZ):
            back = xbr[p, :, :, s * 8 : s * 8 + 8, :].reshape(128, 128)
            first = nn(onehot(at == tslot[2 + p, s : s + 1, :].astype(jnp.int32)), back)
            second = nn(onehot(at == tslot[4 + p, s : s + 1, :].astype(jnp.int32)), back)
            zbs[p, s] = jnp.where(low, first, second).astype(BF)

    def unpack(p):
        keys, values, queries = [], [], []
        rows = zbr[p].reshape(NZ * BACK, 128)
        at = iota((256, NZ * BACK), 1)
        for h in (2 * p, 2 * p + 1):
            cols = tcol[:, 3 * h : 3 * h + 3].astype(jnp.int32)
            got = nn(onehot(at == cols[:, 0:1]), rows)
            first = nn(onehot(at == cols[:, 1:2]), rows)
            second = nn(onehot(at == cols[:, 2:3]), rows)
            keys.append(got[:, :HD])
            queries.append(got[:, HD:])
            values.append(first[:, :HD] + second[:, HD:])
        for ref, parts in ((dq_ref, queries), (dk_ref, keys), (dv_ref, values)):
            ref[:, p * 128 : (p + 1) * 128] = jnp.concatenate(parts, axis=1).astype(BF)

    every = pl.ds(0, BACK)

    def forward(p):
        expand(p)
        for h in range(2):
            send_x(xs, xr, p, h, 5 + 2 * p + h)

    def middle(p, h):
        wait_x(xs, xr, p, h, 5 + 2 * p + h)
        work(p, h)
        send_x(xbs, xbr, p, h, 9 + 2 * p + h)

    def send_back(p):
        for h in range(2):
            wait_x(xbs, xbr, p, h, 9 + 2 * p + h)
        compact(p)
        send_z(zbs.at[p], zbr.at[p], every, 14 + p)

    wait_z(zs, zr, rows_of[0], 2)
    wait_z(zs, zr, rows_of[1], 3)
    forward(0)
    settle(full_xr, NXC - 1, 13, sem_r)
    full = jnp.max(full_xr[...], axis=0)
    full_ys[...] = full
    for i in range(1, NY):
        remote(full_ys, full_yr.at[hd], 16, ypeer(i))
    middle(0, 0)
    middle(0, 1)
    wait_z(zs, zr, rows_of[2], 4)
    forward(1)
    send_back(0)
    middle(1, 0)
    middle(1, 1)
    remote(sum_s, sum_r, 17, zpeer(NZ // 2)[1])
    send_back(1)
    pltpu.make_async_copy(sum_r, sum_r, sem_r.at[17]).wait()
    for p in range(2):
        cols = slice(p * HD, (p + 1) * HD)
        cs_ref[:, p * 128 : (p + 1) * 128] = jnp.concatenate(
            [sum_own[0:2, cols], sum_r[0:2, cols]], axis=1
        )
    settle(full_yr, NY - 1, 16, sem_r)
    for i in range(1, NY):
        full = jnp.maximum(full, full_yr[pl.ds((hd + i) % NY, 1)][0])
    full_ref[...] = full
    for p in range(2):
        wait_z(zbs.at[p], zbr.at[p], every, 14 + p)
        unpack(p)

    for i in range(1, NY):
        pltpu.make_async_copy(og_ref, og_ref, sem_s.at[0]).wait()
        pltpu.make_async_copy(full_ys, full_ys, sem_s.at[16]).wait()
    for i in range(1, NZ):
        pltpu.make_async_copy(meta_s, meta_s, sem_s.at[1]).wait()
    for i in range(1, NXC):
        pltpu.make_async_copy(full_xs, full_xs, sem_s.at[13]).wait()
    pltpu.make_async_copy(sum_s, sum_s, sem_s.at[17]).wait()
    for i in range(3):
        settle(zs, NZ - 1, 2 + i, sem_s, rows_of[i])
    for p in range(2):
        for h in range(2):
            settle(xs.at[p, h], NXC - 1, 5 + 2 * p + h, sem_s)
            settle(xbs.at[p, h], NXC - 1, 9 + 2 * p + h, sem_s)
        settle(zbs.at[p], NZ - 1, 14 + p, sem_s)


def two_hop(queries, keys, values, out_grad, w_out, cluster_ids):
    frames, width = queries.shape
    heads = cluster_ids.shape[0]
    vmem = pl.BlockSpec(memory_space=pltpu.VMEM)
    grad = jax.ShapeDtypeStruct((frames, width), BF)

    def buf(*shape, dtype=BF):
        return pltpu.VMEM(shape, dtype)

    return pl.pallas_call(
        kernel,
        name="two_hop",
        out_shape=(
            grad, grad, grad,
            jax.ShapeDtypeStruct((2, width), F32), jax.ShapeDtypeStruct((8, 128), F32),
        ),
        in_specs=[vmem] * 6,
        out_specs=(vmem,) * 5,
        scratch_shapes=[
            buf(NY, frames, width),
            buf(8, 128),
            buf(NZ, 8, 128),
            buf(NZ, ROWS, 128),
            buf(NZ, ROWS, 128),
            buf(2, 2, NXC, NZ * 8, 128),
            buf(2, 2, NXC, NZ * 8, 128),
            buf(4, 256, 128),
            buf(4, 256, 128),
            buf(2, 2, NXC, NZ * 8, 128),
            buf(2, 2, NXC, NZ * 8, 128),
            buf(2, NZ, BACK, 128),
            buf(2, NZ, BACK, 128),
            buf(256, 128, dtype=F32),
            buf(6, NZ, 128, dtype=F32),
            buf(8, 128, dtype=F32),
            buf(8, 128, dtype=F32),
            buf(8, 128, dtype=F32),
            buf(8, 128, dtype=F32),
            buf(NXC, 8, 128, dtype=F32),
            buf(8, 128, dtype=F32),
            buf(NY, 8, 128, dtype=F32),
            pltpu.SemaphoreType.DMA((18,)),
            pltpu.SemaphoreType.DMA((18,)),
            pltpu.SemaphoreType.DMA((18,)),
        ],
        compiler_params=pltpu.CompilerParams(
            collective_id=0, has_side_effects=True, vmem_limit_bytes=48 << 20
        ),
    )(queries, keys, values, out_grad, w_out, cluster_ids.reshape(heads, 1, frames))


def padded_block(block, live):
    q_rows = block[:, :HD]
    k_rows = block[:, HD : 2 * HD]
    v_rows = block[:, 2 * HD : 3 * HD]
    g_rows = block[:, 3 * HD :]
    scores = 0.125 * jnp.dot(q_rows, k_rows.T, preferred_element_type=jnp.float32)
    scores = jnp.where(live[None, :], scores, jnp.float32(-1e30))
    top = jnp.max(scores, axis=1, keepdims=True)
    expo = jnp.exp(scores - top)
    probs = expo / jnp.sum(expo, axis=1, keepdims=True)
    probs_low = probs.astype(jnp.bfloat16)
    attended = jnp.dot(probs_low, v_rows, preferred_element_type=jnp.float32)
    delta = jnp.sum(g_rows.astype(jnp.float32) * attended, axis=1, keepdims=True)
    dprobs = jnp.dot(g_rows, v_rows.T, preferred_element_type=jnp.float32)
    dscores = (probs * (dprobs - delta)).astype(jnp.bfloat16)
    dq_rows = (0.125 * jnp.dot(dscores, k_rows, preferred_element_type=jnp.float32)).astype(
        jnp.bfloat16
    )
    dk_rows = (0.125 * jnp.dot(dscores.T, q_rows, preferred_element_type=jnp.float32)).astype(
        jnp.bfloat16
    )
    dv_rows = jnp.dot(probs_low.T, g_rows, preferred_element_type=jnp.float32).astype(jnp.bfloat16)
    return jnp.concatenate([dq_rows, dk_rows, dv_rows], axis=1)


def padded_attend(received, per_owner):
    count_items = received.shape[0]
    owners = received.shape[1]
    capacity = owners * MOST
    blocks = received.reshape(count_items, owners, per_owner, MOST, 4 * HD)
    blocks = blocks.transpose(0, 2, 1, 3, 4).reshape(count_items * per_owner, capacity, 4 * HD)
    live = blocks[:, :, 0] < EMPTY / 2
    grads = lax.map(lambda pair: padded_block(pair[0], pair[1]), (blocks, live))
    grads = grads.reshape(count_items, per_owner, owners, MOST, 3 * HD).transpose(0, 2, 1, 3, 4)
    returned = grads.reshape(count_items, owners, per_owner * MOST, 3 * HD)
    key_sums = jnp.sum(blocks[:, :, HD : 2 * HD].astype(jnp.float32), axis=1).reshape(
        count_items, per_owner, HD
    )
    return (returned, key_sums)


def padded(queries, keys, values, out_grad, w_out, cluster_ids):
    frames = queries.shape[0]
    heads = cluster_ids.shape[0]
    owners = lax.axis_size("seq")
    per_owner = CLUSTERS // owners
    d_out = lax.dot_general(
        lax.all_gather(out_grad, "head", axis=1, tiled=True),
        w_out,
        (((1,), (1,)), ((), ())),
        preferred_element_type=jnp.float32,
    ).astype(jnp.bfloat16)

    def split_heads(array):
        return array.reshape(frames, heads, HD).transpose(1, 0, 2)

    key_heads = split_heads(keys)
    rows = jnp.concatenate(
        [split_heads(queries), key_heads, split_heads(values), split_heads(d_out)], axis=2
    )
    ids = cluster_ids[:, :, 0]
    member = (ids[:, :, None] == jnp.arange(CLUSTERS, dtype=jnp.int32)[None, None, :]).astype(
        jnp.int32
    )
    running = jnp.cumsum(member, axis=1)
    rank = jnp.sum(member * (running - 1), axis=2)
    slot = ids * MOST + rank
    flat_index = (jnp.arange(heads, dtype=jnp.int32)[:, None] * (CLUSTERS * MOST) + slot).reshape(
        -1
    )
    empty_row = jnp.where(jnp.arange(4 * HD) == 0, EMPTY, 0.0).astype(jnp.bfloat16)
    outgoing = (
        jnp.broadcast_to(empty_row, (heads * CLUSTERS * MOST, 4 * HD))
        .at[flat_index]
        .set(rows.reshape(-1, 4 * HD))
    )
    outgoing = outgoing.reshape(heads, owners, per_owner * MOST, 4 * HD)
    received = lax.all_to_all(outgoing, "seq", split_axis=1, concat_axis=1, tiled=True)
    returned, key_sums = padded_attend(received, per_owner)
    arrived = lax.all_to_all(returned, "seq", split_axis=1, concat_axis=1, tiled=True)
    picked = arrived.reshape(heads * CLUSTERS * MOST, 3 * HD)[flat_index].reshape(
        heads, frames, 3 * HD
    )

    def join_heads(part):
        return part.transpose(1, 0, 2).reshape(frames, heads * HD)

    query_grad = join_heads(picked[:, :, :HD])
    key_grad = join_heads(picked[:, :, HD : 2 * HD])
    value_grad = join_heads(picked[:, :, 2 * HD :])
    centroid_sums = key_sums.transpose(1, 0, 2).reshape(per_owner, heads * HD)
    return (query_grad, key_grad, value_grad, centroid_sums)


def shards(*args):
    *outs, full = two_hop(*args)
    return lax.cond(full[0, 0] > 0, lambda: tuple(padded(*args)), lambda: tuple(outs))


def solution(mesh):
    placed = (
        P("seq", "head"),
        P("seq", "head"),
        P("seq", "head"),
        P("seq", "head"),
        P("head", None),
        P("head", "seq", None),
    )
    return jax.shard_map(
        shards,
        mesh=mesh,
        in_specs=placed,
        out_specs=(P("seq", "head"), P("seq", "head"), P("seq", "head"), P("seq", "head")),
        check_vma=False,
    )
```

```python
import functools

import jax
import jax.numpy as jnp
from jax import lax
from jax.experimental import pallas as pl
from jax.experimental.pallas import tpu as pltpu
from jax.sharding import PartitionSpec as P

HD = 64
CLUSTERS = 256
MOST = 2
EMPTY = 64.0
MESH = pl.DeviceIdType.MESH
BF = jnp.bfloat16
F32 = jnp.float32
NZ = 16
NXC = 8
NY = 4
CAP = 40
CAP_HEAD = 24
HEAD0 = CAP - CAP_HEAD
HALF = 24
BACK = CAP + HALF
PARTS = ((0, 48), (48, 48), (96, 64))
ROWS = 160


def iota(shape, dim):
    return lax.broadcasted_iota(jnp.int32, shape, dim)


def onehot(cond):
    return jnp.where(cond, 1.0, 0.0).astype(BF)


def nn(a, b):
    return jnp.dot(a, b, preferred_element_type=F32)


def nt(a, b):
    return lax.dot_general(a, b, (((1,), (1,)), ((), ())), preferred_element_type=F32)


def tn(a, b):
    return lax.dot_general(a, b, (((0,), (0,)), ((), ())), preferred_element_type=F32)


def swap_halves(x):
    return jnp.concatenate([x[:, HD:], x[:, :HD]], axis=1)


def cluster_block(qk, vg):
    low = iota((256, 2 * HD), 1) < HD
    q, k = qk[:, :HD], qk[:, HD:]
    v, g = vg[:, :HD], vg[:, HD:]
    live = qk[:, 0:1].astype(F32) < EMPTY / 2
    scores = jnp.where(live, 0.125 * nt(k, q), jnp.float32(-1e30))
    expo = jnp.exp(scores - jnp.max(scores, axis=0, keepdims=True))
    probs = expo / jnp.sum(expo, axis=0, keepdims=True)
    probs_low = probs.astype(BF)
    dprobs = nt(v, g)
    delta = jnp.sum(probs_low.astype(F32) * dprobs, axis=0, keepdims=True)
    dscores = (probs * (dprobs - delta)).astype(BF)
    dk = 0.125 * nn(dscores, qk)
    dq = 0.125 * tn(dscores, qk)
    dv = nn(probs_low, vg)
    return jnp.where(low, dk, dq).astype(BF), jnp.where(low, swap_halves(dv), dv).astype(BF)


def unpack(p, rows, tcol):
    keys, values, queries = [], [], []
    at = iota((256, NZ * BACK), 1)
    for h in (2 * p, 2 * p + 1):
        cols = tcol[:, 3 * h : 3 * h + 3].astype(jnp.int32)
        got = nn(onehot(at == cols[:, 0:1]), rows)
        first = nn(onehot(at == cols[:, 1:2]), rows)
        second = nn(onehot(at == cols[:, 2:3]), rows)
        keys.append(got[:, :HD])
        queries.append(got[:, HD:])
        values.append(first[:, :HD] + second[:, HD:])
    return [jnp.concatenate(x, axis=1).astype(BF) for x in (queries, keys, values)]


def last_kernel(done_ref, rest_ref, tcol, cs_in, dq_ref, dk_ref, dv_ref, cs_ref):
    cs_ref[...] = cs_in[...]
    parts = unpack(1, rest_ref[...], tcol)
    for i, ref in enumerate((dq_ref, dk_ref, dv_ref)):
        ref[:, 0:128] = done_ref[i]
        ref[:, 128:256] = parts[i]


def kernel(
    q_hbm, k_hbm, v_hbm, og_hbm, w_hbm, ids_hbm,
    done_ref, rest_ref, tcol, cs_ref, full_ref,
    q_ref, k_ref, v_ref, og_ref, w_ref, ids_ref, ogr, meta_s, meta_r, zs, zr, xs, xr, yb, zb, xbs, xbr, zbs, zbr, tslot,
    sum_own, sum_s, sum_r, full_xs, full_xr, full_ys, full_yr,
    sem_s, sem_r, sem_l, sem_in,
):
    me, hd = lax.axis_index("seq"), lax.axis_index("head")
    x, z, c = me // (2 * NZ), (me // 2) % NZ, me % 2
    xc = x * 2 + c

    def zpeer(i):
        to = (z + i) % NZ
        return to, (x * (2 * NZ) + to * 2 + c, hd)

    def xpeer(i):
        to = (xc + i) % NXC
        return to, ((to // 2) * (2 * NZ) + z * 2 + to % 2, hd)

    def ypeer(i):
        return (me, (hd + i) % NY)

    zorder = [8, 7, 9, 6, 10, 5, 11, 4, 12, 3, 13, 2, 14, 1, 15]
    barrier = pltpu.get_barrier_semaphore()
    peers = [ypeer(i) for i in range(1, NY)]
    peers += [zpeer(i)[1] for i in range(1, NZ)] + [xpeer(i)[1] for i in range(1, NXC)]
    for peer in peers:
        pl.semaphore_signal(barrier, inc=1, device_id=peer, device_id_type=MESH)

    loads = [
        pltpu.make_async_copy(src, dst, sem_in.at[i])
        for i, (src, dst) in enumerate(
            ((ids_hbm, ids_ref), (q_hbm, q_ref), (k_hbm, k_ref),
             (og_hbm, og_ref), (v_hbm, v_ref), (w_hbm, w_ref))
        )
    ]
    for load in loads:
        load.start()
    loads[0].wait()

    sub, lane = iota((256, 256), 0), iota((256, 256), 1)
    earlier = onehot(sub < lane)
    ones = jnp.ones((256, 256), BF)
    before = onehot((sub // 16 == lane // 16) & (lane < sub))
    member, count, zof = [], [], []
    for h in range(4):
        ids = ids_ref[h]
        row = ((ids >> 2) & 15) * 16 + (ids >> 6) * 4 + (ids & 3)
        zof.append((((row >> 4) + (h % 2) * (NZ // 2)) & (NZ - 1)).astype(F32))
        member.append(onehot(sub == row))
        count.append(nn(member[h], ones).astype(BF))
    poses, targets = [], []
    meta = jnp.zeros((8, 128), F32)
    mrow = iota((8, 128), 0)
    for h in range(4):
        place = nn(before, count[h]) + nn(member[h], earlier)
        nth = jnp.sum(member[h].astype(F32) * place, axis=0, keepdims=True)
        fits = nth < CAP_HEAD
        pos = nth if h % 2 == 0 else CAP - 1 - nth
        poses.append(jnp.where(fits, pos, -1.0))
        back = zof[h] * BACK + pos
        targets.append(jnp.where(fits, back, -1.0))
        targets.append(jnp.where(fits & (pos < HALF), back + CAP, -1.0))
        targets.append(jnp.where(fits & (pos >= HALF), back + CAP - HALF, -1.0))
        held = nt(jnp.ones((8, 256), BF), member[h])
        meta = jnp.where(mrow == 2 * h, held[:, :128], meta)
        meta = jnp.where(mrow == 2 * h + 1, held[:, 128:], meta)
    meta_s[...] = meta.astype(BF)
    meta_r[pl.ds(z, 1)] = meta.astype(BF)[None]
    tcol[...] = jnp.concatenate(targets + [jnp.zeros((128 - 12, 256), F32)], axis=0).T

    def beside(a_ref, b, p):
        a = a_ref[:, p * 128 : (p + 1) * 128].astype(F32)
        b = b[:, p * 128 : (p + 1) * 128].astype(F32)
        low = iota((256, 128), 1) < HD
        return (
            jnp.where(low, a, swap_halves(b)).astype(BF),
            jnp.where(low, swap_halves(a), b).astype(BF),
        )

    def pack(part, pieces):
        at, n = PARTS[part]
        goals, rows = [], []
        for p, pair, first, last, to in pieces:
            for i in range(2):
                pos = poses[2 * p + i]
                fits = (pos >= first) & (pos < last)
                goals.append(jnp.where(fits, zof[2 * p + i] * n + pos + to, -1.0))
                rows.append(pair[i])
        goals = jnp.concatenate(goals, axis=1).astype(jnp.int32)
        rows = jnp.concatenate(rows, axis=0)
        for i in range(4):
            pick = onehot(iota((4 * n, 1024), 0) + i * 4 * n == goals)
            zs[i * 4 : i * 4 + 4, at : at + n, :] = nn(pick, rows).astype(BF).reshape(4, n, 128)

    pl.semaphore_wait(barrier, NY - 1 + NZ - 1 + NXC - 1)

    def remote(src, dst, sem, peer):
        pltpu.make_async_remote_copy(
            src_ref=src, dst_ref=dst, send_sem=sem_s.at[sem], recv_sem=sem_r.at[sem],
            device_id=peer, device_id_type=MESH,
        ).start()

    def settle(buf, n, sem, which, rows=None):
        part = buf.at[pl.ds(0, n)] if rows is None else buf.at[pl.ds(0, n), rows]
        pltpu.make_async_copy(part, part, which.at[sem]).wait()

    for i in range(1, NY):
        remote(og_hbm, ogr.at[hd], 0, ypeer(i))
    for i in zorder:
        remote(meta_s, meta_r.at[z], 1, zpeer(i)[1])

    def send_z(src, dst, rows, sem):
        for i in zorder:
            to, peer = zpeer(i)
            remote(src.at[to, rows], dst.at[z, rows], sem, peer)
        pltpu.make_async_copy(src.at[z, rows], dst.at[z, rows], sem_l.at[sem]).start()

    def wait_z(src, dst, rows, sem):
        settle(dst, NZ - 1, sem, sem_r, rows)
        pltpu.make_async_copy(src.at[z, rows], dst.at[z, rows], sem_l.at[sem]).wait()

    def send_x(src, dst, p, i, sem):
        for step in range(1, NXC):
            to, peer = xpeer(step)
            remote(src.at[p, i, to], dst.at[p, i, xc], sem, peer)
        pltpu.make_async_copy(src.at[p, i, xc], dst.at[p, i, xc], sem_l.at[sem]).start()

    def wait_x(src, dst, p, i, sem):
        settle(dst.at[p, i], NXC - 1, sem, sem_r)
        pltpu.make_async_copy(src.at[p, i, xc], dst.at[p, i, xc], sem_l.at[sem]).wait()

    rows_of = [pl.ds(at, n) for at, n in PARTS]
    loads[1].wait()
    loads[2].wait()
    qk = [beside(q_ref, k_ref, p) for p in range(2)]
    pack(0, [(0, qk[0], 0, CAP, 0), (1, qk[1], 0, 8, CAP)])
    send_z(zs, zr, rows_of[0], 2)
    for load in loads[3:]:
        load.wait()
    settle(ogr, NY - 1, 0, sem_r)
    grad = jnp.zeros((256, 256), F32)
    for i in range(NY):
        y = (hd + i) % NY
        piece = og_ref[...] if i == 0 else ogr[pl.ds(y, 1)][0]
        grad += nt(piece, w_ref[:, pl.ds(pl.multiple_of(y * 256, 256), 256)])
    d_out = grad.astype(BF)
    vg = [beside(v_ref, d_out, p) for p in range(2)]
    pack(1, [(0, vg[0], 0, CAP, 0), (1, qk[1], 8, 16, CAP - 8)])
    send_z(zs, zr, rows_of[1], 3)
    pack(2, [(1, qk[1], 16, CAP, -16), (1, vg[1], 0, CAP, CAP - 16)])
    send_z(zs, zr, rows_of[2], 4)

    settle(meta_r, NZ - 1, 1, sem_r)
    r_i, l_i = iota((128, 128), 0), iota((128, 128), 1)
    meta_all = meta_r[...].reshape(128, 128)
    slot_row = ((l_i // 8) % 8) * 2 + (l_i // 2) % 2
    found = nn(meta_all, onehot((r_i % 16 == slot_row) & (r_i // 16 == z % 8)))
    half = r_i % 2 == (z // 8 + l_i // 64) % 2

    def slot(o):
        return (o // 8) * 4 + o % 4

    smaller = ((r_i // 4) % 2 == 0) & (slot(r_i) < slot(l_i))
    smaller = onehot(smaller & (r_i // 64 == l_i // 64))
    l16 = iota((16, 128), 1)
    first_kind = (l16 // 4) % 2 == 0
    for p in range(2):
        mine = jnp.where(half & ((r_i // 2) % 4 == 2 * p + l_i // 64), found, 0.0)
        held = jnp.sum(mine.reshape(16, 8, 128), axis=1)
        taken = held > (l16 % 2).astype(F32)
        t = nn(onehot(taken), smaller)
        fits = taken & (t < CAP_HEAD)
        t = jnp.where(l16 < 64, t, CAP - 1 - t)
        if p == 0:
            there, empty = jnp.where(first_kind, t, t + 48), 96.0
        else:
            there = jnp.where(first_kind, jnp.where(t < 8, t + 40, t + 80), t + 120)
            empty = float(ROWS)
        there = jnp.where(fits, there, -1.0)
        tslot[p] = jnp.where(taken, there, jnp.where(first_kind, empty, -1.0))
        lower = jnp.where(t < HALF, t + CAP, -1.0)
        upper = jnp.where(t >= HALF, t + CAP - HALF, -1.0)
        tslot[2 + p] = jnp.where(fits, jnp.where(first_kind, t, lower), -1.0)
        tslot[4 + p] = jnp.where(fits, jnp.where(first_kind, t, upper), -1.0)
    pair = (l_i // 8 == r_i // 8) & ((l_i % 8) // 4 == (r_i % 8) // 2)
    pair = pair & ((l_i % 2 + (l_i // 2) % 2) % 2 == r_i % 2)
    places = nn(onehot(pair), meta_all).astype(BF)
    blocks = onehot(r_i // 16 == l_i)
    over = (nn(places, blocks) > CAP) | (nn(meta_all, blocks) > CAP_HEAD)
    over = jnp.max(jnp.where(over, 1.0, 0.0), axis=0, keepdims=True)
    full = jnp.broadcast_to(jnp.max(over, axis=1, keepdims=True), (8, 128))
    full_xs[...] = full
    full_xr[pl.ds(xc, 1)] = full[None]
    for i in range(1, NXC):
        remote(full_xs, full_xr.at[xc], 13, xpeer(i)[1])

    s_i, o_i = iota((256, 256), 0), iota((256, 256), 1)

    def source(o):
        return ((o // 32) % 2) * 128 + ((o // 2) % 16) * 8 + (o // 128) * 4 + ((o // 64) % 2) * 2 + o % 2

    perm = onehot(o_i == source(s_i))
    perm_back = onehot(s_i == source(o_i))
    mark = jnp.where((iota((16, 128), 0) == 0) & (iota((16, 128), 1) == 0), EMPTY, 0.0)
    mark = mark.astype(BF)

    def expand(p):
        n = (96, ROWS)[p]
        at = iota((n + 16, 128), 0)
        for s in range(NZ):
            pick = onehot(at == tslot[p, s : s + 1, :].astype(jnp.int32))
            rows = tn(pick, jnp.concatenate([zr[s, 0:n, :], mark], axis=0))
            xs[p, :, :, s * 8 : s * 8 + 8, :] = rows.reshape(2, 8, 8, 128).astype(BF)

    def work(p, h):
        for i in range(4):
            rows = nn(perm, xr[p, h, 2 * i : 2 * i + 2].reshape(256, 128)).astype(BF)
            for b in range(4):
                yb[b, i * 64 : (i + 1) * 64, :] = rows[b * 64 : (b + 1) * 64]
        for j in range(2):
            zb[j], zb[2 + j] = cluster_block(yb[j], yb[2 + j])
            total = jnp.sum(yb[j].astype(F32), axis=0, keepdims=True)
            (sum_own, sum_s)[h][j : j + 1, p * HD : (p + 1) * HD] = total[:, HD:]
        for i in range(4):
            rows = [zb[b, i * 64 : (i + 1) * 64, :] for b in range(4)]
            rows = nn(perm_back, jnp.concatenate(rows, axis=0)).astype(BF)
            xbs[p, h, 2 * i : 2 * i + 2] = rows.reshape(2, 128, 128)

    def compact_head0(p):
        at = iota((HEAD0, 64), 0)
        for s in range(NZ):
            back = xbr[p, 0, :, s * 8 : s * 8 + 8, :].reshape(64, 128)
            pick = at == tslot[2 + p, s : s + 1, 0:64].astype(jnp.int32)
            zbs[p, s, 0:HEAD0, :] = nn(onehot(pick), back).astype(BF)

    def compact_rest(p):
        low = iota((BACK - HEAD0, 128), 1) < HD
        at = iota((BACK - HEAD0, 128), 0) + HEAD0
        for s in range(NZ):
            back = xbr[p, :, :, s * 8 : s * 8 + 8, :].reshape(128, 128)
            first = nn(onehot(at == tslot[2 + p, s : s + 1, :].astype(jnp.int32)), back)
            second = nn(onehot(at == tslot[4 + p, s : s + 1, :].astype(jnp.int32)), back)
            zbs[p, s, HEAD0:BACK, :] = jnp.where(low, first, second).astype(BF)

    head0, rest = pl.ds(0, HEAD0), pl.ds(HEAD0, BACK - HEAD0)

    def forward(p):
        expand(p)
        for h in range(2):
            send_x(xs, xr, p, h, 5 + 2 * p + h)

    def middle(p, h):
        wait_x(xs, xr, p, h, 5 + 2 * p + h)
        work(p, h)
        send_x(xbs, xbr, p, h, 9 + 2 * p + h)

    def send_back(p):
        wait_x(xbs, xbr, p, 0, 9 + 2 * p)
        compact_head0(p)
        send_z(zbs.at[p], zbr.at[p], head0, 14 + 2 * p)
        wait_x(xbs, xbr, p, 1, 10 + 2 * p)
        compact_rest(p)
        send_z(zbs.at[p], zbr.at[p], rest, 15 + 2 * p)

    def wait_back(p):
        wait_z(zbs.at[p], zbr.at[p], head0, 14 + 2 * p)
        wait_z(zbs.at[p], zbr.at[p], rest, 15 + 2 * p)

    wait_z(zs, zr, rows_of[0], 2)
    wait_z(zs, zr, rows_of[1], 3)
    forward(0)
    settle(full_xr, NXC - 1, 13, sem_r)
    full = jnp.max(full_xr[...], axis=0)
    full_ys[...] = full
    for i in range(1, NY):
        remote(full_ys, full_yr.at[hd], 18, ypeer(i))
    middle(0, 0)
    middle(0, 1)
    wait_z(zs, zr, rows_of[2], 4)
    forward(1)
    send_back(0)
    middle(1, 0)
    middle(1, 1)
    remote(sum_s, sum_r, 19, zpeer(NZ // 2)[1])
    send_back(1)
    pltpu.make_async_copy(sum_r, sum_r, sem_r.at[19]).wait()
    for p in range(2):
        cols = slice(p * HD, (p + 1) * HD)
        cs_ref[:, p * 128 : (p + 1) * 128] = jnp.concatenate(
            [sum_own[0:2, cols], sum_r[0:2, cols]], axis=1
        )
    settle(full_yr, NY - 1, 18, sem_r)
    for i in range(1, NY):
        full = jnp.maximum(full, full_yr[pl.ds((hd + i) % NY, 1)][0])
    full_ref[0, 0] = jnp.max(full).astype(jnp.int32)
    wait_back(0)
    for i, part in enumerate(unpack(0, zbr[0].reshape(NZ * BACK, 128), tcol)):
        done_ref[i] = part
    wait_back(1)
    rest_ref[...] = zbr[1].reshape(NZ * BACK, 128)

    for i in range(1, NY):
        pltpu.make_async_copy(og_ref, og_ref, sem_s.at[0]).wait()
        pltpu.make_async_copy(full_ys, full_ys, sem_s.at[18]).wait()
    for i in range(1, NZ):
        pltpu.make_async_copy(meta_s, meta_s, sem_s.at[1]).wait()
    for i in range(1, NXC):
        pltpu.make_async_copy(full_xs, full_xs, sem_s.at[13]).wait()
    pltpu.make_async_copy(sum_s, sum_s, sem_s.at[19]).wait()
    for i in range(3):
        settle(zs, NZ - 1, 2 + i, sem_s, rows_of[i])
    for p in range(2):
        for h in range(2):
            settle(xs.at[p, h], NXC - 1, 5 + 2 * p + h, sem_s)
            settle(xbs.at[p, h], NXC - 1, 9 + 2 * p + h, sem_s)
        settle(zbs.at[p], NZ - 1, 14 + 2 * p, sem_s, head0)
        settle(zbs.at[p], NZ - 1, 15 + 2 * p, sem_s, rest)


def two_hop(queries, keys, values, out_grad, w_out, cluster_ids):
    frames, width = queries.shape
    heads = cluster_ids.shape[0]
    vmem = pl.BlockSpec(memory_space=pltpu.VMEM)

    def buf(*shape, dtype=BF):
        return pltpu.VMEM(shape, dtype)

    return pl.pallas_call(
        kernel,
        name="two_hop",
        out_shape=(
            jax.ShapeDtypeStruct((3, frames, width // 2), BF),
            jax.ShapeDtypeStruct((NZ * BACK, 128), BF),
            jax.ShapeDtypeStruct((frames, 128), F32),
            jax.ShapeDtypeStruct((2, width), F32),
            jax.ShapeDtypeStruct((1, 1), jnp.int32),
        ),
        in_specs=[pl.BlockSpec(memory_space=pl.ANY)] * 6,
        out_specs=(vmem,) * 4 + (pl.BlockSpec(memory_space=pltpu.SMEM),),
        scratch_shapes=[
            buf(frames, width),
            buf(frames, width),
            buf(frames, width),
            buf(frames, width),
            buf(width, NY * width),
            buf(heads, 1, frames, dtype=jnp.int32),
            buf(NY, frames, width),
            buf(8, 128),
            buf(NZ, 8, 128),
            buf(NZ, ROWS, 128),
            buf(NZ, ROWS, 128),
            buf(2, 2, NXC, NZ * 8, 128),
            buf(2, 2, NXC, NZ * 8, 128),
            buf(4, 256, 128),
            buf(4, 256, 128),
            buf(2, 2, NXC, NZ * 8, 128),
            buf(2, 2, NXC, NZ * 8, 128),
            buf(2, NZ, BACK, 128),
            buf(2, NZ, BACK, 128),
            buf(6, NZ, 128, dtype=F32),
            buf(8, 128, dtype=F32),
            buf(8, 128, dtype=F32),
            buf(8, 128, dtype=F32),
            buf(8, 128, dtype=F32),
            buf(NXC, 8, 128, dtype=F32),
            buf(8, 128, dtype=F32),
            buf(NY, 8, 128, dtype=F32),
            pltpu.SemaphoreType.DMA((20,)),
            pltpu.SemaphoreType.DMA((20,)),
            pltpu.SemaphoreType.DMA((20,)),
            pltpu.SemaphoreType.DMA((6,)),
        ],
        compiler_params=pltpu.CompilerParams(
            collective_id=0, has_side_effects=True, vmem_limit_bytes=48 << 20
        ),
    )(queries, keys, values, out_grad, w_out, cluster_ids.reshape(heads, 1, frames))


def padded_block(block, live):
    q_rows = block[:, :HD]
    k_rows = block[:, HD : 2 * HD]
    v_rows = block[:, 2 * HD : 3 * HD]
    g_rows = block[:, 3 * HD :]
    scores = 0.125 * jnp.dot(q_rows, k_rows.T, preferred_element_type=jnp.float32)
    scores = jnp.where(live[None, :], scores, jnp.float32(-1e30))
    top = jnp.max(scores, axis=1, keepdims=True)
    expo = jnp.exp(scores - top)
    probs = expo / jnp.sum(expo, axis=1, keepdims=True)
    probs_low = probs.astype(jnp.bfloat16)
    attended = jnp.dot(probs_low, v_rows, preferred_element_type=jnp.float32)
    delta = jnp.sum(g_rows.astype(jnp.float32) * attended, axis=1, keepdims=True)
    dprobs = jnp.dot(g_rows, v_rows.T, preferred_element_type=jnp.float32)
    dscores = (probs * (dprobs - delta)).astype(jnp.bfloat16)
    dq_rows = (0.125 * jnp.dot(dscores, k_rows, preferred_element_type=jnp.float32)).astype(
        jnp.bfloat16
    )
    dk_rows = (0.125 * jnp.dot(dscores.T, q_rows, preferred_element_type=jnp.float32)).astype(
        jnp.bfloat16
    )
    dv_rows = jnp.dot(probs_low.T, g_rows, preferred_element_type=jnp.float32).astype(jnp.bfloat16)
    return jnp.concatenate([dq_rows, dk_rows, dv_rows], axis=1)


def padded_attend(received, per_owner):
    count_items = received.shape[0]
    owners = received.shape[1]
    capacity = owners * MOST
    blocks = received.reshape(count_items, owners, per_owner, MOST, 4 * HD)
    blocks = blocks.transpose(0, 2, 1, 3, 4).reshape(count_items * per_owner, capacity, 4 * HD)
    live = blocks[:, :, 0] < EMPTY / 2
    grads = lax.map(lambda pair: padded_block(pair[0], pair[1]), (blocks, live))
    grads = grads.reshape(count_items, per_owner, owners, MOST, 3 * HD).transpose(0, 2, 1, 3, 4)
    returned = grads.reshape(count_items, owners, per_owner * MOST, 3 * HD)
    key_sums = jnp.sum(blocks[:, :, HD : 2 * HD].astype(jnp.float32), axis=1).reshape(
        count_items, per_owner, HD
    )
    return (returned, key_sums)


def padded(queries, keys, values, out_grad, w_out, cluster_ids):
    frames = queries.shape[0]
    heads = cluster_ids.shape[0]
    owners = lax.axis_size("seq")
    per_owner = CLUSTERS // owners
    d_out = lax.dot_general(
        lax.all_gather(out_grad, "head", axis=1, tiled=True),
        w_out,
        (((1,), (1,)), ((), ())),
        preferred_element_type=jnp.float32,
    ).astype(jnp.bfloat16)

    def split_heads(array):
        return array.reshape(frames, heads, HD).transpose(1, 0, 2)

    key_heads = split_heads(keys)
    rows = jnp.concatenate(
        [split_heads(queries), key_heads, split_heads(values), split_heads(d_out)], axis=2
    )
    ids = cluster_ids[:, :, 0]
    member = (ids[:, :, None] == jnp.arange(CLUSTERS, dtype=jnp.int32)[None, None, :]).astype(
        jnp.int32
    )
    running = jnp.cumsum(member, axis=1)
    rank = jnp.sum(member * (running - 1), axis=2)
    slot = ids * MOST + rank
    flat_index = (jnp.arange(heads, dtype=jnp.int32)[:, None] * (CLUSTERS * MOST) + slot).reshape(
        -1
    )
    empty_row = jnp.where(jnp.arange(4 * HD) == 0, EMPTY, 0.0).astype(jnp.bfloat16)
    outgoing = (
        jnp.broadcast_to(empty_row, (heads * CLUSTERS * MOST, 4 * HD))
        .at[flat_index]
        .set(rows.reshape(-1, 4 * HD))
    )
    outgoing = outgoing.reshape(heads, owners, per_owner * MOST, 4 * HD)
    received = lax.all_to_all(outgoing, "seq", split_axis=1, concat_axis=1, tiled=True)
    returned, key_sums = padded_attend(received, per_owner)
    arrived = lax.all_to_all(returned, "seq", split_axis=1, concat_axis=1, tiled=True)
    picked = arrived.reshape(heads * CLUSTERS * MOST, 3 * HD)[flat_index].reshape(
        heads, frames, 3 * HD
    )

    def join_heads(part):
        return part.transpose(1, 0, 2).reshape(frames, heads * HD)

    query_grad = join_heads(picked[:, :, :HD])
    key_grad = join_heads(picked[:, :, HD : 2 * HD])
    value_grad = join_heads(picked[:, :, 2 * HD :])
    centroid_sums = key_sums.transpose(1, 0, 2).reshape(per_owner, heads * HD)
    return (query_grad, key_grad, value_grad, centroid_sums)


def last_step(done, rest, tcol, sums):
    frames, width = done.shape[1], 2 * done.shape[2]
    vmem = pl.BlockSpec(memory_space=pltpu.VMEM)
    grad = jax.ShapeDtypeStruct((frames, width), BF)
    return pl.pallas_call(
        last_kernel,
        name="last_step",
        out_shape=(grad, grad, grad, jax.ShapeDtypeStruct(sums.shape, F32)),
        in_specs=[vmem] * 4,
        out_specs=(vmem,) * 4,
        compiler_params=pltpu.CompilerParams(vmem_limit_bytes=16 << 20),
    )(done, rest, tcol, sums)


def as_parts(dq, dk, dv, sums):
    frames = dq.shape[0]
    done = jnp.stack([x[:, :128] for x in (dq, dk, dv)])
    rest = [jnp.concatenate([dk[:, at : at + HD], dq[:, at : at + HD]], axis=1) for at in (128, 192)]
    rest = jnp.concatenate(rest + [dv[:, 128:], jnp.zeros((NZ * BACK - 3 * frames, 128), BF)])
    at = jnp.arange(frames, dtype=F32)[:, None]
    none = jnp.full((frames, 1), -1.0, F32)
    second = [at, at + 2 * frames, none, at + frames, none, at + 2 * frames]
    cols = [jnp.zeros((frames, 6), F32)] + second + [jnp.zeros((frames, 116), F32)]
    return done, rest, jnp.concatenate(cols, axis=1), sums


def shards(*args):
    *parts, full = two_hop(*args)
    parts = lax.cond(full[0, 0] > 0, lambda: as_parts(*padded(*args)), lambda: tuple(parts))
    return tuple(last_step(*parts))


def solution(mesh):
    placed = (
        P("seq", "head"),
        P("seq", "head"),
        P("seq", "head"),
        P("seq", "head"),
        P("head", None),
        P("head", "seq", None),
    )
    return jax.shard_map(
        shards,
        mesh=mesh,
        in_specs=placed,
        out_specs=(P("seq", "head"), P("seq", "head"), P("seq", "head"), P("seq", "head")),
        check_vma=False,
    )
```

```python
import functools

import jax
import jax.numpy as jnp
from jax import lax
from jax.experimental import pallas as pl
from jax.experimental.pallas import tpu as pltpu
from jax.sharding import PartitionSpec as P

HD = 64
CLUSTERS = 256
MOST = 2
EMPTY = 64.0
MESH = pl.DeviceIdType.MESH
BF = jnp.bfloat16
F32 = jnp.float32
NZ = 16
NXC = 8
NY = 4
CAP = 40
CAP_HEAD = 24
HEAD0 = CAP - CAP_HEAD
HALF = 24
BACK = CAP + HALF
PARTS = ((0, 32), (32, 32), (64, 16), (80, 48), (128, 32))
ROWS = 160


def iota(shape, dim):
    return lax.broadcasted_iota(jnp.int32, shape, dim)


def onehot(cond):
    return jnp.where(cond, 1.0, 0.0).astype(BF)


def nn(a, b):
    return jnp.dot(a, b, preferred_element_type=F32)


def nt(a, b):
    return lax.dot_general(a, b, (((1,), (1,)), ((), ())), preferred_element_type=F32)


def tn(a, b):
    return lax.dot_general(a, b, (((0,), (0,)), ((), ())), preferred_element_type=F32)


def swap_halves(x):
    return jnp.concatenate([x[:, HD:], x[:, :HD]], axis=1)


def cluster_block(qk, vg):
    low = iota((256, 2 * HD), 1) < HD
    q, k = qk[:, :HD], qk[:, HD:]
    v, g = vg[:, :HD], vg[:, HD:]
    live = qk[:, 0:1].astype(F32) < EMPTY / 2
    scores = jnp.where(live, 0.125 * nt(k, q), jnp.float32(-1e30))
    expo = jnp.exp(scores - jnp.max(scores, axis=0, keepdims=True))
    probs = expo / jnp.sum(expo, axis=0, keepdims=True)
    probs_low = probs.astype(BF)
    dprobs = nt(v, g)
    delta = jnp.sum(probs_low.astype(F32) * dprobs, axis=0, keepdims=True)
    dscores = (probs * (dprobs - delta)).astype(BF)
    dk = 0.125 * nn(dscores, qk)
    dq = 0.125 * tn(dscores, qk)
    dv = nn(probs_low, vg)
    return jnp.where(low, dk, dq).astype(BF), jnp.where(low, swap_halves(dv), dv).astype(BF)


def unpack(p, rows, tcol):
    keys, values, queries = [], [], []
    at = iota((256, NZ * BACK), 1)
    for h in (2 * p, 2 * p + 1):
        cols = tcol[:, 3 * h : 3 * h + 3].astype(jnp.int32)
        got = nn(onehot(at == cols[:, 0:1]), rows)
        first = nn(onehot(at == cols[:, 1:2]), rows)
        second = nn(onehot(at == cols[:, 2:3]), rows)
        keys.append(got[:, :HD])
        queries.append(got[:, HD:])
        values.append(first[:, :HD] + second[:, HD:])
    return [jnp.concatenate(x, axis=1).astype(BF) for x in (queries, keys, values)]


def last_kernel(done_ref, rest_ref, tcol, cs_in, dq_ref, dk_ref, dv_ref, cs_ref):
    cs_ref[...] = cs_in[...]
    parts = unpack(1, rest_ref[...], tcol)
    for i, ref in enumerate((dq_ref, dk_ref, dv_ref)):
        ref[:, 0:128] = done_ref[i]
        ref[:, 128:256] = parts[i]


def kernel(
    q_hbm, k_hbm, v_hbm, og_hbm, w_hbm, ids_hbm,
    done_ref, rest_ref, tcol, cs_ref, full_ref,
    q_ref, k_ref, v_ref, og_ref, w_ref, ids_ref, ogr, meta_s, meta_r, zs, zr, xs, xr, yb, zb, xbs, xbr, zbs, zbr, tslot,
    sum_own, sum_s, sum_r, full_xs, full_xr, full_ys, full_yr,
    sem_s, sem_r, sem_l, sem_in,
):
    me, hd = lax.axis_index("seq"), lax.axis_index("head")
    x, z, c = me // (2 * NZ), (me // 2) % NZ, me % 2
    xc = x * 2 + c

    def zpeer(i):
        to = (z + i) % NZ
        return to, (x * (2 * NZ) + to * 2 + c, hd)

    def xpeer(i):
        to = (xc + i) % NXC
        return to, ((to // 2) * (2 * NZ) + z * 2 + to % 2, hd)

    def ypeer(i):
        return (me, (hd + i) % NY)

    zorder = [8, 7, 9, 6, 10, 5, 11, 4, 12, 3, 13, 2, 14, 1, 15]
    barrier = pltpu.get_barrier_semaphore()
    peers = [ypeer(i) for i in range(1, NY)]
    peers += [zpeer(i)[1] for i in range(1, NZ)] + [xpeer(i)[1] for i in range(1, NXC)]
    for peer in peers:
        pl.semaphore_signal(barrier, inc=1, device_id=peer, device_id_type=MESH)

    loads = [
        pltpu.make_async_copy(src, dst, sem_in.at[i])
        for i, (src, dst) in enumerate(
            ((ids_hbm, ids_ref), (q_hbm, q_ref), (k_hbm, k_ref),
             (og_hbm, og_ref), (v_hbm, v_ref), (w_hbm, w_ref))
        )
    ]
    for load in loads:
        load.start()
    loads[0].wait()

    sub, lane = iota((256, 256), 0), iota((256, 256), 1)
    earlier = onehot(sub < lane)
    ones = jnp.ones((256, 256), BF)
    before = onehot((sub // 16 == lane // 16) & (lane < sub))
    member, count, zof = [], [], []
    for h in range(4):
        ids = ids_ref[h]
        row = ((ids >> 2) & 15) * 16 + (ids >> 6) * 4 + (ids & 3)
        zof.append((((row >> 4) + (h % 2) * (NZ // 2)) & (NZ - 1)).astype(F32))
        member.append(onehot(sub == row))
        count.append(nn(member[h], ones).astype(BF))
    poses, targets = [], []
    meta = jnp.zeros((8, 128), F32)
    mrow = iota((8, 128), 0)
    for h in range(4):
        place = nn(before, count[h]) + nn(member[h], earlier)
        nth = jnp.sum(member[h].astype(F32) * place, axis=0, keepdims=True)
        fits = nth < CAP_HEAD
        pos = nth if h % 2 == 0 else CAP - 1 - nth
        poses.append(jnp.where(fits, pos, -1.0))
        back = zof[h] * BACK + pos
        targets.append(jnp.where(fits, back, -1.0))
        targets.append(jnp.where(fits & (pos < HALF), back + CAP, -1.0))
        targets.append(jnp.where(fits & (pos >= HALF), back + CAP - HALF, -1.0))
        held = nt(jnp.ones((8, 256), BF), member[h])
        meta = jnp.where(mrow == 2 * h, held[:, :128], meta)
        meta = jnp.where(mrow == 2 * h + 1, held[:, 128:], meta)
    meta_s[...] = meta.astype(BF)
    meta_r[pl.ds(z, 1)] = meta.astype(BF)[None]
    tcol[...] = jnp.concatenate(targets + [jnp.zeros((128 - 12, 256), F32)], axis=0).T

    def beside(a_ref, b, p):
        a = a_ref[:, p * 128 : (p + 1) * 128].astype(F32)
        b = b[:, p * 128 : (p + 1) * 128].astype(F32)
        low = iota((256, 128), 1) < HD
        return (
            jnp.where(low, a, swap_halves(b)).astype(BF),
            jnp.where(low, swap_halves(a), b).astype(BF),
        )

    def pack(part, pieces):
        at, n = PARTS[part]
        goals, rows = [], []
        for p, pair, first, last, to in pieces:
            for i in range(2):
                pos = poses[2 * p + i]
                fits = (pos >= first) & (pos < last)
                goals.append(jnp.where(fits, zof[2 * p + i] * n + pos + to, -1.0))
                rows.append(pair[i])
        goals = jnp.concatenate(goals, axis=1).astype(jnp.int32)
        rows = jnp.concatenate(rows, axis=0)
        for i in range(4):
            pick = onehot(iota((4 * n, goals.shape[1]), 0) + i * 4 * n == goals)
            zs[i * 4 : i * 4 + 4, at : at + n, :] = nn(pick, rows).astype(BF).reshape(4, n, 128)

    pl.semaphore_wait(barrier, NY - 1 + NZ - 1 + NXC - 1)

    def remote(src, dst, sem, peer):
        pltpu.make_async_remote_copy(
            src_ref=src, dst_ref=dst, send_sem=sem_s.at[sem], recv_sem=sem_r.at[sem],
            device_id=peer, device_id_type=MESH,
        ).start()

    def settle(buf, n, sem, which, rows=None):
        part = buf.at[pl.ds(0, n)] if rows is None else buf.at[pl.ds(0, n), rows]
        pltpu.make_async_copy(part, part, which.at[sem]).wait()

    for i in range(1, NY):
        remote(og_hbm, ogr.at[hd], 0, ypeer(i))
    for i in zorder:
        remote(meta_s, meta_r.at[z], 1, zpeer(i)[1])

    def send_z(src, dst, rows, sem):
        for i in zorder:
            to, peer = zpeer(i)
            remote(src.at[to, rows], dst.at[z, rows], sem, peer)
        pltpu.make_async_copy(src.at[z, rows], dst.at[z, rows], sem_l.at[sem]).start()

    def wait_z(src, dst, rows, sem):
        settle(dst, NZ - 1, sem, sem_r, rows)
        pltpu.make_async_copy(src.at[z, rows], dst.at[z, rows], sem_l.at[sem]).wait()

    def send_x(src, dst, p, i, sem):
        for step in range(1, NXC):
            to, peer = xpeer(step)
            remote(src.at[p, i, to], dst.at[p, i, xc], sem, peer)
        pltpu.make_async_copy(src.at[p, i, xc], dst.at[p, i, xc], sem_l.at[sem]).start()

    def wait_x(src, dst, p, i, sem):
        settle(dst.at[p, i], NXC - 1, sem, sem_r)
        pltpu.make_async_copy(src.at[p, i, xc], dst.at[p, i, xc], sem_l.at[sem]).wait()

    rows_of = [pl.ds(at, n) for at, n in PARTS]
    loads[1].wait()
    loads[2].wait()
    qk = [beside(q_ref, k_ref, p) for p in range(2)]
    pack(0, [(0, qk[0], 0, 32, 0)])
    send_z(zs, zr, rows_of[0], 2)
    for load in loads[3:]:
        load.wait()
    settle(ogr, NY - 1, 0, sem_r)
    grad = jnp.zeros((256, 256), F32)
    for i in range(NY):
        y = (hd + i) % NY
        piece = og_ref[...] if i == 0 else ogr[pl.ds(y, 1)][0]
        grad += nt(piece, w_ref[:, pl.ds(pl.multiple_of(y * 256, 256), 256)])
    d_out = grad.astype(BF)
    vg = [beside(v_ref, d_out, p) for p in range(2)]
    pack(1, [(0, vg[0], 0, 24, 0), (0, qk[0], 32, CAP, -8)])
    send_z(zs, zr, rows_of[1], 3)
    pack(2, [(0, vg[0], 24, CAP, -24)])
    send_z(zs, zr, rows_of[2], 4)
    pack(3, [(1, qk[1], 0, 24, 0), (1, vg[1], 0, 24, 24)])
    send_z(zs, zr, rows_of[3], 20)
    pack(4, [(1, qk[1], 24, CAP, -24), (1, vg[1], 24, CAP, -8)])
    send_z(zs, zr, rows_of[4], 21)

    settle(meta_r, NZ - 1, 1, sem_r)
    r_i, l_i = iota((128, 128), 0), iota((128, 128), 1)
    meta_all = meta_r[...].reshape(128, 128)
    slot_row = ((l_i // 8) % 8) * 2 + (l_i // 2) % 2
    found = nn(meta_all, onehot((r_i % 16 == slot_row) & (r_i // 16 == z % 8)))
    half = r_i % 2 == (z // 8 + l_i // 64) % 2

    def slot(o):
        return (o // 8) * 4 + o % 4

    smaller = ((r_i // 4) % 2 == 0) & (slot(r_i) < slot(l_i))
    smaller = onehot(smaller & (r_i // 64 == l_i // 64))
    l16 = iota((16, 128), 1)
    first_kind = (l16 // 4) % 2 == 0
    for p in range(2):
        mine = jnp.where(half & ((r_i // 2) % 4 == 2 * p + l_i // 64), found, 0.0)
        held = jnp.sum(mine.reshape(16, 8, 128), axis=1)
        taken = held > (l16 % 2).astype(F32)
        t = nn(onehot(taken), smaller)
        fits = taken & (t < CAP_HEAD)
        t = jnp.where(l16 < 64, t, CAP - 1 - t)
        if p == 0:
            there = jnp.where(first_kind, jnp.where(t < 32, t, t + 24), jnp.where(t < 24, t + 32, t + 40))
        else:
            there = t + jnp.where(first_kind, 80.0, 104.0) + jnp.where(t < 24, 0.0, jnp.where(first_kind, 24.0, 16.0))
        there = jnp.where(fits, there, -1.0)
        tslot[p] = jnp.where(taken, there, jnp.where(first_kind, float(ROWS), -1.0))
        lower = jnp.where(t < HALF, t + CAP, -1.0)
        upper = jnp.where(t >= HALF, t + CAP - HALF, -1.0)
        tslot[2 + p] = jnp.where(fits, jnp.where(first_kind, t, lower), -1.0)
        tslot[4 + p] = jnp.where(fits, jnp.where(first_kind, t, upper), -1.0)
    pair = (l_i // 8 == r_i // 8) & ((l_i % 8) // 4 == (r_i % 8) // 2)
    pair = pair & ((l_i % 2 + (l_i // 2) % 2) % 2 == r_i % 2)
    places = nn(onehot(pair), meta_all).astype(BF)
    blocks = onehot(r_i // 16 == l_i)
    over = (nn(places, blocks) > CAP) | (nn(meta_all, blocks) > CAP_HEAD)
    over = jnp.max(jnp.where(over, 1.0, 0.0), axis=0, keepdims=True)
    full = jnp.broadcast_to(jnp.max(over, axis=1, keepdims=True), (8, 128))
    full_xs[...] = full
    full_xr[pl.ds(xc, 1)] = full[None]
    for i in range(1, NXC):
        remote(full_xs, full_xr.at[xc], 13, xpeer(i)[1])

    s_i, o_i = iota((256, 256), 0), iota((256, 256), 1)

    def source(o):
        return ((o // 32) % 2) * 128 + ((o // 2) % 16) * 8 + (o // 128) * 4 + ((o // 64) % 2) * 2 + o % 2

    perm = onehot(o_i == source(s_i))
    perm_back = onehot(s_i == source(o_i))
    mark = jnp.where((iota((16, 128), 0) == 0) & (iota((16, 128), 1) == 0), EMPTY, 0.0)
    mark = mark.astype(BF)

    def expand(p, h):
        first, n = ((0, 64), (0, 80), (80, 48), (80, 80))[2 * p + h]
        at = iota((n + 16, 64), 0)
        at = jnp.where(at < n, at + first, at - n + ROWS)
        for s in range(NZ):
            pick = onehot(at == tslot[p, s : s + 1, h * 64 : h * 64 + 64].astype(jnp.int32))
            rows = tn(pick, jnp.concatenate([zr[s, first : first + n, :], mark], axis=0))
            xs[p, h, :, s * 8 : s * 8 + 8, :] = rows.reshape(8, 8, 128).astype(BF)

    def work(p, h):
        for i in range(4):
            rows = nn(perm, xr[p, h, 2 * i : 2 * i + 2].reshape(256, 128)).astype(BF)
            for b in range(4):
                yb[b, i * 64 : (i + 1) * 64, :] = rows[b * 64 : (b + 1) * 64]
        for j in range(2):
            zb[j], zb[2 + j] = cluster_block(yb[j], yb[2 + j])
            total = jnp.sum(yb[j].astype(F32), axis=0, keepdims=True)
            (sum_own, sum_s)[h][j : j + 1, p * HD : (p + 1) * HD] = total[:, HD:]
        for i in range(4):
            rows = [zb[b, i * 64 : (i + 1) * 64, :] for b in range(4)]
            rows = nn(perm_back, jnp.concatenate(rows, axis=0)).astype(BF)
            xbs[p, h, 2 * i : 2 * i + 2] = rows.reshape(2, 128, 128)

    def compact_head0(p):
        at = iota((HEAD0, 64), 0)
        for s in range(NZ):
            back = xbr[p, 0, :, s * 8 : s * 8 + 8, :].reshape(64, 128)
            pick = at == tslot[2 + p, s : s + 1, 0:64].astype(jnp.int32)
            zbs[p, s, 0:HEAD0, :] = nn(onehot(pick), back).astype(BF)

    def compact_rest(p):
        low = iota((BACK - HEAD0, 128), 1) < HD
        at = iota((BACK - HEAD0, 128), 0) + HEAD0
        for s in range(NZ):
            back = xbr[p, :, :, s * 8 : s * 8 + 8, :].reshape(128, 128)
            first = nn(onehot(at == tslot[2 + p, s : s + 1, :].astype(jnp.int32)), back)
            second = nn(onehot(at == tslot[4 + p, s : s + 1, :].astype(jnp.int32)), back)
            zbs[p, s, HEAD0:BACK, :] = jnp.where(low, first, second).astype(BF)

    head0, rest = pl.ds(0, HEAD0), pl.ds(HEAD0, BACK - HEAD0)

    def forward(p, h):
        expand(p, h)
        send_x(xs, xr, p, h, 5 + 2 * p + h)

    def middle(p, h):
        wait_x(xs, xr, p, h, 5 + 2 * p + h)
        work(p, h)
        send_x(xbs, xbr, p, h, 9 + 2 * p + h)

    def back_head0(p):
        wait_x(xbs, xbr, p, 0, 9 + 2 * p)
        compact_head0(p)
        send_z(zbs.at[p], zbr.at[p], head0, 14 + 2 * p)

    def back_rest(p):
        wait_x(xbs, xbr, p, 1, 10 + 2 * p)
        compact_rest(p)
        send_z(zbs.at[p], zbr.at[p], rest, 15 + 2 * p)

    def wait_back(p):
        wait_z(zbs.at[p], zbr.at[p], head0, 14 + 2 * p)
        wait_z(zbs.at[p], zbr.at[p], rest, 15 + 2 * p)

    wait_z(zs, zr, rows_of[0], 2)
    wait_z(zs, zr, rows_of[1], 3)
    forward(0, 0)
    wait_z(zs, zr, rows_of[2], 4)
    forward(0, 1)
    settle(full_xr, NXC - 1, 13, sem_r)
    full = jnp.max(full_xr[...], axis=0)
    full_ys[...] = full
    for i in range(1, NY):
        remote(full_ys, full_yr.at[hd], 18, ypeer(i))
    middle(0, 0)
    middle(0, 1)
    wait_z(zs, zr, rows_of[3], 20)
    forward(1, 0)
    back_head0(0)
    wait_z(zs, zr, rows_of[4], 21)
    forward(1, 1)
    back_rest(0)
    middle(1, 0)
    middle(1, 1)
    remote(sum_s, sum_r, 19, zpeer(NZ // 2)[1])
    back_head0(1)
    back_rest(1)
    pltpu.make_async_copy(sum_r, sum_r, sem_r.at[19]).wait()
    for p in range(2):
        cols = slice(p * HD, (p + 1) * HD)
        cs_ref[:, p * 128 : (p + 1) * 128] = jnp.concatenate(
            [sum_own[0:2, cols], sum_r[0:2, cols]], axis=1
        )
    settle(full_yr, NY - 1, 18, sem_r)
    for i in range(1, NY):
        full = jnp.maximum(full, full_yr[pl.ds((hd + i) % NY, 1)][0])
    full_ref[0, 0] = jnp.max(full).astype(jnp.int32)
    wait_back(0)
    for i, part in enumerate(unpack(0, zbr[0].reshape(NZ * BACK, 128), tcol)):
        done_ref[i] = part
    wait_back(1)
    rest_ref[...] = zbr[1].reshape(NZ * BACK, 128)

    for i in range(1, NY):
        pltpu.make_async_copy(og_ref, og_ref, sem_s.at[0]).wait()
        pltpu.make_async_copy(full_ys, full_ys, sem_s.at[18]).wait()
    for i in range(1, NZ):
        pltpu.make_async_copy(meta_s, meta_s, sem_s.at[1]).wait()
    for i in range(1, NXC):
        pltpu.make_async_copy(full_xs, full_xs, sem_s.at[13]).wait()
    pltpu.make_async_copy(sum_s, sum_s, sem_s.at[19]).wait()
    for rows, sem in zip(rows_of, (2, 3, 4, 20, 21)):
        settle(zs, NZ - 1, sem, sem_s, rows)
    for p in range(2):
        for h in range(2):
            settle(xs.at[p, h], NXC - 1, 5 + 2 * p + h, sem_s)
            settle(xbs.at[p, h], NXC - 1, 9 + 2 * p + h, sem_s)
        settle(zbs.at[p], NZ - 1, 14 + 2 * p, sem_s, head0)
        settle(zbs.at[p], NZ - 1, 15 + 2 * p, sem_s, rest)


def two_hop(queries, keys, values, out_grad, w_out, cluster_ids):
    frames, width = queries.shape
    heads = cluster_ids.shape[0]
    vmem = pl.BlockSpec(memory_space=pltpu.VMEM)

    def buf(*shape, dtype=BF):
        return pltpu.VMEM(shape, dtype)

    return pl.pallas_call(
        kernel,
        name="two_hop",
        out_shape=(
            jax.ShapeDtypeStruct((3, frames, width // 2), BF),
            jax.ShapeDtypeStruct((NZ * BACK, 128), BF),
            jax.ShapeDtypeStruct((frames, 128), F32),
            jax.ShapeDtypeStruct((2, width), F32),
            jax.ShapeDtypeStruct((1, 1), jnp.int32),
        ),
        in_specs=[pl.BlockSpec(memory_space=pl.ANY)] * 6,
        out_specs=(vmem,) * 4 + (pl.BlockSpec(memory_space=pltpu.SMEM),),
        scratch_shapes=[
            buf(frames, width),
            buf(frames, width),
            buf(frames, width),
            buf(frames, width),
            buf(width, NY * width),
            buf(heads, 1, frames, dtype=jnp.int32),
            buf(NY, frames, width),
            buf(8, 128),
            buf(NZ, 8, 128),
            buf(NZ, ROWS, 128),
            buf(NZ, ROWS, 128),
            buf(2, 2, NXC, NZ * 8, 128),
            buf(2, 2, NXC, NZ * 8, 128),
            buf(4, 256, 128),
            buf(4, 256, 128),
            buf(2, 2, NXC, NZ * 8, 128),
            buf(2, 2, NXC, NZ * 8, 128),
            buf(2, NZ, BACK, 128),
            buf(2, NZ, BACK, 128),
            buf(6, NZ, 128, dtype=F32),
            buf(8, 128, dtype=F32),
            buf(8, 128, dtype=F32),
            buf(8, 128, dtype=F32),
            buf(8, 128, dtype=F32),
            buf(NXC, 8, 128, dtype=F32),
            buf(8, 128, dtype=F32),
            buf(NY, 8, 128, dtype=F32),
            pltpu.SemaphoreType.DMA((22,)),
            pltpu.SemaphoreType.DMA((22,)),
            pltpu.SemaphoreType.DMA((22,)),
            pltpu.SemaphoreType.DMA((6,)),
        ],
        compiler_params=pltpu.CompilerParams(
            collective_id=0, has_side_effects=True, vmem_limit_bytes=48 << 20
        ),
    )(queries, keys, values, out_grad, w_out, cluster_ids.reshape(heads, 1, frames))


def padded_block(block, live):
    q_rows = block[:, :HD]
    k_rows = block[:, HD : 2 * HD]
    v_rows = block[:, 2 * HD : 3 * HD]
    g_rows = block[:, 3 * HD :]
    scores = 0.125 * jnp.dot(q_rows, k_rows.T, preferred_element_type=jnp.float32)
    scores = jnp.where(live[None, :], scores, jnp.float32(-1e30))
    top = jnp.max(scores, axis=1, keepdims=True)
    expo = jnp.exp(scores - top)
    probs = expo / jnp.sum(expo, axis=1, keepdims=True)
    probs_low = probs.astype(jnp.bfloat16)
    attended = jnp.dot(probs_low, v_rows, preferred_element_type=jnp.float32)
    delta = jnp.sum(g_rows.astype(jnp.float32) * attended, axis=1, keepdims=True)
    dprobs = jnp.dot(g_rows, v_rows.T, preferred_element_type=jnp.float32)
    dscores = (probs * (dprobs - delta)).astype(jnp.bfloat16)
    dq_rows = (0.125 * jnp.dot(dscores, k_rows, preferred_element_type=jnp.float32)).astype(
        jnp.bfloat16
    )
    dk_rows = (0.125 * jnp.dot(dscores.T, q_rows, preferred_element_type=jnp.float32)).astype(
        jnp.bfloat16
    )
    dv_rows = jnp.dot(probs_low.T, g_rows, preferred_element_type=jnp.float32).astype(jnp.bfloat16)
    return jnp.concatenate([dq_rows, dk_rows, dv_rows], axis=1)


def padded_attend(received, per_owner):
    count_items = received.shape[0]
    owners = received.shape[1]
    capacity = owners * MOST
    blocks = received.reshape(count_items, owners, per_owner, MOST, 4 * HD)
    blocks = blocks.transpose(0, 2, 1, 3, 4).reshape(count_items * per_owner, capacity, 4 * HD)
    live = blocks[:, :, 0] < EMPTY / 2
    grads = lax.map(lambda pair: padded_block(pair[0], pair[1]), (blocks, live))
    grads = grads.reshape(count_items, per_owner, owners, MOST, 3 * HD).transpose(0, 2, 1, 3, 4)
    returned = grads.reshape(count_items, owners, per_owner * MOST, 3 * HD)
    key_sums = jnp.sum(blocks[:, :, HD : 2 * HD].astype(jnp.float32), axis=1).reshape(
        count_items, per_owner, HD
    )
    return (returned, key_sums)


def padded(queries, keys, values, out_grad, w_out, cluster_ids):
    frames = queries.shape[0]
    heads = cluster_ids.shape[0]
    owners = lax.axis_size("seq")
    per_owner = CLUSTERS // owners
    d_out = lax.dot_general(
        lax.all_gather(out_grad, "head", axis=1, tiled=True),
        w_out,
        (((1,), (1,)), ((), ())),
        preferred_element_type=jnp.float32,
    ).astype(jnp.bfloat16)

    def split_heads(array):
        return array.reshape(frames, heads, HD).transpose(1, 0, 2)

    key_heads = split_heads(keys)
    rows = jnp.concatenate(
        [split_heads(queries), key_heads, split_heads(values), split_heads(d_out)], axis=2
    )
    ids = cluster_ids[:, :, 0]
    member = (ids[:, :, None] == jnp.arange(CLUSTERS, dtype=jnp.int32)[None, None, :]).astype(
        jnp.int32
    )
    running = jnp.cumsum(member, axis=1)
    rank = jnp.sum(member * (running - 1), axis=2)
    slot = ids * MOST + rank
    flat_index = (jnp.arange(heads, dtype=jnp.int32)[:, None] * (CLUSTERS * MOST) + slot).reshape(
        -1
    )
    empty_row = jnp.where(jnp.arange(4 * HD) == 0, EMPTY, 0.0).astype(jnp.bfloat16)
    outgoing = (
        jnp.broadcast_to(empty_row, (heads * CLUSTERS * MOST, 4 * HD))
        .at[flat_index]
        .set(rows.reshape(-1, 4 * HD))
    )
    outgoing = outgoing.reshape(heads, owners, per_owner * MOST, 4 * HD)
    received = lax.all_to_all(outgoing, "seq", split_axis=1, concat_axis=1, tiled=True)
    returned, key_sums = padded_attend(received, per_owner)
    arrived = lax.all_to_all(returned, "seq", split_axis=1, concat_axis=1, tiled=True)
    picked = arrived.reshape(heads * CLUSTERS * MOST, 3 * HD)[flat_index].reshape(
        heads, frames, 3 * HD
    )

    def join_heads(part):
        return part.transpose(1, 0, 2).reshape(frames, heads * HD)

    query_grad = join_heads(picked[:, :, :HD])
    key_grad = join_heads(picked[:, :, HD : 2 * HD])
    value_grad = join_heads(picked[:, :, 2 * HD :])
    centroid_sums = key_sums.transpose(1, 0, 2).reshape(per_owner, heads * HD)
    return (query_grad, key_grad, value_grad, centroid_sums)


def last_step(done, rest, tcol, sums):
    frames, width = done.shape[1], 2 * done.shape[2]
    vmem = pl.BlockSpec(memory_space=pltpu.VMEM)
    grad = jax.ShapeDtypeStruct((frames, width), BF)
    return pl.pallas_call(
        last_kernel,
        name="last_step",
        out_shape=(grad, grad, grad, jax.ShapeDtypeStruct(sums.shape, F32)),
        in_specs=[vmem] * 4,
        out_specs=(vmem,) * 4,
        compiler_params=pltpu.CompilerParams(vmem_limit_bytes=16 << 20),
    )(done, rest, tcol, sums)


def as_parts(dq, dk, dv, sums):
    frames = dq.shape[0]
    done = jnp.stack([x[:, :128] for x in (dq, dk, dv)])
    rest = [jnp.concatenate([dk[:, at : at + HD], dq[:, at : at + HD]], axis=1) for at in (128, 192)]
    rest = jnp.concatenate(rest + [dv[:, 128:], jnp.zeros((NZ * BACK - 3 * frames, 128), BF)])
    at = jnp.arange(frames, dtype=F32)[:, None]
    none = jnp.full((frames, 1), -1.0, F32)
    second = [at, at + 2 * frames, none, at + frames, none, at + 2 * frames]
    cols = [jnp.zeros((frames, 6), F32)] + second + [jnp.zeros((frames, 116), F32)]
    return done, rest, jnp.concatenate(cols, axis=1), sums


def shards(*args):
    *parts, full = two_hop(*args)
    parts = lax.switch(full[0, 0], [lambda: tuple(parts), lambda: as_parts(*padded(*args))])
    return tuple(last_step(*parts))


def solution(mesh):
    placed = (
        P("seq", "head"),
        P("seq", "head"),
        P("seq", "head"),
        P("seq", "head"),
        P("head", None),
        P("head", "seq", None),
    )
    return jax.shard_map(
        shards,
        mesh=mesh,
        in_specs=placed,
        out_specs=(P("seq", "head"), P("seq", "head"), P("seq", "head"), P("seq", "head")),
        check_vma=False,
    )
```

```python
import functools

import jax
import jax.numpy as jnp
from jax import lax
from jax.experimental import pallas as pl
from jax.experimental.pallas import tpu as pltpu
from jax.sharding import PartitionSpec as P

HD = 64
CLUSTERS = 256
MOST = 2
EMPTY = 64.0
MESH = pl.DeviceIdType.MESH
BF = jnp.bfloat16
F32 = jnp.float32
NZ = 16
NXC = 8
NY = 4
CAP = 40
CAP_HEAD = 24
HEAD0 = CAP - CAP_HEAD
HALF = 24
BACK = CAP + HALF
PARTS = ((0, 32), (32, 16), (48, 32), (80, 16), (96, 32), (128, 32))
NEEDS = (((0, 80),), ((0, 96),), ((32, 16), (96, 32)), ((96, 64),))
ROWS = 160


def iota(shape, dim):
    return lax.broadcasted_iota(jnp.int32, shape, dim)


def onehot(cond):
    return jnp.where(cond, 1.0, 0.0).astype(BF)


def nn(a, b):
    return jnp.dot(a, b, preferred_element_type=F32)


def nt(a, b):
    return lax.dot_general(a, b, (((1,), (1,)), ((), ())), preferred_element_type=F32)


def tn(a, b):
    return lax.dot_general(a, b, (((0,), (0,)), ((), ())), preferred_element_type=F32)


def swap_halves(x):
    return jnp.concatenate([x[:, HD:], x[:, :HD]], axis=1)


def cluster_block(qk, vg):
    low = iota((256, 2 * HD), 1) < HD
    q, k = qk[:, :HD], qk[:, HD:]
    v, g = vg[:, :HD], vg[:, HD:]
    live = qk[:, 0:1].astype(F32) < EMPTY / 2
    scores = jnp.where(live, 0.125 * nt(k, q), jnp.float32(-1e30))
    expo = jnp.exp(scores - jnp.max(scores, axis=0, keepdims=True))
    probs = expo / jnp.sum(expo, axis=0, keepdims=True)
    probs_low = probs.astype(BF)
    dprobs = nt(v, g)
    delta = jnp.sum(probs_low.astype(F32) * dprobs, axis=0, keepdims=True)
    dscores = (probs * (dprobs - delta)).astype(BF)
    dk = 0.125 * nn(dscores, qk)
    dq = 0.125 * tn(dscores, qk)
    dv = nn(probs_low, vg)
    return jnp.where(low, dk, dq).astype(BF), jnp.where(low, swap_halves(dv), dv).astype(BF)


def unpack(p, rows, tcol):
    keys, values, queries = [], [], []
    at = iota((256, NZ * BACK), 1)
    for h in (2 * p, 2 * p + 1):
        cols = tcol[:, 3 * h : 3 * h + 3].astype(jnp.int32)
        got = nn(onehot(at == cols[:, 0:1]), rows)
        first = nn(onehot(at == cols[:, 1:2]), rows)
        second = nn(onehot(at == cols[:, 2:3]), rows)
        keys.append(got[:, :HD])
        queries.append(got[:, HD:])
        values.append(first[:, :HD] + second[:, HD:])
    return [jnp.concatenate(x, axis=1).astype(BF) for x in (queries, keys, values)]


def last_kernel(done_ref, rest_ref, tcol, cs_in, dq_ref, dk_ref, dv_ref, cs_ref):
    cs_ref[...] = cs_in[...]
    parts = unpack(1, rest_ref[...], tcol)
    for i, ref in enumerate((dq_ref, dk_ref, dv_ref)):
        ref[:, 0:128] = done_ref[i]
        ref[:, 128:256] = parts[i]


def kernel(
    q_hbm, k_hbm, v_hbm, og_hbm, w_hbm, ids_hbm,
    done_ref, rest_ref, tcol, cs_ref, full_ref,
    q_ref, k_ref, v_ref, og_ref, w_ref, ids_ref, ogr, meta_s, meta_r, zs, zr, xs, xr, yb, zb, xbs, xbr, zbs, zbr, tslot,
    sum_own, sum_s, sum_r, full_xs, full_xr, full_ys, full_yr,
    sem_s, sem_r, sem_l, sem_in,
):
    me, hd = lax.axis_index("seq"), lax.axis_index("head")
    x, z, c = me // (2 * NZ), (me // 2) % NZ, me % 2
    xc = x * 2 + c

    def zpeer(i):
        to = (z + i) % NZ
        return to, (x * (2 * NZ) + to * 2 + c, hd)

    def xpeer(i):
        to = (xc + i) % NXC
        return to, ((to // 2) * (2 * NZ) + z * 2 + to % 2, hd)

    def ypeer(i):
        return (me, (hd + i) % NY)

    zorder = [8, 7, 9, 6, 10, 5, 11, 4, 12, 3, 13, 2, 14, 1, 15]
    barrier = pltpu.get_barrier_semaphore()
    peers = [ypeer(i) for i in range(1, NY)]
    peers += [zpeer(i)[1] for i in range(1, NZ)] + [xpeer(i)[1] for i in range(1, NXC)]
    for peer in peers:
        pl.semaphore_signal(barrier, inc=1, device_id=peer, device_id_type=MESH)

    loads = [
        pltpu.make_async_copy(src, dst, sem_in.at[i])
        for i, (src, dst) in enumerate(
            ((ids_hbm, ids_ref), (q_hbm, q_ref), (k_hbm, k_ref),
             (og_hbm, og_ref), (v_hbm, v_ref), (w_hbm, w_ref))
        )
    ]
    for load in loads:
        load.start()
    loads[0].wait()

    sub, lane = iota((256, 256), 0), iota((256, 256), 1)
    earlier = onehot(sub < lane)
    ones = jnp.ones((256, 256), BF)
    before = onehot((sub // 16 == lane // 16) & (lane < sub))
    member, count, zof, poses, targets = [], [], [], [], []

    def place_rows(h):
        ids = ids_ref[h]
        row = ((ids >> 2) & 15) * 16 + (ids >> 6) * 4 + (ids & 3)
        zof.append((((row >> 4) + (h % 2) * (NZ // 2)) & (NZ - 1)).astype(F32))
        member.append(onehot(sub == row))
        count.append(nn(member[h], ones).astype(BF))
        place = nn(before, count[h]) + nn(member[h], earlier)
        nth = jnp.sum(member[h].astype(F32) * place, axis=0, keepdims=True)
        fits = nth < CAP_HEAD
        pos = nth if h % 2 == 0 else CAP - 1 - nth
        poses.append(jnp.where(fits, pos, -1.0))
        back = zof[h] * BACK + pos
        targets.append(jnp.where(fits, back, -1.0))
        targets.append(jnp.where(fits & (pos < HALF), back + CAP, -1.0))
        targets.append(jnp.where(fits & (pos >= HALF), back + CAP - HALF, -1.0))

    def beside(a_ref, b, p):
        a = a_ref[:, p * 128 : (p + 1) * 128].astype(F32)
        b = b[:, p * 128 : (p + 1) * 128].astype(F32)
        low = iota((256, 128), 1) < HD
        return (
            jnp.where(low, a, swap_halves(b)).astype(BF),
            jnp.where(low, swap_halves(a), b).astype(BF),
        )

    def pack(part, pieces):
        at, n = PARTS[part]
        goals, rows = [], []
        for p, pair, first, last, to in pieces:
            for i in range(2):
                pos = poses[2 * p + i]
                fits = (pos >= first) & (pos < last)
                goals.append(jnp.where(fits, zof[2 * p + i] * n + pos + to, -1.0))
                rows.append(pair[i])
        goals = jnp.concatenate(goals, axis=1).astype(jnp.int32)
        rows = jnp.concatenate(rows, axis=0)
        for i in range(4):
            pick = onehot(iota((4 * n, goals.shape[1]), 0) + i * 4 * n == goals)
            zs[i * 4 : i * 4 + 4, at : at + n, :] = nn(pick, rows).astype(BF).reshape(4, n, 128)

    for h in range(2):
        place_rows(h)
    loads[1].wait()
    loads[2].wait()
    qk = [beside(q_ref, k_ref, 0)]
    pack(0, [(0, qk[0], 0, 32, 0)])

    pl.semaphore_wait(barrier, NY - 1 + NZ - 1 + NXC - 1)

    def remote(src, dst, sem, peer):
        pltpu.make_async_remote_copy(
            src_ref=src, dst_ref=dst, send_sem=sem_s.at[sem], recv_sem=sem_r.at[sem],
            device_id=peer, device_id_type=MESH,
        ).start()

    def settle(buf, n, sem, which, rows=None):
        part = buf.at[pl.ds(0, n)] if rows is None else buf.at[pl.ds(0, n), rows]
        pltpu.make_async_copy(part, part, which.at[sem]).wait()

    for i in range(1, NY):
        remote(og_hbm, ogr.at[hd], 0, ypeer(i))
    def send_z(src, dst, rows, sem):
        for i in zorder:
            to, peer = zpeer(i)
            remote(src.at[to, rows], dst.at[z, rows], sem, peer)
        pltpu.make_async_copy(src.at[z, rows], dst.at[z, rows], sem_l.at[sem]).start()

    def wait_z(src, dst, rows, sem):
        settle(dst, NZ - 1, sem, sem_r, rows)
        pltpu.make_async_copy(src.at[z, rows], dst.at[z, rows], sem_l.at[sem]).wait()

    def send_x(src, dst, p, i, sem):
        for step in range(1, NXC):
            to, peer = xpeer(step)
            remote(src.at[p, i, to], dst.at[p, i, xc], sem, peer)
        pltpu.make_async_copy(src.at[p, i, xc], dst.at[p, i, xc], sem_l.at[sem]).start()

    def wait_x(src, dst, p, i, sem):
        settle(dst.at[p, i], NXC - 1, sem, sem_r)
        pltpu.make_async_copy(src.at[p, i, xc], dst.at[p, i, xc], sem_l.at[sem]).wait()

    rows_of = [pl.ds(at, n) for at, n in PARTS]
    send_z(zs, zr, rows_of[0], 2)
    for h in range(2, 4):
        place_rows(h)
    qk.append(beside(q_ref, k_ref, 1))
    pack(1, [(1, qk[1], 0, 16, 0)])
    send_z(zs, zr, rows_of[1], 3)
    meta = jnp.zeros((8, 128), F32)
    mrow = iota((8, 128), 0)
    for h in range(4):
        held = nt(jnp.ones((8, 256), BF), member[h])
        meta = jnp.where(mrow == 2 * h, held[:, :128], meta)
        meta = jnp.where(mrow == 2 * h + 1, held[:, 128:], meta)
    meta_s[...] = meta.astype(BF)
    meta_r[pl.ds(z, 1)] = meta.astype(BF)[None]
    for i in zorder:
        remote(meta_s, meta_r.at[z], 1, zpeer(i)[1])
    tcol[...] = jnp.concatenate(targets + [jnp.zeros((128 - 12, 256), F32)], axis=0).T
    for load in loads[3:]:
        load.wait()
    grad = jnp.zeros((256, 256), F32)
    for i in range(NY):
        y = (hd + i) % NY
        if i == 1:
            settle(ogr, NY - 1, 0, sem_r)
        piece = og_ref[...] if i == 0 else ogr[pl.ds(y, 1)][0]
        grad += nt(piece, w_ref[:, pl.ds(pl.multiple_of(y * 256, 256), 256)])
    d_out = grad.astype(BF)
    vg = [beside(v_ref, d_out, p) for p in range(2)]
    pack(2, [(0, vg[0], 0, 24, 0), (0, qk[0], 32, CAP, -8)])
    send_z(zs, zr, rows_of[2], 4)
    pack(3, [(0, vg[0], 24, CAP, -24)])
    send_z(zs, zr, rows_of[3], 20)
    pack(4, [(1, vg[1], 0, 24, 0), (1, qk[1], 16, 24, 8)])
    send_z(zs, zr, rows_of[4], 21)
    pack(5, [(1, qk[1], 24, CAP, -24), (1, vg[1], 24, CAP, -8)])
    send_z(zs, zr, rows_of[5], 22)

    settle(meta_r, NZ - 1, 1, sem_r)
    r_i, l_i = iota((128, 128), 0), iota((128, 128), 1)
    meta_all = meta_r[...].reshape(128, 128)
    slot_row = ((l_i // 8) % 8) * 2 + (l_i // 2) % 2
    found = nn(meta_all, onehot((r_i % 16 == slot_row) & (r_i // 16 == z % 8)))
    half = r_i % 2 == (z // 8 + l_i // 64) % 2

    def slot(o):
        return (o // 8) * 4 + o % 4

    smaller = ((r_i // 4) % 2 == 0) & (slot(r_i) < slot(l_i))
    smaller = onehot(smaller & (r_i // 64 == l_i // 64))
    l16 = iota((16, 128), 1)
    first_kind = (l16 // 4) % 2 == 0
    for p in range(2):
        mine = jnp.where(half & ((r_i // 2) % 4 == 2 * p + l_i // 64), found, 0.0)
        held = jnp.sum(mine.reshape(16, 8, 128), axis=1)
        taken = held > (l16 % 2).astype(F32)
        t = nn(onehot(taken), smaller)
        fits = taken & (t < CAP_HEAD)
        t = jnp.where(l16 < 64, t, CAP - 1 - t)
        if p == 0:
            there = jnp.where(first_kind, jnp.where(t < 32, t, t + 40), jnp.where(t < 24, t + 48, t + 56))
        else:
            there = jnp.where(first_kind, jnp.where(t < 16, t + 32, t + 104), jnp.where(t < 24, t + 96, t + 120))
        there = jnp.where(fits, there, -1.0)
        tslot[p] = jnp.where(taken, there, jnp.where(first_kind, float(ROWS), -1.0))
        lower = jnp.where(t < HALF, t + CAP, -1.0)
        upper = jnp.where(t >= HALF, t + CAP - HALF, -1.0)
        tslot[2 + p] = jnp.where(fits, jnp.where(first_kind, t, lower), -1.0)
        tslot[4 + p] = jnp.where(fits, jnp.where(first_kind, t, upper), -1.0)
    pair = (l_i // 8 == r_i // 8) & ((l_i % 8) // 4 == (r_i % 8) // 2)
    pair = pair & ((l_i % 2 + (l_i // 2) % 2) % 2 == r_i % 2)
    places = nn(onehot(pair), meta_all).astype(BF)
    blocks = onehot(r_i // 16 == l_i)
    over = (nn(places, blocks) > CAP) | (nn(meta_all, blocks) > CAP_HEAD)
    over = jnp.max(jnp.where(over, 1.0, 0.0), axis=0, keepdims=True)
    full = jnp.broadcast_to(jnp.max(over, axis=1, keepdims=True), (8, 128))
    full_xs[...] = full
    full_xr[pl.ds(xc, 1)] = full[None]
    for i in range(1, NXC):
        remote(full_xs, full_xr.at[xc], 13, xpeer(i)[1])

    s_i, o_i = iota((256, 256), 0), iota((256, 256), 1)

    def source(o):
        return ((o // 32) % 2) * 128 + ((o // 2) % 16) * 8 + (o // 128) * 4 + ((o // 64) % 2) * 2 + o % 2

    perm = onehot(o_i == source(s_i))
    perm_back = onehot(s_i == source(o_i))
    mark = jnp.where((iota((16, 128), 0) == 0) & (iota((16, 128), 1) == 0), EMPTY, 0.0)
    mark = mark.astype(BF)

    def expand(p, h):
        needs = NEEDS[2 * p + h]
        i = iota((sum(n for _, n in needs) + 16, 64), 0)
        at, done = i - i.shape[0] + 16 + ROWS, i.shape[0] - 16
        for first, n in reversed(needs):
            done -= n
            at = jnp.where(i < done + n, i - done + first, at)
        for s in range(NZ):
            pick = onehot(at == tslot[p, s : s + 1, h * 64 : h * 64 + 64].astype(jnp.int32))
            rows = [zr[s, first : first + n, :] for first, n in needs]
            rows = tn(pick, jnp.concatenate(rows + [mark], axis=0))
            xs[p, h, :, s * 8 : s * 8 + 8, :] = rows.reshape(8, 8, 128).astype(BF)

    def work(p, h):
        for i in range(4):
            rows = nn(perm, xr[p, h, 2 * i : 2 * i + 2].reshape(256, 128)).astype(BF)
            for b in range(4):
                yb[b, i * 64 : (i + 1) * 64, :] = rows[b * 64 : (b + 1) * 64]
        for j in range(2):
            zb[j], zb[2 + j] = cluster_block(yb[j], yb[2 + j])
            total = jnp.sum(yb[j].astype(F32), axis=0, keepdims=True)
            (sum_own, sum_s)[h][j : j + 1, p * HD : (p + 1) * HD] = total[:, HD:]
        for i in range(4):
            rows = [zb[b, i * 64 : (i + 1) * 64, :] for b in range(4)]
            rows = nn(perm_back, jnp.concatenate(rows, axis=0)).astype(BF)
            xbs[p, h, 2 * i : 2 * i + 2] = rows.reshape(2, 128, 128)

    def compact_head0(p):
        at = iota((HEAD0, 64), 0)
        for s in range(NZ):
            back = xbr[p, 0, :, s * 8 : s * 8 + 8, :].reshape(64, 128)
            pick = at == tslot[2 + p, s : s + 1, 0:64].astype(jnp.int32)
            zbs[p, s, 0:HEAD0, :] = nn(onehot(pick), back).astype(BF)

    def compact_rest(p):
        low = iota((BACK - HEAD0, 128), 1) < HD
        at = iota((BACK - HEAD0, 128), 0) + HEAD0
        for s in range(NZ):
            back = xbr[p, :, :, s * 8 : s * 8 + 8, :].reshape(128, 128)
            first = nn(onehot(at == tslot[2 + p, s : s + 1, :].astype(jnp.int32)), back)
            second = nn(onehot(at == tslot[4 + p, s : s + 1, :].astype(jnp.int32)), back)
            zbs[p, s, HEAD0:BACK, :] = jnp.where(low, first, second).astype(BF)

    head0, rest = pl.ds(0, HEAD0), pl.ds(HEAD0, BACK - HEAD0)

    def forward(p, h):
        expand(p, h)
        send_x(xs, xr, p, h, 5 + 2 * p + h)

    def middle(p, h):
        wait_x(xs, xr, p, h, 5 + 2 * p + h)
        work(p, h)
        send_x(xbs, xbr, p, h, 9 + 2 * p + h)

    def back_head0(p):
        wait_x(xbs, xbr, p, 0, 9 + 2 * p)
        compact_head0(p)
        send_z(zbs.at[p], zbr.at[p], head0, 14 + 2 * p)

    def back_rest(p):
        wait_x(xbs, xbr, p, 1, 10 + 2 * p)
        compact_rest(p)
        send_z(zbs.at[p], zbr.at[p], rest, 15 + 2 * p)

    def wait_back(p):
        wait_z(zbs.at[p], zbr.at[p], head0, 14 + 2 * p)
        wait_z(zbs.at[p], zbr.at[p], rest, 15 + 2 * p)

    wait_z(zs, zr, rows_of[0], 2)
    wait_z(zs, zr, rows_of[1], 3)
    wait_z(zs, zr, rows_of[2], 4)
    forward(0, 0)
    wait_z(zs, zr, rows_of[3], 20)
    forward(0, 1)
    settle(full_xr, NXC - 1, 13, sem_r)
    full = jnp.max(full_xr[...], axis=0)
    full_ys[...] = full
    for i in range(1, NY):
        remote(full_ys, full_yr.at[hd], 18, ypeer(i))
    middle(0, 0)
    middle(0, 1)
    wait_z(zs, zr, rows_of[4], 21)
    forward(1, 0)
    back_head0(0)
    wait_z(zs, zr, rows_of[5], 22)
    forward(1, 1)
    back_rest(0)
    middle(1, 0)
    middle(1, 1)
    remote(sum_s, sum_r, 19, zpeer(NZ // 2)[1])
    back_head0(1)
    back_rest(1)
    pltpu.make_async_copy(sum_r, sum_r, sem_r.at[19]).wait()
    for p in range(2):
        cols = slice(p * HD, (p + 1) * HD)
        cs_ref[:, p * 128 : (p + 1) * 128] = jnp.concatenate(
            [sum_own[0:2, cols], sum_r[0:2, cols]], axis=1
        )
    settle(full_yr, NY - 1, 18, sem_r)
    for i in range(1, NY):
        full = jnp.maximum(full, full_yr[pl.ds((hd + i) % NY, 1)][0])
    full_ref[0, 0] = jnp.max(full).astype(jnp.int32)
    wait_back(0)
    for i, part in enumerate(unpack(0, zbr[0].reshape(NZ * BACK, 128), tcol)):
        done_ref[i] = part
    wait_back(1)
    rest_ref[...] = zbr[1].reshape(NZ * BACK, 128)

    for i in range(1, NY):
        pltpu.make_async_copy(og_ref, og_ref, sem_s.at[0]).wait()
        pltpu.make_async_copy(full_ys, full_ys, sem_s.at[18]).wait()
    for i in range(1, NZ):
        pltpu.make_async_copy(meta_s, meta_s, sem_s.at[1]).wait()
    for i in range(1, NXC):
        pltpu.make_async_copy(full_xs, full_xs, sem_s.at[13]).wait()
    pltpu.make_async_copy(sum_s, sum_s, sem_s.at[19]).wait()
    for rows, sem in zip(rows_of, (2, 3, 4, 20, 21, 22)):
        settle(zs, NZ - 1, sem, sem_s, rows)
    for p in range(2):
        for h in range(2):
            settle(xs.at[p, h], NXC - 1, 5 + 2 * p + h, sem_s)
            settle(xbs.at[p, h], NXC - 1, 9 + 2 * p + h, sem_s)
        settle(zbs.at[p], NZ - 1, 14 + 2 * p, sem_s, head0)
        settle(zbs.at[p], NZ - 1, 15 + 2 * p, sem_s, rest)


def two_hop(queries, keys, values, out_grad, w_out, cluster_ids):
    frames, width = queries.shape
    heads = cluster_ids.shape[0]
    vmem = pl.BlockSpec(memory_space=pltpu.VMEM)

    def buf(*shape, dtype=BF):
        return pltpu.VMEM(shape, dtype)

    return pl.pallas_call(
        kernel,
        name="two_hop",
        out_shape=(
            jax.ShapeDtypeStruct((3, frames, width // 2), BF),
            jax.ShapeDtypeStruct((NZ * BACK, 128), BF),
            jax.ShapeDtypeStruct((frames, 128), F32),
            jax.ShapeDtypeStruct((2, width), F32),
            jax.ShapeDtypeStruct((1, 1), jnp.int32),
        ),
        in_specs=[pl.BlockSpec(memory_space=pl.ANY)] * 6,
        out_specs=(vmem,) * 4 + (pl.BlockSpec(memory_space=pltpu.SMEM),),
        scratch_shapes=[
            buf(frames, width),
            buf(frames, width),
            buf(frames, width),
            buf(frames, width),
            buf(width, NY * width),
            buf(heads, 1, frames, dtype=jnp.int32),
            buf(NY, frames, width),
            buf(8, 128),
            buf(NZ, 8, 128),
            buf(NZ, ROWS, 128),
            buf(NZ, ROWS, 128),
            buf(2, 2, NXC, NZ * 8, 128),
            buf(2, 2, NXC, NZ * 8, 128),
            buf(4, 256, 128),
            buf(4, 256, 128),
            buf(2, 2, NXC, NZ * 8, 128),
            buf(2, 2, NXC, NZ * 8, 128),
            buf(2, NZ, BACK, 128),
            buf(2, NZ, BACK, 128),
            buf(6, NZ, 128, dtype=F32),
            buf(8, 128, dtype=F32),
            buf(8, 128, dtype=F32),
            buf(8, 128, dtype=F32),
            buf(8, 128, dtype=F32),
            buf(NXC, 8, 128, dtype=F32),
            buf(8, 128, dtype=F32),
            buf(NY, 8, 128, dtype=F32),
            pltpu.SemaphoreType.DMA((23,)),
            pltpu.SemaphoreType.DMA((23,)),
            pltpu.SemaphoreType.DMA((23,)),
            pltpu.SemaphoreType.DMA((6,)),
        ],
        compiler_params=pltpu.CompilerParams(
            collective_id=0, has_side_effects=True, vmem_limit_bytes=48 << 20
        ),
    )(queries, keys, values, out_grad, w_out, cluster_ids.reshape(heads, 1, frames))


def padded_block(block, live):
    q_rows = block[:, :HD]
    k_rows = block[:, HD : 2 * HD]
    v_rows = block[:, 2 * HD : 3 * HD]
    g_rows = block[:, 3 * HD :]
    scores = 0.125 * jnp.dot(q_rows, k_rows.T, preferred_element_type=jnp.float32)
    scores = jnp.where(live[None, :], scores, jnp.float32(-1e30))
    top = jnp.max(scores, axis=1, keepdims=True)
    expo = jnp.exp(scores - top)
    probs = expo / jnp.sum(expo, axis=1, keepdims=True)
    probs_low = probs.astype(jnp.bfloat16)
    attended = jnp.dot(probs_low, v_rows, preferred_element_type=jnp.float32)
    delta = jnp.sum(g_rows.astype(jnp.float32) * attended, axis=1, keepdims=True)
    dprobs = jnp.dot(g_rows, v_rows.T, preferred_element_type=jnp.float32)
    dscores = (probs * (dprobs - delta)).astype(jnp.bfloat16)
    dq_rows = (0.125 * jnp.dot(dscores, k_rows, preferred_element_type=jnp.float32)).astype(
        jnp.bfloat16
    )
    dk_rows = (0.125 * jnp.dot(dscores.T, q_rows, preferred_element_type=jnp.float32)).astype(
        jnp.bfloat16
    )
    dv_rows = jnp.dot(probs_low.T, g_rows, preferred_element_type=jnp.float32).astype(jnp.bfloat16)
    return jnp.concatenate([dq_rows, dk_rows, dv_rows], axis=1)


def padded_attend(received, per_owner):
    count_items = received.shape[0]
    owners = received.shape[1]
    capacity = owners * MOST
    blocks = received.reshape(count_items, owners, per_owner, MOST, 4 * HD)
    blocks = blocks.transpose(0, 2, 1, 3, 4).reshape(count_items * per_owner, capacity, 4 * HD)
    live = blocks[:, :, 0] < EMPTY / 2
    grads = lax.map(lambda pair: padded_block(pair[0], pair[1]), (blocks, live))
    grads = grads.reshape(count_items, per_owner, owners, MOST, 3 * HD).transpose(0, 2, 1, 3, 4)
    returned = grads.reshape(count_items, owners, per_owner * MOST, 3 * HD)
    key_sums = jnp.sum(blocks[:, :, HD : 2 * HD].astype(jnp.float32), axis=1).reshape(
        count_items, per_owner, HD
    )
    return (returned, key_sums)


def padded(queries, keys, values, out_grad, w_out, cluster_ids):
    frames = queries.shape[0]
    heads = cluster_ids.shape[0]
    owners = lax.axis_size("seq")
    per_owner = CLUSTERS // owners
    d_out = lax.dot_general(
        lax.all_gather(out_grad, "head", axis=1, tiled=True),
        w_out,
        (((1,), (1,)), ((), ())),
        preferred_element_type=jnp.float32,
    ).astype(jnp.bfloat16)

    def split_heads(array):
        return array.reshape(frames, heads, HD).transpose(1, 0, 2)

    key_heads = split_heads(keys)
    rows = jnp.concatenate(
        [split_heads(queries), key_heads, split_heads(values), split_heads(d_out)], axis=2
    )
    ids = cluster_ids[:, :, 0]
    member = (ids[:, :, None] == jnp.arange(CLUSTERS, dtype=jnp.int32)[None, None, :]).astype(
        jnp.int32
    )
    running = jnp.cumsum(member, axis=1)
    rank = jnp.sum(member * (running - 1), axis=2)
    slot = ids * MOST + rank
    flat_index = (jnp.arange(heads, dtype=jnp.int32)[:, None] * (CLUSTERS * MOST) + slot).reshape(
        -1
    )
    empty_row = jnp.where(jnp.arange(4 * HD) == 0, EMPTY, 0.0).astype(jnp.bfloat16)
    outgoing = (
        jnp.broadcast_to(empty_row, (heads * CLUSTERS * MOST, 4 * HD))
        .at[flat_index]
        .set(rows.reshape(-1, 4 * HD))
    )
    outgoing = outgoing.reshape(heads, owners, per_owner * MOST, 4 * HD)
    received = lax.all_to_all(outgoing, "seq", split_axis=1, concat_axis=1, tiled=True)
    returned, key_sums = padded_attend(received, per_owner)
    arrived = lax.all_to_all(returned, "seq", split_axis=1, concat_axis=1, tiled=True)
    picked = arrived.reshape(heads * CLUSTERS * MOST, 3 * HD)[flat_index].reshape(
        heads, frames, 3 * HD
    )

    def join_heads(part):
        return part.transpose(1, 0, 2).reshape(frames, heads * HD)

    query_grad = join_heads(picked[:, :, :HD])
    key_grad = join_heads(picked[:, :, HD : 2 * HD])
    value_grad = join_heads(picked[:, :, 2 * HD :])
    centroid_sums = key_sums.transpose(1, 0, 2).reshape(per_owner, heads * HD)
    return (query_grad, key_grad, value_grad, centroid_sums)


def last_step(done, rest, tcol, sums):
    frames, width = done.shape[1], 2 * done.shape[2]
    vmem = pl.BlockSpec(memory_space=pltpu.VMEM)
    grad = jax.ShapeDtypeStruct((frames, width), BF)
    return pl.pallas_call(
        last_kernel,
        name="last_step",
        out_shape=(grad, grad, grad, jax.ShapeDtypeStruct(sums.shape, F32)),
        in_specs=[vmem] * 4,
        out_specs=(vmem,) * 4,
        compiler_params=pltpu.CompilerParams(vmem_limit_bytes=16 << 20),
    )(done, rest, tcol, sums)


def as_parts(dq, dk, dv, sums):
    frames = dq.shape[0]
    done = jnp.stack([x[:, :128] for x in (dq, dk, dv)])
    rest = [jnp.concatenate([dk[:, at : at + HD], dq[:, at : at + HD]], axis=1) for at in (128, 192)]
    rest = jnp.concatenate(rest + [dv[:, 128:], jnp.zeros((NZ * BACK - 3 * frames, 128), BF)])
    at = jnp.arange(frames, dtype=F32)[:, None]
    none = jnp.full((frames, 1), -1.0, F32)
    second = [at, at + 2 * frames, none, at + frames, none, at + 2 * frames]
    cols = [jnp.zeros((frames, 6), F32)] + second + [jnp.zeros((frames, 116), F32)]
    return done, rest, jnp.concatenate(cols, axis=1), sums


def shards(*args):
    *parts, full = two_hop(*args)
    parts = lax.switch(full[0, 0], [lambda: tuple(parts), lambda: as_parts(*padded(*args))])
    return tuple(last_step(*parts))


def solution(mesh):
    placed = (
        P("seq", "head"),
        P("seq", "head"),
        P("seq", "head"),
        P("seq", "head"),
        P("head", None),
        P("head", "seq", None),
    )
    return jax.shard_map(
        shards,
        mesh=mesh,
        in_specs=placed,
        out_specs=(P("seq", "head"), P("seq", "head"), P("seq", "head"), P("seq", "head")),
        check_vma=False,
    )
```

```python
import functools

import jax
import jax.numpy as jnp
from jax import lax
from jax.experimental import pallas as pl
from jax.experimental.pallas import tpu as pltpu
from jax.sharding import PartitionSpec as P

HD = 64
CLUSTERS = 256
MOST = 2
EMPTY = 64.0
MESH = pl.DeviceIdType.MESH
BF = jnp.bfloat16
F32 = jnp.float32
NZ = 16
NXC = 8
NY = 4
CAP = 40
CAP_HEAD = 24
HEAD0 = CAP - CAP_HEAD
HALF = 24
BACK = CAP + HALF
PARTS = ((0, 32), (32, 16), (48, 32), (80, 16), (96, 32), (128, 32))
NEEDS = (((0, 80),), ((0, 96),), ((32, 16), (96, 32)), ((96, 64),))
ROWS = 160


def iota(shape, dim):
    return lax.broadcasted_iota(jnp.int32, shape, dim)


def onehot(cond):
    return jnp.where(cond, 1.0, 0.0).astype(BF)


def nn(a, b):
    return jnp.dot(a, b, preferred_element_type=F32)


def nt(a, b):
    return lax.dot_general(a, b, (((1,), (1,)), ((), ())), preferred_element_type=F32)


def tn(a, b):
    return lax.dot_general(a, b, (((0,), (0,)), ((), ())), preferred_element_type=F32)


def swap_halves(x):
    return jnp.concatenate([x[:, HD:], x[:, :HD]], axis=1)


def cluster_block(qk, vg):
    low = iota((256, 2 * HD), 1) < HD
    q, k = qk[:, :HD], qk[:, HD:]
    v, g = vg[:, :HD], vg[:, HD:]
    live = qk[:, 0:1].astype(F32) < EMPTY / 2
    scores = jnp.where(live, 0.125 * nt(k, q), jnp.float32(-1e30))
    expo = jnp.exp(scores - jnp.max(scores, axis=0, keepdims=True))
    probs = expo / jnp.sum(expo, axis=0, keepdims=True)
    probs_low = probs.astype(BF)
    dprobs = nt(v, g)
    delta = jnp.sum(probs_low.astype(F32) * dprobs, axis=0, keepdims=True)
    dscores = (probs * (dprobs - delta)).astype(BF)
    dk = 0.125 * nn(dscores, qk)
    dq = 0.125 * tn(dscores, qk)
    dv = nn(probs_low, vg)
    return jnp.where(low, dk, dq).astype(BF), jnp.where(low, swap_halves(dv), dv).astype(BF)


def unpack(p, rows, v_rows, tcol):
    keys, values, queries = [], [], []
    at, v_at = iota((256, NZ * CAP), 1), iota((256, NZ * HALF), 1)
    for h in (2 * p, 2 * p + 1):
        cols = tcol[:, 3 * h : 3 * h + 3].astype(jnp.int32)
        got = nn(onehot(at == cols[:, 0:1]), rows)
        first = nn(onehot(v_at == cols[:, 1:2]), v_rows)
        second = nn(onehot(v_at == cols[:, 2:3]), v_rows)
        keys.append(got[:, :HD])
        queries.append(got[:, HD:])
        values.append(first[:, :HD] + second[:, HD:])
    return [jnp.concatenate(x, axis=1).astype(BF) for x in (queries, keys, values)]


def last_kernel(done_ref, rest_ref, rest_v_ref, tcol, cs_in, dq_ref, dk_ref, dv_ref, cs_ref):
    cs_ref[...] = cs_in[...]
    parts = unpack(1, rest_ref[...], rest_v_ref[...], tcol)
    for i, ref in enumerate((dq_ref, dk_ref, dv_ref)):
        ref[:, 0:128] = done_ref[i]
        ref[:, 128:256] = parts[i]


def kernel(
    q_hbm, k_hbm, v_hbm, og_hbm, w_hbm, ids_hbm,
    done_ref, rest_ref, rest_v_ref, tcol, cs_ref, full_ref,
    q_ref, k_ref, v_ref, og_ref, w_ref, ids_ref, ogr, meta_s, meta_r, zs, zr, xs, xr, yb, zb, xbs, xbr, zbs, zbr, tslot,
    sum_own, sum_s, sum_r, full_xs, full_xr, full_ys, full_yr,
    sem_s, sem_r, sem_l, sem_in,
):
    me, hd = lax.axis_index("seq"), lax.axis_index("head")
    x, z, c = me // (2 * NZ), (me // 2) % NZ, me % 2
    xc = x * 2 + c

    def zpeer(i):
        to = (z + i) % NZ
        return to, (x * (2 * NZ) + to * 2 + c, hd)

    def xpeer(i):
        to = (xc + i) % NXC
        return to, ((to // 2) * (2 * NZ) + z * 2 + to % 2, hd)

    def ypeer(i):
        return (me, (hd + i) % NY)

    zorder = [8, 7, 9, 6, 10, 5, 11, 4, 12, 3, 13, 2, 14, 1, 15]
    barrier = pltpu.get_barrier_semaphore()
    peers = [ypeer(i) for i in range(1, NY)]
    peers += [zpeer(i)[1] for i in range(1, NZ)] + [xpeer(i)[1] for i in range(1, NXC)]
    for peer in peers:
        pl.semaphore_signal(barrier, inc=1, device_id=peer, device_id_type=MESH)

    loads = [
        pltpu.make_async_copy(src, dst, sem_in.at[i])
        for i, (src, dst) in enumerate(
            ((ids_hbm, ids_ref), (q_hbm, q_ref), (k_hbm, k_ref),
             (og_hbm, og_ref), (v_hbm, v_ref), (w_hbm, w_ref))
        )
    ]
    for load in loads:
        load.start()
    loads[0].wait()

    sub, lane = iota((256, 256), 0), iota((256, 256), 1)
    earlier = onehot(sub < lane)
    ones = jnp.ones((256, 256), BF)
    before = onehot((sub // 16 == lane // 16) & (lane < sub))
    member, count, zof, poses, targets = [], [], [], [], []

    def place_rows(h):
        ids = ids_ref[h]
        row = ((ids >> 2) & 15) * 16 + (ids >> 6) * 4 + (ids & 3)
        zof.append((((row >> 4) + (h % 2) * (NZ // 2)) & (NZ - 1)).astype(F32))
        member.append(onehot(sub == row))
        count.append(nn(member[h], ones).astype(BF))
        place = nn(before, count[h]) + nn(member[h], earlier)
        nth = jnp.sum(member[h].astype(F32) * place, axis=0, keepdims=True)
        fits = nth < CAP_HEAD
        pos = nth if h % 2 == 0 else CAP - 1 - nth
        poses.append(jnp.where(fits, pos, -1.0))
        targets.append(jnp.where(fits, zof[h] * CAP + pos, -1.0))
        back = zof[h] * HALF + pos
        targets.append(jnp.where(fits & (pos < HALF), back, -1.0))
        targets.append(jnp.where(fits & (pos >= HALF), back - HALF, -1.0))

    def beside(a_ref, b, p):
        a = a_ref[:, p * 128 : (p + 1) * 128].astype(F32)
        b = b[:, p * 128 : (p + 1) * 128].astype(F32)
        low = iota((256, 128), 1) < HD
        return (
            jnp.where(low, a, swap_halves(b)).astype(BF),
            jnp.where(low, swap_halves(a), b).astype(BF),
        )

    def pack(part, pieces):
        at, n = PARTS[part]
        goals, rows = [], []
        for p, pair, first, last, to in pieces:
            for i in range(2):
                pos = poses[2 * p + i]
                fits = (pos >= first) & (pos < last)
                goals.append(jnp.where(fits, zof[2 * p + i] * n + pos + to, -1.0))
                rows.append(pair[i])
        goals = jnp.concatenate(goals, axis=1).astype(jnp.int32)
        rows = jnp.concatenate(rows, axis=0)
        for i in range(4):
            pick = onehot(iota((4 * n, goals.shape[1]), 0) + i * 4 * n == goals)
            zs[i * 4 : i * 4 + 4, at : at + n, :] = nn(pick, rows).astype(BF).reshape(4, n, 128)

    for h in range(2):
        place_rows(h)
    loads[1].wait()
    loads[2].wait()
    qk = [beside(q_ref, k_ref, 0)]
    pack(0, [(0, qk[0], 0, 32, 0)])

    pl.semaphore_wait(barrier, NY - 1 + NZ - 1 + NXC - 1)

    def remote(src, dst, sem, peer):
        pltpu.make_async_remote_copy(
            src_ref=src, dst_ref=dst, send_sem=sem_s.at[sem], recv_sem=sem_r.at[sem],
            device_id=peer, device_id_type=MESH,
        ).start()

    def settle(buf, n, sem, which, rows=None):
        part = buf.at[pl.ds(0, n)] if rows is None else buf.at[pl.ds(0, n), rows]
        pltpu.make_async_copy(part, part, which.at[sem]).wait()

    for i in range(1, NY):
        remote(og_hbm, ogr.at[hd], 0, ypeer(i))
    def send_z(src, dst, rows, sem):
        for i in zorder:
            to, peer = zpeer(i)
            remote(src.at[to, rows], dst.at[z, rows], sem, peer)
        pltpu.make_async_copy(src.at[z, rows], dst.at[z, rows], sem_l.at[sem]).start()

    def wait_z(src, dst, rows, sem):
        settle(dst, NZ - 1, sem, sem_r, rows)
        pltpu.make_async_copy(src.at[z, rows], dst.at[z, rows], sem_l.at[sem]).wait()

    def send_x(src, dst, p, i, sem):
        for step in range(1, NXC):
            to, peer = xpeer(step)
            remote(src.at[p, i, to], dst.at[p, i, xc], sem, peer)
        pltpu.make_async_copy(src.at[p, i, xc], dst.at[p, i, xc], sem_l.at[sem]).start()

    def wait_x(src, dst, p, i, sem):
        settle(dst.at[p, i], NXC - 1, sem, sem_r)
        pltpu.make_async_copy(src.at[p, i, xc], dst.at[p, i, xc], sem_l.at[sem]).wait()

    rows_of = [pl.ds(at, n) for at, n in PARTS]
    send_z(zs, zr, rows_of[0], 2)
    for h in range(2, 4):
        place_rows(h)
    qk.append(beside(q_ref, k_ref, 1))
    pack(1, [(1, qk[1], 0, 16, 0)])
    send_z(zs, zr, rows_of[1], 3)
    meta = jnp.zeros((8, 128), F32)
    mrow = iota((8, 128), 0)
    for h in range(4):
        held = nt(jnp.ones((8, 256), BF), member[h])
        meta = jnp.where(mrow == 2 * h, held[:, :128], meta)
        meta = jnp.where(mrow == 2 * h + 1, held[:, 128:], meta)
    meta_s[...] = meta.astype(BF)
    meta_r[pl.ds(z, 1)] = meta.astype(BF)[None]
    for i in zorder:
        remote(meta_s, meta_r.at[z], 1, zpeer(i)[1])
    tcol[...] = jnp.concatenate(targets + [jnp.zeros((128 - 12, 256), F32)], axis=0).T
    for load in loads[3:]:
        load.wait()
    grad = jnp.zeros((256, 256), F32)
    for i in range(NY):
        y = (hd + i) % NY
        if i == 1:
            settle(ogr, NY - 1, 0, sem_r)
        piece = og_ref[...] if i == 0 else ogr[pl.ds(y, 1)][0]
        grad += nt(piece, w_ref[:, pl.ds(pl.multiple_of(y * 256, 256), 256)])
    d_out = grad.astype(BF)
    vg = [beside(v_ref, d_out, p) for p in range(2)]
    pack(2, [(0, vg[0], 0, 24, 0), (0, qk[0], 32, CAP, -8)])
    send_z(zs, zr, rows_of[2], 4)
    pack(3, [(0, vg[0], 24, CAP, -24)])
    send_z(zs, zr, rows_of[3], 20)
    pack(4, [(1, vg[1], 0, 24, 0), (1, qk[1], 16, 24, 8)])
    send_z(zs, zr, rows_of[4], 21)
    pack(5, [(1, qk[1], 24, CAP, -24), (1, vg[1], 24, CAP, -8)])
    send_z(zs, zr, rows_of[5], 22)

    settle(meta_r, NZ - 1, 1, sem_r)
    r_i, l_i = iota((128, 128), 0), iota((128, 128), 1)
    meta_all = meta_r[...].reshape(128, 128)
    slot_row = ((l_i // 8) % 8) * 2 + (l_i // 2) % 2
    found = nn(meta_all, onehot((r_i % 16 == slot_row) & (r_i // 16 == z % 8)))
    half = r_i % 2 == (z // 8 + l_i // 64) % 2

    def slot(o):
        return (o // 8) * 4 + o % 4

    smaller = ((r_i // 4) % 2 == 0) & (slot(r_i) < slot(l_i))
    smaller = onehot(smaller & (r_i // 64 == l_i // 64))
    l16 = iota((16, 128), 1)
    first_kind = (l16 // 4) % 2 == 0
    for p in range(2):
        mine = jnp.where(half & ((r_i // 2) % 4 == 2 * p + l_i // 64), found, 0.0)
        held = jnp.sum(mine.reshape(16, 8, 128), axis=1)
        taken = held > (l16 % 2).astype(F32)
        t = nn(onehot(taken), smaller)
        fits = taken & (t < CAP_HEAD)
        t = jnp.where(l16 < 64, t, CAP - 1 - t)
        if p == 0:
            there = jnp.where(first_kind, jnp.where(t < 32, t, t + 40), jnp.where(t < 24, t + 48, t + 56))
        else:
            there = jnp.where(first_kind, jnp.where(t < 16, t + 32, t + 104), jnp.where(t < 24, t + 96, t + 120))
        there = jnp.where(fits, there, -1.0)
        tslot[p] = jnp.where(taken, there, jnp.where(first_kind, float(ROWS), -1.0))
        lower = jnp.where(t < HALF, t + CAP, -1.0)
        upper = jnp.where(t >= HALF, t + CAP - HALF, -1.0)
        tslot[2 + p] = jnp.where(fits, jnp.where(first_kind, t, lower), -1.0)
        tslot[4 + p] = jnp.where(fits, jnp.where(first_kind, t, upper), -1.0)
    pair = (l_i // 8 == r_i // 8) & ((l_i % 8) // 4 == (r_i % 8) // 2)
    pair = pair & ((l_i % 2 + (l_i // 2) % 2) % 2 == r_i % 2)
    places = nn(onehot(pair), meta_all).astype(BF)
    blocks = onehot(r_i // 16 == l_i)
    over = (nn(places, blocks) > CAP) | (nn(meta_all, blocks) > CAP_HEAD)
    over = jnp.max(jnp.where(over, 1.0, 0.0), axis=0, keepdims=True)
    full = jnp.broadcast_to(jnp.max(over, axis=1, keepdims=True), (8, 128))
    full_xs[...] = full
    full_xr[pl.ds(xc, 1)] = full[None]
    for i in range(1, NXC):
        remote(full_xs, full_xr.at[xc], 13, xpeer(i)[1])

    s_i, o_i = iota((256, 256), 0), iota((256, 256), 1)

    def source(o):
        return ((o // 32) % 2) * 128 + ((o // 2) % 16) * 8 + (o // 128) * 4 + ((o // 64) % 2) * 2 + o % 2

    perm = onehot(o_i == source(s_i))
    perm_back = onehot(s_i == source(o_i))
    mark = jnp.where((iota((16, 128), 0) == 0) & (iota((16, 128), 1) == 0), EMPTY, 0.0)
    mark = mark.astype(BF)

    def expand(p, h):
        needs = NEEDS[2 * p + h]
        i = iota((sum(n for _, n in needs) + 16, 64), 0)
        at, done = i - i.shape[0] + 16 + ROWS, i.shape[0] - 16
        for first, n in reversed(needs):
            done -= n
            at = jnp.where(i < done + n, i - done + first, at)
        for s in range(NZ):
            pick = onehot(at == tslot[p, s : s + 1, h * 64 : h * 64 + 64].astype(jnp.int32))
            rows = [zr[s, first : first + n, :] for first, n in needs]
            rows = tn(pick, jnp.concatenate(rows + [mark], axis=0))
            xs[p, h, :, s * 8 : s * 8 + 8, :] = rows.reshape(8, 8, 128).astype(BF)

    def work(p, h):
        for i in range(4):
            rows = nn(perm, xr[p, h, 2 * i : 2 * i + 2].reshape(256, 128)).astype(BF)
            for b in range(4):
                yb[b, i * 64 : (i + 1) * 64, :] = rows[b * 64 : (b + 1) * 64]
        for j in range(2):
            zb[j], zb[2 + j] = cluster_block(yb[j], yb[2 + j])
            total = jnp.sum(yb[j].astype(F32), axis=0, keepdims=True)
            (sum_own, sum_s)[h][j : j + 1, p * HD : (p + 1) * HD] = total[:, HD:]
        for i in range(4):
            rows = [zb[b, i * 64 : (i + 1) * 64, :] for b in range(4)]
            rows = nn(perm_back, jnp.concatenate(rows, axis=0)).astype(BF)
            xbs[p, h, 2 * i : 2 * i + 2] = rows.reshape(2, 128, 128)

    def compact_head0(p):
        at = iota((HEAD0, 64), 0)
        for s in range(NZ):
            back = xbr[p, 0, :, s * 8 : s * 8 + 8, :].reshape(64, 128)
            pick = at == tslot[2 + p, s : s + 1, 0:64].astype(jnp.int32)
            zbs[p, s, 0:HEAD0, :] = nn(onehot(pick), back).astype(BF)

    def compact_rest(p):
        low = iota((BACK - HEAD0, 128), 1) < HD
        at = iota((BACK - HEAD0, 128), 0) + HEAD0
        for s in range(NZ):
            back = xbr[p, :, :, s * 8 : s * 8 + 8, :].reshape(128, 128)
            first = nn(onehot(at == tslot[2 + p, s : s + 1, :].astype(jnp.int32)), back)
            second = nn(onehot(at == tslot[4 + p, s : s + 1, :].astype(jnp.int32)), back)
            zbs[p, s, HEAD0:BACK, :] = jnp.where(low, first, second).astype(BF)

    head0, rest = pl.ds(0, HEAD0), pl.ds(HEAD0, BACK - HEAD0)

    def forward(p, h):
        expand(p, h)
        send_x(xs, xr, p, h, 5 + 2 * p + h)

    def middle(p, h):
        wait_x(xs, xr, p, h, 5 + 2 * p + h)
        work(p, h)
        send_x(xbs, xbr, p, h, 9 + 2 * p + h)

    def back_head0(p):
        wait_x(xbs, xbr, p, 0, 9 + 2 * p)
        compact_head0(p)
        send_z(zbs.at[p], zbr.at[p], head0, 14 + 2 * p)

    def back_rest(p):
        wait_x(xbs, xbr, p, 1, 10 + 2 * p)
        compact_rest(p)
        send_z(zbs.at[p], zbr.at[p], rest, 15 + 2 * p)

    def wait_back(p):
        wait_z(zbs.at[p], zbr.at[p], head0, 14 + 2 * p)
        wait_z(zbs.at[p], zbr.at[p], rest, 15 + 2 * p)

    wait_z(zs, zr, rows_of[0], 2)
    wait_z(zs, zr, rows_of[1], 3)
    wait_z(zs, zr, rows_of[2], 4)
    forward(0, 0)
    wait_z(zs, zr, rows_of[3], 20)
    forward(0, 1)
    settle(full_xr, NXC - 1, 13, sem_r)
    full = jnp.max(full_xr[...], axis=0)
    full_ys[...] = full
    for i in range(1, NY):
        remote(full_ys, full_yr.at[hd], 18, ypeer(i))
    middle(0, 0)
    middle(0, 1)
    wait_z(zs, zr, rows_of[4], 21)
    forward(1, 0)
    back_head0(0)
    wait_z(zs, zr, rows_of[5], 22)
    forward(1, 1)
    back_rest(0)
    middle(1, 0)
    middle(1, 1)
    remote(sum_s, sum_r, 19, zpeer(NZ // 2)[1])
    back_head0(1)
    back_rest(1)
    pltpu.make_async_copy(sum_r, sum_r, sem_r.at[19]).wait()
    for p in range(2):
        cols = slice(p * HD, (p + 1) * HD)
        cs_ref[:, p * 128 : (p + 1) * 128] = jnp.concatenate(
            [sum_own[0:2, cols], sum_r[0:2, cols]], axis=1
        )
    settle(full_yr, NY - 1, 18, sem_r)
    for i in range(1, NY):
        full = jnp.maximum(full, full_yr[pl.ds((hd + i) % NY, 1)][0])
    full_ref[0, 0] = jnp.max(full).astype(jnp.int32)
    def gather(p):
        for i in range(NZ):
            rest_ref[i * CAP : i * CAP + CAP, :] = zbr[p, i, 0:CAP, :]
            rest_v_ref[i * HALF : i * HALF + HALF, :] = zbr[p, i, CAP:BACK, :]

    wait_back(0)
    gather(0)
    for i, part in enumerate(unpack(0, rest_ref[...], rest_v_ref[...], tcol)):
        done_ref[i] = part
    wait_back(1)
    gather(1)

    for i in range(1, NY):
        pltpu.make_async_copy(og_ref, og_ref, sem_s.at[0]).wait()
        pltpu.make_async_copy(full_ys, full_ys, sem_s.at[18]).wait()
    for i in range(1, NZ):
        pltpu.make_async_copy(meta_s, meta_s, sem_s.at[1]).wait()
    for i in range(1, NXC):
        pltpu.make_async_copy(full_xs, full_xs, sem_s.at[13]).wait()
    pltpu.make_async_copy(sum_s, sum_s, sem_s.at[19]).wait()
    for rows, sem in zip(rows_of, (2, 3, 4, 20, 21, 22)):
        settle(zs, NZ - 1, sem, sem_s, rows)
    for p in range(2):
        for h in range(2):
            settle(xs.at[p, h], NXC - 1, 5 + 2 * p + h, sem_s)
            settle(xbs.at[p, h], NXC - 1, 9 + 2 * p + h, sem_s)
        settle(zbs.at[p], NZ - 1, 14 + 2 * p, sem_s, head0)
        settle(zbs.at[p], NZ - 1, 15 + 2 * p, sem_s, rest)


def two_hop(queries, keys, values, out_grad, w_out, cluster_ids):
    frames, width = queries.shape
    heads = cluster_ids.shape[0]
    vmem = pl.BlockSpec(memory_space=pltpu.VMEM)

    def buf(*shape, dtype=BF):
        return pltpu.VMEM(shape, dtype)

    return pl.pallas_call(
        kernel,
        name="two_hop",
        out_shape=(
            jax.ShapeDtypeStruct((3, frames, width // 2), BF),
            jax.ShapeDtypeStruct((NZ * CAP, 128), BF),
            jax.ShapeDtypeStruct((NZ * HALF, 128), BF),
            jax.ShapeDtypeStruct((frames, 128), F32),
            jax.ShapeDtypeStruct((2, width), F32),
            jax.ShapeDtypeStruct((1, 1), jnp.int32),
        ),
        in_specs=[pl.BlockSpec(memory_space=pl.ANY)] * 6,
        out_specs=(vmem,) * 5 + (pl.BlockSpec(memory_space=pltpu.SMEM),),
        scratch_shapes=[
            buf(frames, width),
            buf(frames, width),
            buf(frames, width),
            buf(frames, width),
            buf(width, NY * width),
            buf(heads, 1, frames, dtype=jnp.int32),
            buf(NY, frames, width),
            buf(8, 128),
            buf(NZ, 8, 128),
            buf(NZ, ROWS, 128),
            buf(NZ, ROWS, 128),
            buf(2, 2, NXC, NZ * 8, 128),
            buf(2, 2, NXC, NZ * 8, 128),
            buf(4, 256, 128),
            buf(4, 256, 128),
            buf(2, 2, NXC, NZ * 8, 128),
            buf(2, 2, NXC, NZ * 8, 128),
            buf(2, NZ, BACK, 128),
            buf(2, NZ, BACK, 128),
            buf(6, NZ, 128, dtype=F32),
            buf(8, 128, dtype=F32),
            buf(8, 128, dtype=F32),
            buf(8, 128, dtype=F32),
            buf(8, 128, dtype=F32),
            buf(NXC, 8, 128, dtype=F32),
            buf(8, 128, dtype=F32),
            buf(NY, 8, 128, dtype=F32),
            pltpu.SemaphoreType.DMA((23,)),
            pltpu.SemaphoreType.DMA((23,)),
            pltpu.SemaphoreType.DMA((23,)),
            pltpu.SemaphoreType.DMA((6,)),
        ],
        compiler_params=pltpu.CompilerParams(
            collective_id=0, has_side_effects=True, vmem_limit_bytes=48 << 20
        ),
    )(queries, keys, values, out_grad, w_out, cluster_ids.reshape(heads, 1, frames))


def padded_block(block, live):
    q_rows = block[:, :HD]
    k_rows = block[:, HD : 2 * HD]
    v_rows = block[:, 2 * HD : 3 * HD]
    g_rows = block[:, 3 * HD :]
    scores = 0.125 * jnp.dot(q_rows, k_rows.T, preferred_element_type=jnp.float32)
    scores = jnp.where(live[None, :], scores, jnp.float32(-1e30))
    top = jnp.max(scores, axis=1, keepdims=True)
    expo = jnp.exp(scores - top)
    probs = expo / jnp.sum(expo, axis=1, keepdims=True)
    probs_low = probs.astype(jnp.bfloat16)
    attended = jnp.dot(probs_low, v_rows, preferred_element_type=jnp.float32)
    delta = jnp.sum(g_rows.astype(jnp.float32) * attended, axis=1, keepdims=True)
    dprobs = jnp.dot(g_rows, v_rows.T, preferred_element_type=jnp.float32)
    dscores = (probs * (dprobs - delta)).astype(jnp.bfloat16)
    dq_rows = (0.125 * jnp.dot(dscores, k_rows, preferred_element_type=jnp.float32)).astype(
        jnp.bfloat16
    )
    dk_rows = (0.125 * jnp.dot(dscores.T, q_rows, preferred_element_type=jnp.float32)).astype(
        jnp.bfloat16
    )
    dv_rows = jnp.dot(probs_low.T, g_rows, preferred_element_type=jnp.float32).astype(jnp.bfloat16)
    return jnp.concatenate([dq_rows, dk_rows, dv_rows], axis=1)


def padded_attend(received, per_owner):
    count_items = received.shape[0]
    owners = received.shape[1]
    capacity = owners * MOST
    blocks = received.reshape(count_items, owners, per_owner, MOST, 4 * HD)
    blocks = blocks.transpose(0, 2, 1, 3, 4).reshape(count_items * per_owner, capacity, 4 * HD)
    live = blocks[:, :, 0] < EMPTY / 2
    grads = lax.map(lambda pair: padded_block(pair[0], pair[1]), (blocks, live))
    grads = grads.reshape(count_items, per_owner, owners, MOST, 3 * HD).transpose(0, 2, 1, 3, 4)
    returned = grads.reshape(count_items, owners, per_owner * MOST, 3 * HD)
    key_sums = jnp.sum(blocks[:, :, HD : 2 * HD].astype(jnp.float32), axis=1).reshape(
        count_items, per_owner, HD
    )
    return (returned, key_sums)


def padded(queries, keys, values, out_grad, w_out, cluster_ids):
    frames = queries.shape[0]
    heads = cluster_ids.shape[0]
    owners = lax.axis_size("seq")
    per_owner = CLUSTERS // owners
    d_out = lax.dot_general(
        lax.all_gather(out_grad, "head", axis=1, tiled=True),
        w_out,
        (((1,), (1,)), ((), ())),
        preferred_element_type=jnp.float32,
    ).astype(jnp.bfloat16)

    def split_heads(array):
        return array.reshape(frames, heads, HD).transpose(1, 0, 2)

    key_heads = split_heads(keys)
    rows = jnp.concatenate(
        [split_heads(queries), key_heads, split_heads(values), split_heads(d_out)], axis=2
    )
    ids = cluster_ids[:, :, 0]
    member = (ids[:, :, None] == jnp.arange(CLUSTERS, dtype=jnp.int32)[None, None, :]).astype(
        jnp.int32
    )
    running = jnp.cumsum(member, axis=1)
    rank = jnp.sum(member * (running - 1), axis=2)
    slot = ids * MOST + rank
    flat_index = (jnp.arange(heads, dtype=jnp.int32)[:, None] * (CLUSTERS * MOST) + slot).reshape(
        -1
    )
    empty_row = jnp.where(jnp.arange(4 * HD) == 0, EMPTY, 0.0).astype(jnp.bfloat16)
    outgoing = (
        jnp.broadcast_to(empty_row, (heads * CLUSTERS * MOST, 4 * HD))
        .at[flat_index]
        .set(rows.reshape(-1, 4 * HD))
    )
    outgoing = outgoing.reshape(heads, owners, per_owner * MOST, 4 * HD)
    received = lax.all_to_all(outgoing, "seq", split_axis=1, concat_axis=1, tiled=True)
    returned, key_sums = padded_attend(received, per_owner)
    arrived = lax.all_to_all(returned, "seq", split_axis=1, concat_axis=1, tiled=True)
    picked = arrived.reshape(heads * CLUSTERS * MOST, 3 * HD)[flat_index].reshape(
        heads, frames, 3 * HD
    )

    def join_heads(part):
        return part.transpose(1, 0, 2).reshape(frames, heads * HD)

    query_grad = join_heads(picked[:, :, :HD])
    key_grad = join_heads(picked[:, :, HD : 2 * HD])
    value_grad = join_heads(picked[:, :, 2 * HD :])
    centroid_sums = key_sums.transpose(1, 0, 2).reshape(per_owner, heads * HD)
    return (query_grad, key_grad, value_grad, centroid_sums)


def last_step(done, rest, rest_v, tcol, sums):
    frames, width = done.shape[1], 2 * done.shape[2]
    vmem = pl.BlockSpec(memory_space=pltpu.VMEM)
    grad = jax.ShapeDtypeStruct((frames, width), BF)
    return pl.pallas_call(
        last_kernel,
        name="last_step",
        out_shape=(grad, grad, grad, jax.ShapeDtypeStruct(sums.shape, F32)),
        in_specs=[vmem] * 5,
        out_specs=(vmem,) * 4,
        compiler_params=pltpu.CompilerParams(vmem_limit_bytes=16 << 20),
    )(done, rest, rest_v, tcol, sums)


def as_parts(dq, dk, dv, sums):
    frames = dq.shape[0]
    done = jnp.stack([x[:, :128] for x in (dq, dk, dv)])
    rest = [jnp.concatenate([dk[:, at : at + HD], dq[:, at : at + HD]], axis=1) for at in (128, 192)]
    rest = jnp.concatenate(rest + [jnp.zeros((NZ * CAP - 2 * frames, 128), BF)])
    rest_v = jnp.concatenate([dv[:, 128:], jnp.zeros((NZ * HALF - frames, 128), BF)])
    at = jnp.arange(frames, dtype=F32)[:, None]
    none = jnp.full((frames, 1), -1.0, F32)
    second = [at, at, none, at + frames, none, at]
    cols = [jnp.zeros((frames, 6), F32)] + second + [jnp.zeros((frames, 116), F32)]
    return done, rest, rest_v, jnp.concatenate(cols, axis=1), sums


def shards(*args):
    *parts, full = two_hop(*args)
    parts = lax.switch(full[0, 0], [lambda: tuple(parts), lambda: as_parts(*padded(*args))])
    return tuple(last_step(*parts))


def solution(mesh):
    placed = (
        P("seq", "head"),
        P("seq", "head"),
        P("seq", "head"),
        P("seq", "head"),
        P("head", None),
        P("head", "seq", None),
    )
    return jax.shard_map(
        shards,
        mesh=mesh,
        in_specs=placed,
        out_specs=(P("seq", "head"), P("seq", "head"), P("seq", "head"), P("seq", "head")),
        check_vma=False,
    )
```
